32 devices in a mesh: lat: 8 (over z, x), chan: 4 (over y, core).
Axes of the slice: x: 2, y: 2, z: 4, core: 2. Of those that a mesh axis runs over, the one named last changes fastest.
Arguments:
- coarse_state: float32 [4, 96, 180, 641], P('chan', 'lat'), may hold values from -6 to 6
- fine_state: float32 [4, 184, 360, 641], P('chan', 'lat'), may hold values from -6 to 6
- coarse_noise: int32 [4, 96, 180, 8], P('chan', 'lat'), may hold values from 0 to 262143
- fine_noise: int32 [4, 184, 360, 8], P('chan', 'lat'), may hold values from 0 to 262143
- coarse_rows: int32 [96], replicated, may hold values from -1 to 89, as said below
- fine_rows: int32 [184], replicated, may hold values from -1 to 179, as said below
- pair_slots: int32 [96], replicated, may hold values from -1 to 89, as said below
- first_gain: float32 [641], replicated, may hold values from 0.5 to 1.5
- first_bias: float32 [641], replicated, may hold values from -3 to 3
- mix_weight: bfloat16 [192, 2, 649, 641], P('lat'), may hold values from -0.15625 to 0.15625
- second_gain: float32 [641], replicated, may hold values from 0.5 to 1.5
- second_bias: float32 [641], replicated, may hold values from -3 to 3
- up_weight: bfloat16 [641, 1282], replicated, may hold values from -0.25 to 0.25
- up_bias: float32 [1282], replicated, may hold values from -3 to 3
- down_weight: bfloat16 [1282, 641], replicated, may hold values from -0.15625 to 0.15625
- down_bias: float32 [641], replicated, may hold values from -3 to 3
- coarse_cotangent: float32 [4, 96, 180, 641], P('chan', 'lat'), may hold values from -6 to 6
- fine_cotangent: float32 [4, 184, 360, 641], P('chan', 'lat'), may hold values from -6 to 6
Outputs:
- coarse_out: float32 [4, 96, 180, 641], P('chan', 'lat')
- fine_out: float32 [4, 184, 360, 641], P('chan', 'lat')
- coarse_grad: float32 [4, 96, 180, 641], P('chan', 'lat')
- fine_grad: float32 [4, 184, 360, 641], P('chan', 'lat')
- first_gain_grad: float32 [641], replicated
- first_bias_grad: float32 [641], replicated
- mix_grad: float32 [192, 2, 649, 641], P(('lat', 'chan'))
- second_gain_grad: float32 [641], replicated
- second_bias_grad: float32 [641], replicated
- up_weight_grad: float32 [641, 1282], replicated
- up_bias_grad: float32 [1282], replicated
- down_weight_grad: float32 [1282, 641], replicated
- down_bias_grad: float32 [641], replicated
The draws below stay inside these ranges and needn't reach their ends.
Inputs may be any that keep to these rules, and one draw needn't show every extreme that they name: `coarse_rows`: each latitude row 0 to 89 stands in exactly one slot; the other slots hold -1. `fine_rows`: each latitude row 0 to 179 stands in exactly one slot; the other slots hold -1. `pair_slots`: each pair 0 to 89 stands in exactly one slot; the other slots hold -1.
All inputs are finite; a program needn't handle non-finite values.
Results may differ from the reference program's by a relative error of at most 0.02.
Values may be sent and summed in bfloat16 or wider, within the bound.
No kernel may reach another device: no remote copies, remote signals or barrier semaphores. Data moves between devices by JAX's collectives and lax.ppermute only.
A program may use at most 832 MiB of HBM per device.

```python
import math
import jax
import jax.numpy as jnp
from jax import lax

C = 641
HID = 1282
NOISE = 8
LA = 90
LB = 180
BATCH = 4
WIDE = 649
NLA = 180
NLB = 360
RA_DEV = 12
RB_DEV = 23
RSA = 96
RSB = 184
PAIR_DEV = 12
MSLOTS = 192
N_LAT = 8


def draw_coarse_rows(key, part):
    key = jax.random.fold_in(key, 11)
    shuffled = jax.random.permutation(key, RA_DEV * N_LAT)
    return jnp.where(shuffled < LA, shuffled, -1).astype(jnp.int32)


def draw_fine_rows(key, part):
    key = jax.random.fold_in(key, 23)
    shuffled = jax.random.permutation(key, RB_DEV * N_LAT)
    return jnp.where(shuffled < LB, shuffled, -1).astype(jnp.int32)


def draw_pair_slots(key, part):
    key = jax.random.fold_in(key, 37)
    shuffled = jax.random.permutation(key, PAIR_DEV * N_LAT)
    return jnp.where(shuffled < LA, shuffled, -1).astype(jnp.int32)


def set_ends(result, key, least, high):
    spot = [jax.random.randint(jax.random.fold_in(key, axis), (), 0, length) for axis, length in enumerate(result.shape)]
    widest = result.shape.index(max(result.shape))
    beside = spot[:widest] + [(spot[widest] + 1) % result.shape[widest]] + spot[widest + 1:]
    return result.at[tuple(spot)].set(least).at[tuple(beside)].set(high)


def block_scale(own_key, dims, split, low, top_value):
    factor_of = 1.0
    for dim, parts in split:
        draws = jax.random.uniform(jax.random.fold_in(jax.random.fold_in(own_key, 6), dim), (parts,), jnp.float32, low / len(split), top_value / len(split))
        factor_of = factor_of * jnp.repeat(jnp.exp(draws), dims[dim] // parts).reshape((-1,) + (1,) * (len(dims) - 1 - dim))
    return factor_of


def centred(own_key, extent, deviation, bound, cuts=(), kind=jnp.bfloat16):
    values = jax.random.normal(own_key, extent, jnp.float32) * deviation
    if len(cuts) > 0:
        values = block_scale(own_key, extent, cuts, -0.22, 0.18) * values
    return jnp.clip(values, min=-bound, max=bound).astype(kind)


def setup_inputs(seed: int = 0) -> dict:
    seeds = jax.random.split(jax.random.key(seed), 19)
    coarse_state = centred(seeds[0], (BATCH, RSA, NLA, C), 1.0, 6.0, ((0, 4), (1, 8)), jnp.float32)
    fine_state = centred(seeds[1], (BATCH, RSB, NLB, C), 1.0, 6.0, ((0, 4), (1, 8)), jnp.float32)
    coarse_noise = set_ends(jax.random.randint(seeds[2], (BATCH, RSA, NLA, NOISE), 0, 262144), jax.random.fold_in(seeds[2], 1), 0, 262143).astype(jnp.int32)
    fine_noise = set_ends(jax.random.randint(seeds[3], (BATCH, RSB, NLB, NOISE), 0, 262144), jax.random.fold_in(seeds[3], 1), 0, 262143).astype(jnp.int32)
    coarse_rows = draw_coarse_rows(jax.random.fold_in(seeds[18], 71), 0)
    fine_rows = draw_fine_rows(jax.random.fold_in(seeds[18], 71), 0)
    pair_slots = draw_pair_slots(jax.random.fold_in(seeds[18], 71), 0)
    first_gain = jnp.clip(1.0 + 0.1 * jax.random.normal(seeds[7], (C,), jnp.float32), 0.5, 1.5)
    first_bias = centred(seeds[8], (C,), 0.5, 3.0, (), jnp.float32)
    mix_weight = centred(seeds[9], (MSLOTS, 2, WIDE, C), (2 * WIDE) ** -0.5, 0.15625, ((0, 8),))
    second_gain = jnp.clip(1.0 + 0.1 * jax.random.normal(seeds[10], (C,), jnp.float32), 0.5, 1.5)
    second_bias = centred(seeds[11], (C,), 0.5, 3.0, (), jnp.float32)
    up_weight = centred(seeds[12], (C, HID), C ** -0.5, 0.25)
    up_bias = centred(seeds[13], (HID,), 0.5, 3.0, (), jnp.float32)
    down_weight = centred(seeds[14], (HID, C), HID ** -0.5, 0.15625)
    down_bias = centred(seeds[15], (C,), 0.5, 3.0, (), jnp.float32)
    coarse_cotangent = centred(seeds[16], (BATCH, RSA, NLA, C), 1.0, 6.0, ((0, 4), (1, 8)), jnp.float32)
    fine_cotangent = centred(seeds[17], (BATCH, RSB, NLB, C), 1.0, 6.0, ((0, 4), (1, 8)), jnp.float32)
    return {"coarse_state": coarse_state, "fine_state": fine_state, "coarse_noise": coarse_noise, "fine_noise": fine_noise, "coarse_rows": coarse_rows, "fine_rows": fine_rows, "pair_slots": pair_slots, "first_gain": first_gain, "first_bias": first_bias, "mix_weight": mix_weight, "second_gain": second_gain, "second_bias": second_bias, "up_weight": up_weight, "up_bias": up_bias, "down_weight": down_weight, "down_bias": down_bias, "coarse_cotangent": coarse_cotangent, "fine_cotangent": fine_cotangent}


@jax.custom_vjp
def low(v):
    return lax.optimization_barrier(v.astype(jnp.bfloat16)).astype(jnp.float32)

@jax.custom_vjp
def low_back(v):
    return v

def low_keep(v):
    return (low(v), None)

def low_pass(kept, grad):
    return (grad,)

def back_keep(v):
    return (v, None)

def back_low(kept, grad):
    return (low(grad),)
low.defvjp(low_keep, low_pass)
low_back.defvjp(back_keep, back_low)
epsilon = 1e-05
noise_scale = 1.0 / 262144.0
highest = lax.Precision.HIGHEST

def noise_value(noise_ints):
    return ((noise_ints.astype(jnp.float32) + 0.5) * noise_scale - 0.5) * math.sqrt(12.0)

def layer_norm(values, gain_vector, bias_vector):
    centered = values - lax.optimization_barrier(jnp.mean(values, axis=-1, keepdims=True))
    variance = lax.optimization_barrier(jnp.mean(centered * centered, axis=-1, keepdims=True))
    return centered * lax.rsqrt(variance + epsilon) * gain_vector + bias_vector

def legendre(orders, cosines, sines, degree_total):
    order_real = orders.astype(cosines.dtype)[:, None]
    log_start = 0.5 * jnp.log((2.0 * order_real + 1.0) / (4.0 * math.pi))
    log_start = log_start + 0.5 * (lax.lgamma(2.0 * order_real + 1.0) - 2.0 * order_real * math.log(2.0) - 2.0 * lax.lgamma(order_real + 1.0))
    diagonal = jnp.exp(log_start + order_real * jnp.log(sines)[None, :])

    def recur_step(carry, degree):
        previous, earlier = carry
        degree_real = degree.astype(cosines.dtype)
        grow_factor = jnp.sqrt((4.0 * degree_real * degree_real - 1.0) / jnp.maximum(degree_real * degree_real - order_real * order_real, 1.0))
        damp_factor = jnp.sqrt(jnp.maximum((degree_real - 1.0) ** 2 - order_real * order_real, 0.0) / jnp.maximum(4.0 * (degree_real - 1.0) ** 2 - 1.0, 1.0))
        recurred = grow_factor * (cosines[None, :] * previous - damp_factor * earlier)
        current = jnp.where(degree == orders[:, None], diagonal, jnp.where(degree > orders[:, None], recurred, jnp.zeros_like(recurred)))
        return ((current, previous), current)
    zero_state = jnp.zeros((orders.shape[0], cosines.shape[0]), cosines.dtype)
    unused, stacked = lax.scan(recur_step, (zero_state, zero_state), jnp.arange(degree_total, dtype=jnp.int32))
    return stacked

def sphere_tables(orders, row_table, degree_total, dtype):
    occupied = (row_table >= 0).astype(dtype)
    colatitude = math.pi * (jnp.maximum(row_table, 0).astype(dtype) + 0.5) / degree_total
    sines = jnp.sin(colatitude)
    plain_table = legendre(orders, jnp.cos(colatitude), sines, degree_total) * occupied
    quad_table = plain_table * (sines * occupied * (2.0 * math.pi * math.pi / degree_total))
    return (quad_table, plain_table)

def fourier_table(lon_count, degree_total, dtype):
    orders = jnp.arange(degree_total, dtype=jnp.int32)[:, None]
    points = jnp.arange(lon_count, dtype=jnp.int32)[None, :]
    phase_angle = (orders * points % lon_count).astype(dtype) * (2.0 * math.pi / lon_count)
    retained = jnp.ones((degree_total, 1), dtype)
    return jnp.stack([jnp.cos(phase_angle) * retained / lon_count, -jnp.sin(phase_angle) * retained / lon_count])

def inverse_table(lon_count, degree_total, dtype):
    orders = jnp.arange(degree_total, dtype=jnp.int32)[:, None]
    points = jnp.arange(lon_count, dtype=jnp.int32)[None, :]
    phase_angle = (orders * points % lon_count).astype(dtype) * (2.0 * math.pi / lon_count)
    doubling = jnp.where(orders == 0, 1.0, 2.0).astype(dtype) * jnp.ones((degree_total, 1), dtype)
    return jnp.stack([jnp.cos(phase_angle) * doubling, -jnp.sin(phase_angle) * doubling], axis=1)

def member_degrees(pair_slots, with_upper):
    pair_ok = pair_slots >= 0
    pair_safe = jnp.maximum(pair_slots, 0)
    lower_member = jnp.where(pair_ok, pair_safe, -1)
    if with_upper:
        upper_member = jnp.where(pair_ok, LB - 1 - pair_safe, -1)
    else:
        upper_member = jnp.full_like(pair_slots, -1)
    return jnp.stack([lower_member, upper_member], axis=1).reshape(-1).astype(jnp.int32)

def holder_of(slot_degree, degree_total):
    compare = slot_degree[None, :] == jnp.arange(degree_total, dtype=jnp.int32)[:, None]
    slot_index = jnp.arange(slot_degree.shape[0], dtype=jnp.int32)[None, :]
    return lax.optimization_barrier(jnp.sum(jnp.where(compare, slot_index, 0), axis=1)).astype(jnp.int32)

def sample_block(state, noise_ints, row_table, slot_degree, holder, degree_total, params):
    first_gain, first_bias, mix_weight, second_gain, second_bias, up_weight, up_bias, down_weight, down_bias = params
    row_slots, lon_count, channels = state.shape
    wide_count = channels + noise_ints.shape[-1]
    spread_in = low(jnp.concatenate([layer_norm(state, first_gain, first_bias), noise_value(noise_ints)], axis=-1))
    forward_dft = low(fourier_table(lon_count, degree_total, jnp.float32))
    spectrum = jnp.einsum('tmk,rkc->rmtc', forward_dft, spread_in, precision=highest)
    spectrum = low_back(low(spectrum.reshape(row_slots, degree_total, 2 * wide_count)))
    quad_table, plain_table = sphere_tables(jnp.arange(degree_total, dtype=jnp.int32), row_table, degree_total, jnp.float32)
    coef = low_back(low(jnp.einsum('lmj,jmc->lmc', low(quad_table), spectrum, precision=highest)))
    slot_live = (slot_degree >= 0).astype(jnp.float32)
    slotted = jnp.take(coef, jnp.maximum(slot_degree, 0), axis=0) * slot_live[:, None, None]
    real_in = slotted[..., :wide_count]
    imag_in = slotted[..., wide_count:]
    real_weight = mix_weight[:, 0]
    imag_weight = mix_weight[:, 1]
    real_out = jnp.einsum('qmi,qio->qmo', real_in, real_weight, precision=highest) - jnp.einsum('qmi,qio->qmo', imag_in, imag_weight, precision=highest)
    imag_out = jnp.einsum('qmi,qio->qmo', real_in, imag_weight, precision=highest) + jnp.einsum('qmi,qio->qmo', imag_in, real_weight, precision=highest)
    mixed = low_back(low(jnp.concatenate([real_out, imag_out], axis=-1)))
    by_degree = jnp.take(mixed, holder, axis=0)
    synth = low_back(low(jnp.einsum('lmj,lmo->jmo', low(plain_table), by_degree, precision=highest)))
    backward_dft = low(inverse_table(lon_count, degree_total, jnp.float32))
    synthesized = low_back(jnp.einsum('mtk,jmtc->jkc', backward_dft, synth.reshape(row_slots, degree_total, 2, channels), precision=highest))
    middle = state + synthesized
    normed_low = low(layer_norm(middle, second_gain, second_bias))
    pre_act = low_back(jnp.einsum('rkc,ch->rkh', normed_low, up_weight, precision=highest)) + up_bias
    hidden_low = low(jax.nn.gelu(pre_act, approximate=False))
    return middle + low_back(jnp.einsum('rkh,hc->rkc', hidden_low, down_weight, precision=highest)) + down_bias

def make_sample(row_table, slot_degree, holder, degree_total, params):

    def one_sample(sample_pair):
        return sample_block(sample_pair[0], sample_pair[1], row_table, slot_degree, holder, degree_total, params)
    return jax.checkpoint(one_sample)

def reference(coarse_state, fine_state, coarse_noise, fine_noise, coarse_rows, fine_rows, pair_slots, first_gain, first_bias, mix_weight, second_gain, second_bias, up_weight, up_bias, down_weight, down_bias, coarse_cotangent, fine_cotangent):
    coarse_slots = member_degrees(pair_slots, False)
    fine_slots = member_degrees(pair_slots, True)
    coarse_holder = holder_of(coarse_slots, LA)
    fine_holder = holder_of(fine_slots, LB)

    def forward(coarse_in, fine_in, *params):
        coarse_fn = make_sample(coarse_rows, coarse_slots, coarse_holder, LA, params)
        fine_fn = make_sample(fine_rows, fine_slots, fine_holder, LB, params)
        return (lax.map(coarse_fn, (coarse_in, coarse_noise)), lax.map(fine_fn, (fine_in, fine_noise)))
    primals = (coarse_state, fine_state, first_gain, first_bias, mix_weight.astype(jnp.float32), second_gain, second_bias, up_weight.astype(jnp.float32), up_bias, down_weight.astype(jnp.float32), down_bias)
    outputs, pull = jax.vjp(forward, *primals)
    grads = pull((coarse_cotangent, fine_cotangent))
    return (outputs[0], outputs[1], grads[0], grads[1], grads[2], grads[3], grads[4], grads[5], grads[6], grads[7], grads[8], grads[9], grads[10])
```

```python
import functools
import math

import jax
import jax.numpy as jnp
from jax import lax
from jax.experimental import pallas as pl
from jax.experimental.pallas import tpu as pltpu
from jax.sharding import PartitionSpec as P

C = 641
NOISE = 8
WIDE = C + NOISE
LA = 90
LB = 180

TILE = 128
MAIN = C // TILE * TILE
HALF = TILE // 2
LANES = 2 * MAIN + TILE
PADDED = MAIN + TILE

epsilon = 1e-05
noise_scale = 1.0 / 262144.0
bf16 = jnp.bfloat16
f32 = jnp.float32
VMEM_LIMIT = 60 * 2**20


def call(body, name, flops, moved, **options):
    scratch = options.pop("scratch_shapes", [])
    return pl.pallas_call(
        body,
        scratch_shapes=scratch,
        compiler_params=pltpu.CompilerParams(vmem_limit_bytes=VMEM_LIMIT),
        cost_estimate=pl.CostEstimate(flops=int(flops), bytes_accessed=int(moved), transcendentals=0),
        name=name,
        **options,
    )


def dot(left, right, left_dim, right_dim):
    return lax.dot_general(
        left, right, (((left_dim,), (right_dim,)), ((), ())), preferred_element_type=f32
    )


def join_parts(real, imag, count):
    tail = real[:, MAIN:] + pltpu.roll(imag[:, MAIN:], HALF, 1)
    return jnp.concatenate([real[:, :MAIN], imag[:, :MAIN], tail], axis=1)


def join_narrow(real, imag):
    lane = lax.broadcasted_iota(jnp.int32, (real.shape[0], TILE), 1)
    tail = jnp.where(
        lane == 0, real[:, MAIN:C], jnp.where(lane == HALF, imag[:, MAIN:C], 0.0)
    )
    return jnp.concatenate([real[:, :MAIN], imag[:, :MAIN], tail], axis=1)


def split_parts(joined, count):
    tail = joined[:, 2 * MAIN :]
    real = jnp.concatenate([joined[:, :MAIN], tail], axis=1)[:, :count]
    imag = jnp.concatenate(
        [joined[:, MAIN : 2 * MAIN], pltpu.roll(tail, HALF, 1)], axis=1
    )[:, :count]
    return real, imag


def flat(block):
    return block.astype(f32).reshape(-1, block.shape[-1])


def norm_stats(values):
    centered = values - jnp.mean(values, axis=0, keepdims=True)
    variance = jnp.mean(centered * centered, axis=0, keepdims=True)
    scale = lax.rsqrt(variance + epsilon)
    return centered * scale, scale


def spread_body(state, noise, gain, bias, table, out, held):
    @pl.when(pl.program_id(0) == 0)
    def _():
        held[...] = jnp.zeros_like(held)

    xhat, unused = norm_stats(state[0][:, 0, :])
    held[:C] = xhat * gain[...] + bias[...]
    held[C:WIDE] = ((noise[0].astype(f32) + 0.5) * noise_scale - 0.5) * math.sqrt(12.0)
    result = dot(table[...], held[...].astype(bf16), 1, 1)
    rows = result.shape[0] // 2
    joined = join_parts(result[:rows], result[rows:], WIDE)
    out[:, 0] = joined.reshape(out.shape[0], out.shape[2], LANES).astype(bf16)


def spread(state, noise, gain, bias, table, n_lat, first, count):
    points = state.shape[3]
    subs = table.shape[0] // (2 * n_lat)
    const = lambda r: (0, 0)
    return call(
        spread_body,
        "norm_and_dft",
        2 * count * table.shape[0] * points * PADDED,
        count * (C * points * 4 + n_lat * subs * LANES * 2),
        grid=(count,),
        in_specs=[
            pl.BlockSpec((1, C, 1, points), lambda r: (r + first, 0, 0, 0)),
            pl.BlockSpec((1, NOISE, points), lambda r: (r + first, 0, 0)),
            pl.BlockSpec((C, 1), const),
            pl.BlockSpec((C, 1), const),
            pl.BlockSpec(table.shape, const),
        ],
        out_specs=pl.BlockSpec((n_lat, 1, subs, LANES), lambda r: (0, r, 0, 0)),
        out_shape=jax.ShapeDtypeStruct((n_lat, count, subs, LANES), bf16),
        scratch_shapes=[pltpu.VMEM((PADDED, points), f32)],
    )(state, noise, gain, bias, table)


def legendre_body(total, pairs, order_a, order_b, diag_a, diag_b, cosine, classes, *refs):
    two = order_b is not None
    outs, (held_a, held_b) = refs[: 3 if two else 1], (refs[3:] if two else (refs[1], None))

    def advance(degree, order, diagonal, previous, earlier):
        real = degree.astype(f32)
        grow = jnp.sqrt(
            (4.0 * real * real - 1.0) / jnp.maximum(real * real - order * order, 1.0)
        )
        damp = jnp.sqrt(
            jnp.maximum((real - 1.0) * (real - 1.0) - order * order, 0.0)
            / jnp.maximum(4.0 * (real - 1.0) * (real - 1.0) - 1.0, 1.0)
        )
        grown = grow * (cosine[...] * previous - damp * earlier)
        return jnp.where(real == order, diagonal, jnp.where(real > order, grown, 0.0))

    def step(degree, carry):
        now_a = advance(degree, order_a[...], diag_a[...], carry[0], carry[1])
        held_a[degree] = now_a
        if not two:
            return (now_a, carry[0])
        now_b = advance(degree, order_b[...], diag_b[...], carry[2], carry[3])
        held_b[degree] = now_b
        return (now_a, carry[0], now_b, carry[2])

    zero = diag_a[...] * 0.0
    lax.fori_loop(0, total, step, (zero,) * (4 if two else 2))

    def pick(slot, unused):
        pair = pairs[slot]
        safe = jnp.maximum(pair, 0)
        live = jnp.where(pair >= 0, 1.0, 0.0)
        low = classes[...] <= pair
        near = held_a[safe] * live
        if two:
            far = held_a[LB - 1 - safe] * live
            outs[0][slot] = jnp.where(low, near, far)
            outs[1][slot] = jnp.where(low, far, 0.0)
            outs[2][slot] = jnp.where(low, 0.0, held_b[LB - 1 - safe] * live)
        else:
            outs[0][slot] = jnp.where(low, near, 0.0)
        return unused

    lax.fori_loop(0, pairs.shape[0], pick, 0)


def diagonal_values(orders, live, sines):
    order_real = orders.astype(f32)[:, None]
    log_start = 0.5 * jnp.log((2.0 * order_real + 1.0) / (4.0 * math.pi))
    log_start = log_start + 0.5 * (
        lax.lgamma(2.0 * order_real + 1.0)
        - 2.0 * order_real * math.log(2.0)
        - 2.0 * lax.lgamma(order_real + 1.0)
    )
    diagonal = jnp.exp(log_start + order_real * jnp.log(sines)[None, :])
    return jnp.where(live[:, None], diagonal, 0.0)


def legendre_tables(row_table, pair_slots, classes, total, two):
    slots, rows, wide = pair_slots.shape[0], row_table.shape[0], classes.shape[0]
    occupied = (row_table >= 0).astype(f32)
    colatitude = math.pi * (jnp.maximum(row_table, 0).astype(f32) + 0.5) / total
    sines = jnp.sin(colatitude)
    cosine = jnp.broadcast_to(jnp.cos(colatitude)[None, :], (wide, rows))
    spread_out = lambda v: jnp.broadcast_to(v.astype(f32)[:, None], (wide, rows))
    top = LB // 2 if two else LA - 1
    order_a = jnp.where(classes <= top, classes, 0)
    diag_a = diagonal_values(order_a, classes <= top, sines)
    live_b = (classes >= 1) & (classes <= LB // 2 - 1)
    order_b = jnp.where(live_b, LB - classes, 0)
    diag_b = diagonal_values(order_b, live_b, sines)
    class_wide = jnp.broadcast_to(classes[:, None], (wide, rows))
    if two:
        arrays = [spread_out(order_a), spread_out(order_b), diag_a, diag_b, cosine, class_wide]
        body = functools.partial(legendre_body, total)
    else:
        arrays = [spread_out(order_a), diag_a, cosine, class_wide]

        def body(pairs, order, diagonal, cosines, class_ref, *refs):
            legendre_body(total, pairs, order, None, diagonal, None, cosines, class_ref, *refs)

    shape = jax.ShapeDtypeStruct((slots, wide, rows), f32)
    count = 3 if two else 1
    tables = call(
        body,
        "legendre_tables",
        total * wide * rows * 40,
        count * slots * wide * rows * 4,
        in_specs=[pl.BlockSpec(memory_space=pltpu.SMEM)]
        + [pl.BlockSpec(memory_space=pltpu.VMEM)] * len(arrays),
        out_specs=[pl.BlockSpec(memory_space=pltpu.VMEM)] * count,
        out_shape=[shape] * count,
        scratch_shapes=[pltpu.VMEM((total, wide, rows), f32)] * (2 if two else 1),
    )(pair_slots, *arrays)
    plain = [table * occupied for table in tables]
    weight = sines * occupied * (2.0 * math.pi * math.pi / total)
    return plain, [table * weight for table in plain]


def by_class(table, n_lat, pair_dev):
    split = table.reshape(n_lat, pair_dev // 2, 2, table.shape[1], table.shape[2])
    moved = split.transpose(3, 2, 0, 1, 4)[:pair_dev]
    return moved.reshape(pair_dev, n_lat * pair_dev, table.shape[2]).astype(bf16)


def to_degrees_fine_body(pair_dev, n_chunks, *refs):
    chunks, (table_a, table_b, out) = refs[:n_chunks], refs[n_chunks : n_chunks + 3]
    held, result = refs[n_chunks + 3 : -1], refs[-1]
    n_lat, unused, subs, lanes = out.shape
    half = n_lat * pair_dev // 2
    for chunk, keep in zip(chunks, held):
        keep[...] = flat(chunk[...])
    if subs != 2 * pair_dev:
        result[...] = jnp.zeros_like(result)

    def order_rows(sub):
        parts = [
            keep[pl.ds(sub, keep.shape[0] // subs, stride=subs), :] for keep in held
        ]
        return (parts[0] if len(parts) == 1 else jnp.concatenate(parts, axis=0)).astype(bf16)

    for index in range(pair_dev):
        from_a = dot(table_a[index], order_rows(2 * index), 1, 0)
        from_b = dot(table_b[index], order_rows(2 * index + 1), 1, 0)
        first, second = from_a[: 2 * half], from_a[2 * half :] + from_b
        for odd in range(2):
            rows = slice(odd * half, (odd + 1) * half)
            start = odd * subs + index
            result[pl.ds(start + (1 - odd) * pair_dev, half, stride=2 * subs), :] = first[rows]
            result[pl.ds(start + odd * pair_dev, half, stride=2 * subs), :] = second[rows]
    out[...] = result[...].reshape(out.shape).astype(bf16)


def to_degrees_coarse_body(pair_dev, chunk, table, out, held, result):
    n_lat, unused, subs, lanes = out.shape
    half = n_lat * pair_dev // 2
    held[...] = flat(chunk[...])
    if subs != 2 * pair_dev:
        result[...] = jnp.zeros_like(result)
    rows = held.shape[0] // subs
    for index in range(pair_dev):
        taken = jnp.concatenate(
            [held[pl.ds(odd * pair_dev + index, rows, stride=subs), :] for odd in range(2)], axis=0
        ).astype(bf16)
        made = dot(table[index], taken, 1, 0)
        for odd in range(2):
            result[pl.ds(odd * pair_dev + index, half, stride=subs), :] = made[
                odd * half : (odd + 1) * half
            ]
    out[...] = result[...].reshape(out.shape).astype(bf16)


def to_orders_fine_body(pair_dev, n_chunks, chunk, table_a, table_b, *refs):
    outs, (held, *results) = refs[:n_chunks], refs[n_chunks:]
    n_lat, unused, subs, lanes = chunk.shape
    half = n_lat * pair_dev // 2
    held[...] = flat(chunk[...])
    if subs != 2 * pair_dev:
        for result in results:
            result[...] = jnp.zeros_like(result)
    for index in range(pair_dev):
        first, second = [], []
        for odd in range(2):
            start = odd * subs + index
            first.append(held[pl.ds(start + (1 - odd) * pair_dev, half, stride=2 * subs), :])
            second.append(held[pl.ds(start + odd * pair_dev, half, stride=2 * subs), :])
        second = jnp.concatenate(second, axis=0)
        both = jnp.concatenate(first + [second], axis=0).astype(bf16)
        made = (dot(table_a[index], both, 1, 0), dot(table_b[index], second.astype(bf16), 1, 0))
        for member in range(2):
            begin = 0
            for result in results:
                rows = result.shape[0] // subs
                result[pl.ds(2 * index + member, rows, stride=subs), :] = made[member][
                    begin : begin + rows
                ]
                begin += rows
    for out, result in zip(outs, results):
        out[...] = result[...].reshape(out.shape).astype(bf16)


def to_orders_coarse_body(pair_dev, chunk, table, out, held, result):
    n_lat, unused, subs, lanes = chunk.shape
    half = n_lat * pair_dev // 2
    held[...] = flat(chunk[...])
    if subs != 2 * pair_dev:
        result[...] = jnp.zeros_like(result)
    rows = result.shape[0] // subs
    for index in range(pair_dev):
        taken = jnp.concatenate(
            [held[pl.ds(odd * pair_dev + index, half, stride=subs), :] for odd in range(2)], axis=0
        ).astype(bf16)
        made = dot(table[index], taken, 1, 0)
        for odd in range(2):
            result[pl.ds(odd * pair_dev + index, rows, stride=subs), :] = made[
                odd * rows : (odd + 1) * rows
            ]
    out[...] = result[...].reshape(out.shape).astype(bf16)


def lane_call(body, name, inputs, tables, outs):
    tiled = lambda shape: pl.BlockSpec(tuple(shape[:3]) + (TILE,), lambda t: (0, 0, 0, t))
    whole = lambda shape: pl.BlockSpec(shape, lambda t: (0, 0, 0))
    held = lambda shape: pltpu.VMEM((shape[0] * shape[1] * shape[2], TILE), f32)
    moved = sum(2 * math.prod(s) for s in [a.shape for a in inputs] + outs)
    flops = sum(2 * math.prod(t.shape) for t in tables) * LANES
    made = call(
        body,
        name,
        flops,
        moved,
        grid=(LANES // TILE,),
        in_specs=[tiled(a.shape) for a in inputs] + [whole(t.shape) for t in tables],
        out_specs=[tiled(shape) for shape in outs],
        out_shape=[jax.ShapeDtypeStruct(tuple(shape), bf16) for shape in outs],
        scratch_shapes=[held(a.shape) for a in inputs] + [held(shape) for shape in outs],
    )(*inputs, *tables)
    return made


def mix_body(pair_dev, backward, pairs, fine, coarse, weight, fine_out, coarse_out, members):
    n_lat, unused, subs, lanes = fine.shape
    rows = n_lat * subs
    row = lax.broadcasted_iota(jnp.int32, (rows, 1), 0)
    sub = row % subs
    group = sub // pair_dev
    order_class = row // subs * pair_dev + sub % pair_dev
    coarse_rows = flat(coarse[:, 0])
    count = C if backward else WIDE

    def apply(values, slot):
        real, imag = split_parts(values, count)
        stacked = jnp.concatenate([real, imag], axis=0).astype(bf16)
        by_real = dot(stacked, weight[slot, 0], 1, 0 if backward else 1)
        by_imag = dot(stacked, weight[slot, 1], 1, 0 if backward else 1)
        if backward:
            out_real = by_real[:rows] + by_imag[rows:]
            out_imag = by_real[rows:] - by_imag[:rows]
        else:
            out_real = by_real[:rows] - by_imag[rows:]
            out_imag = by_imag[:rows] + by_real[rows:]
        return join_narrow(out_real[:, :C], out_imag[:, :C])

    coarse_made = jnp.zeros((rows, lanes), f32)
    for odd in range(2):
        pair = pairs[2 * pl.program_id(0) + odd]
        own = group == odd
        low = order_class <= pair
        fine_rows = flat(fine[:, odd])
        lower = jnp.where(own, coarse_rows, jnp.where(low, fine_rows, 0.0))
        upper = jnp.where(own | ~low, fine_rows, 0.0)
        members[2 * odd] = lower.reshape(n_lat, subs, lanes).astype(bf16)
        members[2 * odd + 1] = upper.reshape(n_lat, subs, lanes).astype(bf16)
        from_lower = apply(lower, 2 * odd)
        from_upper = apply(upper, 2 * odd + 1)
        made = jnp.where(own, from_upper, from_lower + from_upper)
        fine_out[:, odd] = made.reshape(n_lat, subs, lanes).astype(bf16)
        coarse_made = jnp.where(own, from_lower, coarse_made)
    coarse_out[:, 0] = coarse_made.reshape(n_lat, subs, lanes).astype(bf16)


def mix(fine, coarse, weight, local_pairs, backward):
    n_lat, pair_dev, subs, lanes = fine.shape
    fine_spec = pl.BlockSpec((n_lat, 2, subs, lanes), lambda k, pairs: (0, k, 0, 0))
    coarse_spec = pl.BlockSpec((n_lat, 1, subs, lanes), lambda k, pairs: (0, k, 0, 0))
    return call(
        functools.partial(mix_body, pair_dev, backward),
        "mix_back" if backward else "mix",
        2 * pair_dev * n_lat * subs * 8 * PADDED * PADDED,
        2 * weight.size + 12 * fine.size,
        grid_spec=pltpu.PrefetchScalarGridSpec(
            num_scalar_prefetch=1,
            grid=(pair_dev // 2,),
            in_specs=[
                fine_spec,
                coarse_spec,
                pl.BlockSpec((4,) + weight.shape[1:], lambda k, pairs: (k, 0, 0, 0)),
            ],
            out_specs=[
                fine_spec,
                coarse_spec,
                pl.BlockSpec((4, n_lat, subs, lanes), lambda k, pairs: (k, 0, 0, 0)),
            ],
        ),
        out_shape=[
            jax.ShapeDtypeStruct(fine.shape, bf16),
            jax.ShapeDtypeStruct(coarse.shape, bf16),
            jax.ShapeDtypeStruct((2 * pair_dev, n_lat, subs, lanes), bf16),
        ],
    )(local_pairs, fine, coarse, weight)


def mix_grad_body(n_parts, *refs):
    values, grads, out = refs[:n_parts], refs[n_parts : 2 * n_parts], refs[2 * n_parts]
    gather = lambda parts: jnp.concatenate([flat(part[0]) for part in parts], axis=0)
    value_real, value_imag = [v.astype(bf16) for v in split_parts(gather(values), WIDE)]
    grad_real, grad_imag = [v.astype(bf16) for v in split_parts(gather(grads), C)]
    out[0, 0] = dot(grad_real, value_real, 0, 0) + dot(grad_imag, value_imag, 0, 0)
    out[0, 1] = dot(grad_imag, value_real, 0, 0) - dot(grad_real, value_imag, 0, 0)


def mix_gradient(values, grads):
    slots = values[0].shape[0]
    shape = values[0].shape[1:]
    spec = pl.BlockSpec((1,) + shape, lambda k: (k, 0, 0, 0))
    rows = len(values) * math.prod(shape[:2])
    return call(
        functools.partial(mix_grad_body, len(values)),
        "mix_gradient",
        8 * slots * rows * C * WIDE,
        slots * (4 * rows * LANES + 8 * C * WIDE),
        grid=(slots,),
        in_specs=[spec] * (2 * len(values)),
        out_specs=pl.BlockSpec((1, 2, C, WIDE), lambda k: (k, 0, 0, 0)),
        out_shape=jax.ShapeDtypeStruct((slots, 2, C, WIDE), f32),
    )(*values, *grads)


def pixel_body(
    synth, state, cotangent, table, gain, bias, up, up_turned, up_bias, down, down_turned,
    down_bias, out, middle_grad, synth_grad, up_grad, down_grad, wide_sums, narrow_sums, held,
    wide_held, narrow_held,
):
    step = pl.program_id(0)

    @pl.when(step == 0)
    def _():
        held[...] = jnp.zeros_like(held)
        up_grad[...] = jnp.zeros_like(up_grad)
        down_grad[...] = jnp.zeros_like(down_grad)
        wide_held[...] = jnp.zeros_like(wide_held)
        narrow_held[...] = jnp.zeros_like(narrow_held)

    real, imag = split_parts(flat(synth[:, 0]), C)
    stacked = jnp.concatenate([real, imag], axis=0).astype(bf16)
    middle = state[0][:, 0, :] + dot(stacked, table[...], 0, 0)
    xhat, scale = norm_stats(middle)
    normed_low = (xhat * gain[...] + bias[...]).astype(bf16)
    pre_act = dot(up_turned[...], normed_low, 1, 0) + up_bias[...]
    share = 0.5 * (1.0 + lax.erf(pre_act * math.sqrt(0.5)))
    density = jnp.exp(-0.5 * pre_act * pre_act) * (1.0 / math.sqrt(2.0 * math.pi))
    hidden_low = (pre_act * share).astype(bf16)
    slope = share + pre_act * density
    out[0] = (middle + dot(down_turned[...], hidden_low, 1, 0) + down_bias[...])[:, None, :]
    grad = cotangent[0][:, 0, :]
    grad_low = grad.astype(bf16)
    pre_grad = dot(down[...], grad_low, 1, 0) * slope
    pre_low = pre_grad.astype(bf16)
    wide_held[...] += pre_grad
    down_grad[...] += dot(grad_low, hidden_low, 1, 1)
    up_grad[...] += dot(normed_low, pre_low, 1, 1)
    normed_grad = dot(up[...], pre_low, 1, 0)
    narrow_held[0] += normed_grad * xhat
    narrow_held[1] += normed_grad
    narrow_held[2] += grad
    scaled = normed_grad * gain[...]
    total = grad + scale * (
        scaled
        - jnp.mean(scaled, axis=0, keepdims=True)
        - xhat * jnp.mean(scaled * xhat, axis=0, keepdims=True)
    )
    middle_grad[0] = total
    held[:C] = total
    result = dot(table[...], held[...].astype(bf16), 1, 1)
    rows = result.shape[0] // 2
    joined = join_parts(result[:rows], result[rows:], C)
    synth_grad[:, 0] = joined.reshape(synth_grad.shape[0], synth_grad.shape[2], LANES).astype(bf16)

    @pl.when(step == pl.num_programs(0) - 1)
    def _():
        wide_sums[...] = jnp.sum(wide_held[...], axis=1, keepdims=True)
        narrow_sums[...] = jnp.sum(narrow_held[...], axis=2, keepdims=True)


def pixels(synth, state, cotangent, table, params, first):
    n_lat, count, subs, lanes = synth.shape
    points = state.shape[3]
    hidden = params[2].shape[1]
    row_spec = pl.BlockSpec((1, C, 1, points), lambda r: (r + first, 0, 0, 0))
    const = lambda array: pl.BlockSpec(array.shape, lambda r: (0,) * array.ndim)
    row_out = lambda shape: pl.BlockSpec((1,) + shape, lambda r: (r,) + (0,) * len(shape))
    wave = pl.BlockSpec((n_lat, 1, subs, lanes), lambda r: (0, r, 0, 0))
    whole = lambda shape: pl.BlockSpec(shape, lambda r: (0,) * len(shape))
    shaped = lambda shape, kind=f32: jax.ShapeDtypeStruct(shape, kind)
    return call(
        pixel_body,
        "feed_forward",
        2 * count * points * (6 * C * hidden + 2 * table.shape[0] * PADDED),
        count * (4 * C * points * 4 + 4 * n_lat * subs * lanes),
        grid=(count,),
        in_specs=[wave, row_spec, row_spec, const(table)] + [const(p) for p in params],
        out_specs=[
            row_out((C, 1, points)),
            row_out((C, points)),
            wave,
            whole((C, hidden)),
            whole((C, hidden)),
            whole((hidden, 1)),
            whole((3, C, 1)),
        ],
        out_shape=[
            shaped((count, C, 1, points)),
            shaped((count, C, points)),
            shaped(synth.shape, bf16),
            shaped((C, hidden)),
            shaped((C, hidden)),
            shaped((hidden, 1)),
            shaped((3, C, 1)),
        ],
        scratch_shapes=[
            pltpu.VMEM((PADDED, points), f32),
            pltpu.VMEM((hidden, points), f32),
            pltpu.VMEM((3, C, points), f32),
        ],
    )(synth, state, cotangent, table, *params)


def final_body(wave, state, middle_grad, table, gain, out, sums, held):
    step = pl.program_id(0)

    @pl.when(step == 0)
    def _():
        held[...] = jnp.zeros_like(held)

    real, imag = split_parts(flat(wave[:, 0]), C)
    stacked = jnp.concatenate([real, imag], axis=0).astype(bf16)
    spread_grad = dot(stacked, table[...], 0, 0)
    xhat, scale = norm_stats(state[0][:, 0, :])
    held[0] += spread_grad * xhat
    held[1] += spread_grad
    scaled = spread_grad * gain[...]
    out[0] = (
        middle_grad[0]
        + scale
        * (
            scaled
            - jnp.mean(scaled, axis=0, keepdims=True)
            - xhat * jnp.mean(scaled * xhat, axis=0, keepdims=True)
        )
    )[:, None, :]

    @pl.when(step == pl.num_programs(0) - 1)
    def _():
        sums[...] = jnp.sum(held[...], axis=2, keepdims=True)


def finish(wave, state, middle_grad, table, gain, first):
    n_lat, count, subs, lanes = wave.shape
    points = state.shape[3]
    return call(
        final_body,
        "first_norm_back",
        2 * count * points * table.shape[0] * PADDED,
        count * (3 * C * points * 4 + 2 * n_lat * subs * lanes),
        grid=(count,),
        in_specs=[
            pl.BlockSpec((n_lat, 1, subs, lanes), lambda r: (0, r, 0, 0)),
            pl.BlockSpec((1, C, 1, points), lambda r: (r + first, 0, 0, 0)),
            pl.BlockSpec((1, C, points), lambda r: (r, 0, 0)),
            pl.BlockSpec(table.shape, lambda r: (0, 0)),
            pl.BlockSpec((C, 1), lambda r: (0, 0)),
        ],
        out_specs=[
            pl.BlockSpec((1, C, 1, points), lambda r: (r, 0, 0, 0)),
            pl.BlockSpec((2, C, 1), lambda r: (0, 0, 0)),
        ],
        out_shape=[
            jax.ShapeDtypeStruct((count, C, 1, points), f32),
            jax.ShapeDtypeStruct((2, C, 1), f32),
        ],
        scratch_shapes=[pltpu.VMEM((2, C, points), f32)],
    )(wave, state, middle_grad, table, gain)


def fourier_tables(orders, live, points, lon_count):
    phase = (orders * points % lon_count).astype(f32) * (2.0 * math.pi / lon_count)
    kept = live.astype(f32)
    cosine, sine = jnp.cos(phase) * kept, -jnp.sin(phase) * kept
    doubling = jnp.where(orders == 0, 1.0, 2.0).astype(f32)
    forward = jnp.concatenate([cosine / lon_count, sine / lon_count], axis=0)
    inverse = jnp.concatenate([cosine * doubling, sine * doubling], axis=0)
    return forward.astype(bf16), inverse.astype(bf16)


def order_rows(n_lat, pair_dev, subs):
    index = jnp.arange(n_lat * subs, dtype=jnp.int32)[:, None]
    return index // subs, index % subs


def fine_fourier(n_lat, pair_dev, subs, lon_count):
    device, sub = order_rows(n_lat, pair_dev, subs)
    kind = device * pair_dev + sub // 2
    member = sub % 2
    live = (sub < 2 * pair_dev) & jnp.where(
        member == 0, kind <= LB // 2, (kind >= 1) & (kind <= LB // 2 - 1)
    )
    orders = jnp.where(live, jnp.where(member == 0, kind, LB - kind), 0)
    points = jnp.arange(lon_count, dtype=jnp.int32)[None, :]
    return fourier_tables(orders, live, points, lon_count)


def coarse_fourier(n_lat, pair_dev, subs, lon_count):
    device, sub = order_rows(n_lat, pair_dev, subs)
    order = device * pair_dev + sub % pair_dev
    points = jnp.arange(2 * lon_count, dtype=jnp.int32)[None, :]
    live = (sub < 2 * pair_dev) & (order < LA) & (sub // pair_dev == points // lon_count)
    orders = jnp.where((sub < 2 * pair_dev) & (order < LA), order, 0)
    return fourier_tables(orders, live, points % lon_count, lon_count)


def swap(values):
    return lax.all_to_all(values, "lat", split_axis=0, concat_axis=0, tiled=True)


def share_slots(members, n_chan):
    share = members.shape[0] // n_chan
    rank = lax.axis_index("chan")
    parts = []
    for step in range(n_chan):
        partner = jnp.bitwise_xor(rank, step) if n_chan & (n_chan - 1) == 0 else (rank + step) % n_chan
        block = lax.dynamic_slice_in_dim(members, partner * share, share)
        if step:
            if n_chan & (n_chan - 1) == 0:
                route = [(k, k ^ step) for k in range(n_chan)]
            else:
                route = [(k, (k + step) % n_chan) for k in range(n_chan)]
            block = lax.ppermute(block, "chan", route)
        parts.append(block)
    return parts


def shards(
    n_lat, n_chan, coarse_state, fine_state, coarse_noise, fine_noise, coarse_rows, fine_rows,
    pair_slots, first_gain, first_bias, mix_weight, second_gain, second_bias, up_weight, up_bias,
    down_weight, down_bias, coarse_cotangent, fine_cotangent,
):
    pair_dev = mix_weight.shape[0] // 2
    subs = -(-2 * pair_dev // 8) * 8
    lat_rank = lax.axis_index("lat")
    fine_dev, fine_points = fine_state.shape[1], fine_state.shape[2]
    coarse_dev, coarse_points = coarse_state.shape[1], coarse_state.shape[2]
    coarse_two = coarse_dev // 2
    column = lambda vector: vector[:, None]

    def fine_in(values):
        return values.transpose(1, 3, 0, 2)

    def coarse_in(values):
        paired = values[0].reshape(coarse_two, 2 * coarse_points, values.shape[3])
        return paired.transpose(0, 2, 1)[:, :, None, :]

    def fine_back(values):
        return values.transpose(2, 0, 3, 1)

    def coarse_back(values):
        turned = values[:, :, 0, :].transpose(0, 2, 1)
        return turned.reshape(1, coarse_dev, coarse_points, C)

    coarse_x, fine_x = coarse_in(coarse_state), fine_in(fine_state)
    coarse_g, fine_g = coarse_in(coarse_cotangent), fine_in(fine_cotangent)
    coarse_forward, coarse_inverse = coarse_fourier(n_lat, pair_dev, subs, coarse_points)
    fine_forward, fine_inverse = fine_fourier(n_lat, pair_dev, subs, fine_points)
    gain_one, bias_one = column(first_gain), column(first_bias)

    coarse_four = swap(
        spread(coarse_x, coarse_in(coarse_noise)[:, :, 0, :], gain_one, bias_one, coarse_forward,
               n_lat, 0, coarse_two)
    )
    fine_four = swap(
        spread(fine_x, fine_in(fine_noise)[:, :, 0, :], gain_one, bias_one, fine_forward,
               n_lat, 0, fine_dev)
    )

    wide = -(-pair_dev // 8) * 8
    classes = lat_rank * pair_dev + jnp.arange(wide, dtype=jnp.int32)
    classes = jnp.where(jnp.arange(wide) < pair_dev, classes, LB).astype(jnp.int32)
    coarse_order = coarse_rows.reshape(-1, 2).T.reshape(-1)
    fine_plain, fine_quad = legendre_tables(fine_rows, pair_slots, classes, LB, True)
    coarse_plain, coarse_quad = legendre_tables(coarse_order, pair_slots, classes, LA, False)
    turn = lambda table: by_class(table, n_lat, pair_dev)

    def fine_tables(parts):
        first, near, far = [turn(part) for part in parts]
        table_a = jnp.concatenate([first, near], axis=1)
        return (table_a, far), (table_a.transpose(0, 2, 1), far.transpose(0, 2, 1))

    fine_quad_in, fine_quad_out = fine_tables(fine_quad)
    fine_plain_in, fine_plain_out = fine_tables(fine_plain)
    coarse_quad_in = turn(coarse_quad[0])
    coarse_plain_in = turn(coarse_plain[0])
    coarse_quad_out = coarse_quad_in.transpose(0, 2, 1)
    coarse_plain_out = coarse_plain_in.transpose(0, 2, 1)
    local_pairs = lax.dynamic_slice_in_dim(pair_slots, lat_rank * pair_dev, pair_dev)
    weight = mix_weight.transpose(0, 1, 3, 2)

    fine_degrees = [n_lat, pair_dev, subs, LANES]
    coarse_degrees = [n_lat, pair_dev // 2, subs, LANES]
    fine_waves = [n_lat, fine_dev, subs, LANES]
    coarse_waves = [n_lat, coarse_two, subs, LANES]

    def to_degrees(coarse_chunk, fine_chunks, coarse_table, fine_pair):
        coarse_made = lane_call(
            functools.partial(to_degrees_coarse_body, pair_dev), "rows_to_degrees",
            [coarse_chunk], [coarse_table], [coarse_degrees],
        )[0]
        fine_made = lane_call(
            functools.partial(to_degrees_fine_body, pair_dev, len(fine_chunks)), "rows_to_degrees",
            fine_chunks, list(fine_pair), [fine_degrees],
        )[0]
        return swap(coarse_made), swap(fine_made)

    def to_orders(coarse_chunk, fine_chunk, coarse_table, fine_pair):
        coarse_made = lane_call(
            functools.partial(to_orders_coarse_body, pair_dev), "degrees_to_rows",
            [coarse_chunk], [coarse_table], [coarse_waves],
        )[0]
        fine_made = lane_call(
            functools.partial(to_orders_fine_body, pair_dev, 1), "degrees_to_rows",
            [fine_chunk], list(fine_pair), [fine_waves],
        )[0]
        return swap(coarse_made), swap(fine_made)

    coarse_coef, fine_coef = to_degrees(coarse_four, [fine_four], coarse_quad_in, fine_quad_in)
    fine_mixed, coarse_mixed, members = mix(fine_coef, coarse_coef, weight, local_pairs, False)
    values = share_slots(members, n_chan)
    coarse_synth, fine_synth = to_orders(
        swap(coarse_mixed), swap(fine_mixed), coarse_plain_out, fine_plain_out
    )

    params = [
        column(second_gain), column(second_bias), up_weight, up_weight.T, column(up_bias),
        down_weight, down_weight.T, column(down_bias),
    ]
    coarse_made = pixels(coarse_synth, coarse_x, coarse_g, coarse_inverse, params, 0)
    fine_made = pixels(fine_synth, fine_x, fine_g, fine_inverse, params, 0)
    coarse_sgrad, fine_sgrad = swap(coarse_made[2]), swap(fine_made[2])
    dense = lax.psum(
        tuple(a + b for a, b in zip(coarse_made[3:], fine_made[3:])), ("lat", "chan")
    )

    coarse_dgrad, fine_dgrad = to_degrees(
        coarse_sgrad, [fine_sgrad], coarse_plain_in, fine_plain_in
    )
    fine_cgrad, coarse_cgrad, grad_members = mix(
        fine_dgrad, coarse_dgrad, weight, local_pairs, True
    )
    grads = share_slots(grad_members, n_chan)
    mix_grad = mix_gradient(values, grads).transpose(0, 1, 3, 2)
    coarse_fgrad, fine_fgrad = to_orders(
        swap(coarse_cgrad), swap(fine_cgrad), coarse_quad_out, fine_quad_out
    )
    coarse_end, coarse_sums = finish(
        coarse_fgrad, coarse_x, coarse_made[1], coarse_forward, gain_one, 0
    )
    fine_end, fine_sums = finish(fine_fgrad, fine_x, fine_made[1], fine_forward, gain_one, 0)
    first_sums = lax.psum(coarse_sums + fine_sums, ("lat", "chan"))[:, :, 0]
    up_grad, down_grad, wide_sums, narrow_sums = dense
    return (
        coarse_back(coarse_made[0]),
        fine_back(fine_made[0]),
        coarse_back(coarse_end),
        fine_back(fine_end),
        first_sums[0],
        first_sums[1],
        mix_grad,
        narrow_sums[0, :, 0],
        narrow_sums[1, :, 0],
        up_grad,
        wide_sums[:, 0],
        down_grad.T,
        narrow_sums[2, :, 0],
    )


def solution(mesh):
    pixel = P("chan", "lat", None, None)
    slots = P("lat", None, None, None)
    return jax.shard_map(
        functools.partial(shards, mesh.shape["lat"], mesh.shape["chan"]),
        mesh=mesh,
        in_specs=(pixel,) * 4 + (P(),) * 5 + (slots,) + (P(),) * 6 + (pixel,) * 2,
        out_specs=(pixel,) * 4 + (P(),) * 2 + (P(("lat", "chan"), None, None, None),) + (P(),) * 6,
        check_vma=False,
    )
```

```python
import functools
import math

import jax
import jax.numpy as jnp
from jax import lax
from jax.experimental import pallas as pl
from jax.experimental.pallas import tpu as pltpu
from jax.sharding import PartitionSpec as P

C = 641
NOISE = 8
WIDE = C + NOISE
LA = 90
LB = 180

TILE = 128
MAIN = C // TILE * TILE
HALF = TILE // 2
LANES = 2 * MAIN + TILE
PADDED = MAIN + TILE

epsilon = 1e-05
noise_scale = 1.0 / 262144.0
bf16 = jnp.bfloat16
f32 = jnp.float32
VMEM_LIMIT = 60 * 2**20


def call(body, name, flops, moved, **options):
    scratch = options.pop("scratch_shapes", [])
    return pl.pallas_call(
        body,
        scratch_shapes=scratch,
        compiler_params=pltpu.CompilerParams(vmem_limit_bytes=VMEM_LIMIT),
        cost_estimate=pl.CostEstimate(flops=int(flops), bytes_accessed=int(moved), transcendentals=0),
        name=name,
        **options,
    )


def filled(body, into, position, output=0):
    if into is None:
        return body, [], {}

    def skipping(*refs):
        body(*refs[:position], *refs[position + 1 :])

    return skipping, [pl.BlockSpec(memory_space=pl.ANY)], {position: output}


def dot(left, right, left_dim, right_dim):
    return lax.dot_general(
        left, right, (((left_dim,), (right_dim,)), ((), ())), preferred_element_type=f32
    )


def join_parts(real, imag, count):
    tail = real[:, MAIN:] + pltpu.roll(imag[:, MAIN:], HALF, 1)
    return jnp.concatenate([real[:, :MAIN], imag[:, :MAIN], tail], axis=1)


def join_narrow(real, imag):
    lane = lax.broadcasted_iota(jnp.int32, (real.shape[0], TILE), 1)
    tail = jnp.where(
        lane == 0, real[:, MAIN:C], jnp.where(lane == HALF, imag[:, MAIN:C], 0.0)
    )
    return jnp.concatenate([real[:, :MAIN], imag[:, :MAIN], tail], axis=1)


def split_parts(joined, count):
    tail = joined[:, 2 * MAIN :]
    real = jnp.concatenate([joined[:, :MAIN], tail], axis=1)[:, :count]
    imag = jnp.concatenate(
        [joined[:, MAIN : 2 * MAIN], pltpu.roll(tail, HALF, 1)], axis=1
    )[:, :count]
    return real, imag


def flat(block):
    return block.astype(f32).reshape(-1, block.shape[-1])


def joined_rows(parts):
    return parts[0] if len(parts) == 1 else jnp.concatenate(parts, axis=0)


def norm_stats(values):
    centered = values - jnp.mean(values, axis=0, keepdims=True)
    variance = jnp.mean(centered * centered, axis=0, keepdims=True)
    scale = lax.rsqrt(variance + epsilon)
    return centered * scale, scale


def spread_body(state, noise, gain, bias, table, out, held):
    @pl.when(pl.program_id(0) == 0)
    def _():
        held[...] = jnp.zeros_like(held)

    xhat, unused = norm_stats(state[0][:, 0, :])
    held[:C] = xhat * gain[...] + bias[...]
    held[C:WIDE] = ((noise[0].astype(f32) + 0.5) * noise_scale - 0.5) * math.sqrt(12.0)
    result = dot(table[...], held[...].astype(bf16), 1, 1)
    rows = result.shape[0] // 2
    joined = join_parts(result[:rows], result[rows:], WIDE)
    out[:, 0] = joined.reshape(out.shape[0], out.shape[2], LANES).astype(bf16)


def spread(state, noise, gain, bias, table, n_lat, first, count):
    points = state.shape[3]
    subs = table.shape[0] // (2 * n_lat)
    const = lambda r: (0, 0)
    return call(
        spread_body,
        "norm_and_dft",
        2 * count * table.shape[0] * points * PADDED,
        count * (C * points * 4 + n_lat * subs * LANES * 2),
        grid=(count,),
        in_specs=[
            pl.BlockSpec((1, C, 1, points), lambda r: (r + first, 0, 0, 0)),
            pl.BlockSpec((1, NOISE, points), lambda r: (r + first, 0, 0)),
            pl.BlockSpec((C, 1), const),
            pl.BlockSpec((C, 1), const),
            pl.BlockSpec(table.shape, const),
        ],
        out_specs=pl.BlockSpec((n_lat, 1, subs, LANES), lambda r: (0, r, 0, 0)),
        out_shape=jax.ShapeDtypeStruct((n_lat, count, subs, LANES), bf16),
        scratch_shapes=[pltpu.VMEM((PADDED, points), f32)],
    )(state, noise, gain, bias, table)


def legendre_body(total, pairs, order_a, order_b, diag_a, diag_b, cosine, classes, *refs):
    two = order_b is not None
    outs, (held_a, held_b) = refs[: 3 if two else 1], (refs[3:] if two else (refs[1], None))

    def advance(degree, order, diagonal, previous, earlier):
        real = degree.astype(f32)
        grow = jnp.sqrt(
            (4.0 * real * real - 1.0) / jnp.maximum(real * real - order * order, 1.0)
        )
        damp = jnp.sqrt(
            jnp.maximum((real - 1.0) * (real - 1.0) - order * order, 0.0)
            / jnp.maximum(4.0 * (real - 1.0) * (real - 1.0) - 1.0, 1.0)
        )
        grown = grow * (cosine[...] * previous - damp * earlier)
        return jnp.where(real == order, diagonal, jnp.where(real > order, grown, 0.0))

    def step(degree, carry):
        now_a = advance(degree, order_a[...], diag_a[...], carry[0], carry[1])
        held_a[degree] = now_a
        if not two:
            return (now_a, carry[0])
        now_b = advance(degree, order_b[...], diag_b[...], carry[2], carry[3])
        held_b[degree] = now_b
        return (now_a, carry[0], now_b, carry[2])

    zero = diag_a[...] * 0.0
    lax.fori_loop(0, total, step, (zero,) * (4 if two else 2))

    def pick(slot, unused):
        pair = pairs[slot]
        safe = jnp.maximum(pair, 0)
        live = jnp.where(pair >= 0, 1.0, 0.0)
        low = classes[...] <= pair
        near = held_a[safe] * live
        if two:
            far = held_a[LB - 1 - safe] * live
            outs[0][slot] = jnp.where(low, near, far)
            outs[1][slot] = jnp.where(low, far, 0.0)
            outs[2][slot] = jnp.where(low, 0.0, held_b[LB - 1 - safe] * live)
        else:
            outs[0][slot] = jnp.where(low, near, 0.0)
        return unused

    lax.fori_loop(0, pairs.shape[0], pick, 0)


def diagonal_values(orders, live, sines):
    order_real = orders.astype(f32)[:, None]
    log_start = 0.5 * jnp.log((2.0 * order_real + 1.0) / (4.0 * math.pi))
    log_start = log_start + 0.5 * (
        lax.lgamma(2.0 * order_real + 1.0)
        - 2.0 * order_real * math.log(2.0)
        - 2.0 * lax.lgamma(order_real + 1.0)
    )
    diagonal = jnp.exp(log_start + order_real * jnp.log(sines)[None, :])
    return jnp.where(live[:, None], diagonal, 0.0)


def legendre_tables(row_table, pair_slots, classes, total, two):
    slots, rows, wide = pair_slots.shape[0], row_table.shape[0], classes.shape[0]
    occupied = (row_table >= 0).astype(f32)
    colatitude = math.pi * (jnp.maximum(row_table, 0).astype(f32) + 0.5) / total
    sines = jnp.sin(colatitude)
    cosine = jnp.broadcast_to(jnp.cos(colatitude)[None, :], (wide, rows))
    spread_out = lambda v: jnp.broadcast_to(v.astype(f32)[:, None], (wide, rows))
    top = LB // 2 if two else LA - 1
    order_a = jnp.where(classes <= top, classes, 0)
    diag_a = diagonal_values(order_a, classes <= top, sines)
    live_b = (classes >= 1) & (classes <= LB // 2 - 1)
    order_b = jnp.where(live_b, LB - classes, 0)
    diag_b = diagonal_values(order_b, live_b, sines)
    class_wide = jnp.broadcast_to(classes[:, None], (wide, rows))
    if two:
        arrays = [spread_out(order_a), spread_out(order_b), diag_a, diag_b, cosine, class_wide]
        body = functools.partial(legendre_body, total)
    else:
        arrays = [spread_out(order_a), diag_a, cosine, class_wide]

        def body(pairs, order, diagonal, cosines, class_ref, *refs):
            legendre_body(total, pairs, order, None, diagonal, None, cosines, class_ref, *refs)

    shape = jax.ShapeDtypeStruct((slots, wide, rows), f32)
    count = 3 if two else 1
    tables = call(
        body,
        "legendre_tables",
        total * wide * rows * 40,
        count * slots * wide * rows * 4,
        in_specs=[pl.BlockSpec(memory_space=pltpu.SMEM)]
        + [pl.BlockSpec(memory_space=pltpu.VMEM)] * len(arrays),
        out_specs=[pl.BlockSpec(memory_space=pltpu.VMEM)] * count,
        out_shape=[shape] * count,
        scratch_shapes=[pltpu.VMEM((total, wide, rows), f32)] * (2 if two else 1),
    )(pair_slots, *arrays)
    plain = [table * occupied for table in tables]
    weight = sines * occupied * (2.0 * math.pi * math.pi / total)
    return plain, [table * weight for table in plain]


def by_class(table, n_lat, pair_dev, n_chunks):
    split = table.reshape(n_lat, n_chunks, pair_dev // (2 * n_chunks), 2, *table.shape[1:])
    moved = split.transpose(4, 3, 1, 0, 2, 5)[:pair_dev]
    return moved.reshape(pair_dev, n_lat * pair_dev, table.shape[2]).astype(bf16)


def to_degrees_fine_body(pair_dev, n_in, n_out, *refs):
    chunks, (table_a, table_b), rest = refs[:n_in], refs[n_in : n_in + 2], refs[n_in + 2 :]
    outs, held, results = rest[:n_out], rest[n_out : n_out + n_in], rest[n_out + n_in :]
    n_lat, unused, subs, lanes = outs[0].shape
    half = n_lat * pair_dev // 2
    for chunk, keep in zip(chunks, held):
        keep[...] = flat(chunk[...])
    if subs != 2 * pair_dev:
        for result in results:
            result[...] = jnp.zeros_like(result)

    def order_rows(sub):
        parts = [keep[pl.ds(sub, keep.shape[0] // subs, stride=subs), :] for keep in held]
        return joined_rows(parts).astype(bf16)

    for index in range(pair_dev):
        from_a = dot(table_a[index], order_rows(2 * index), 1, 0)
        from_b = dot(table_b[index], order_rows(2 * index + 1), 1, 0)
        first, second = from_a[: 2 * half], from_a[2 * half :] + from_b
        begin = 0
        for odd in range(2):
            start = odd * subs + index
            for result in results:
                count = result.shape[0] // (2 * subs)
                rows = slice(begin, begin + count)
                begin += count
                result[pl.ds(start + (1 - odd) * pair_dev, count, stride=2 * subs), :] = first[rows]
                result[pl.ds(start + odd * pair_dev, count, stride=2 * subs), :] = second[rows]
    for out, result in zip(outs, results):
        out[...] = result[...].reshape(out.shape).astype(bf16)


def to_degrees_coarse_body(pair_dev, n_in, n_out, chunk, table, out, held, result):
    n_lat, unused, subs, lanes = out.shape
    held[...] = flat(chunk[...])
    if subs != 2 * pair_dev:
        result[...] = jnp.zeros_like(result)
    rows, half = held.shape[0] // subs, result.shape[0] // subs
    for index in range(pair_dev):
        taken = joined_rows(
            [held[pl.ds(odd * pair_dev + index, rows, stride=subs), :] for odd in range(2)]
        ).astype(bf16)
        made = dot(table[index], taken, 1, 0)
        for odd in range(2):
            result[pl.ds(odd * pair_dev + index, half, stride=subs), :] = made[
                odd * half : (odd + 1) * half
            ]
    out[...] = result[...].reshape(out.shape).astype(bf16)


def to_orders_fine_body(pair_dev, n_in, n_out, *refs):
    chunks, (table_a, table_b), rest = refs[:n_in], refs[n_in : n_in + 2], refs[n_in + 2 :]
    outs, held, results = rest[:n_out], rest[n_out : n_out + n_in], rest[n_out + n_in :]
    n_lat, unused, subs, lanes = chunks[0].shape
    for chunk, keep in zip(chunks, held):
        keep[...] = flat(chunk[...])
    if subs != 2 * pair_dev:
        for result in results:
            result[...] = jnp.zeros_like(result)
    for index in range(pair_dev):
        first, second = [], []
        for odd in range(2):
            start = odd * subs + index
            for keep in held:
                count = keep.shape[0] // (2 * subs)
                first.append(keep[pl.ds(start + (1 - odd) * pair_dev, count, stride=2 * subs), :])
                second.append(keep[pl.ds(start + odd * pair_dev, count, stride=2 * subs), :])
        second = joined_rows(second)
        both = joined_rows(first + [second]).astype(bf16)
        made = (dot(table_a[index], both, 1, 0), dot(table_b[index], second.astype(bf16), 1, 0))
        for member in range(2):
            begin = 0
            for result in results:
                rows = result.shape[0] // subs
                result[pl.ds(2 * index + member, rows, stride=subs), :] = made[member][
                    begin : begin + rows
                ]
                begin += rows
    for out, result in zip(outs, results):
        out[...] = result[...].reshape(out.shape).astype(bf16)


def to_orders_coarse_body(pair_dev, n_in, n_out, chunk, table, out, held, result):
    n_lat, unused, subs, lanes = out.shape
    held[...] = flat(chunk[...])
    if subs != 2 * pair_dev:
        result[...] = jnp.zeros_like(result)
    rows, half = result.shape[0] // subs, held.shape[0] // subs
    for index in range(pair_dev):
        taken = joined_rows(
            [held[pl.ds(odd * pair_dev + index, half, stride=subs), :] for odd in range(2)]
        ).astype(bf16)
        made = dot(table[index], taken, 1, 0)
        for odd in range(2):
            result[pl.ds(odd * pair_dev + index, rows, stride=subs), :] = made[
                odd * rows : (odd + 1) * rows
            ]
    out[...] = result[...].reshape(out.shape).astype(bf16)


def lane_call(body, name, inputs, tables, outs):
    tiled = lambda shape: pl.BlockSpec(tuple(shape[:3]) + (TILE,), lambda t: (0, 0, 0, t))
    whole = lambda shape: pl.BlockSpec(shape, lambda t: (0, 0, 0))
    held = lambda shape: pltpu.VMEM((shape[0] * shape[1] * shape[2], TILE), f32)
    moved = sum(2 * math.prod(s) for s in [a.shape for a in inputs] + outs)
    flops = sum(2 * math.prod(t.shape) for t in tables) * LANES
    made = call(
        functools.partial(body, len(inputs), len(outs)),
        name,
        flops,
        moved,
        grid=(LANES // TILE,),
        in_specs=[tiled(a.shape) for a in inputs] + [whole(t.shape) for t in tables],
        out_specs=[tiled(shape) for shape in outs],
        out_shape=[jax.ShapeDtypeStruct(tuple(shape), bf16) for shape in outs],
        scratch_shapes=[held(a.shape) for a in inputs] + [held(shape) for shape in outs],
    )(*inputs, *tables)
    return made


def mix_body(pair_dev, first, backward, pairs, fine, coarse, weight, fine_out, coarse_out, members):
    n_lat, unused, subs, lanes = fine.shape
    rows = n_lat * subs
    row = lax.broadcasted_iota(jnp.int32, (rows, 1), 0)
    sub = row % subs
    group = sub // pair_dev
    order_class = row // subs * pair_dev + sub % pair_dev
    coarse_rows = flat(coarse[:, 0])
    count = C if backward else WIDE

    def apply(values, slot):
        real, imag = split_parts(values, count)
        stacked = jnp.concatenate([real, imag], axis=0).astype(bf16)
        by_real = dot(stacked, weight[slot, 0], 1, 0 if backward else 1)
        by_imag = dot(stacked, weight[slot, 1], 1, 0 if backward else 1)
        if backward:
            out_real = by_real[:rows] + by_imag[rows:]
            out_imag = by_real[rows:] - by_imag[:rows]
        else:
            out_real = by_real[:rows] - by_imag[rows:]
            out_imag = by_imag[:rows] + by_real[rows:]
        return join_narrow(out_real[:, :C], out_imag[:, :C])

    coarse_made = jnp.zeros((rows, lanes), f32)
    for odd in range(2):
        pair = pairs[2 * (pl.program_id(0) + first) + odd]
        own = group == odd
        low = order_class <= pair
        fine_rows = flat(fine[:, odd])
        lower = jnp.where(own, coarse_rows, jnp.where(low, fine_rows, 0.0))
        upper = jnp.where(own | ~low, fine_rows, 0.0)
        members[2 * odd] = lower.reshape(n_lat, subs, lanes).astype(bf16)
        members[2 * odd + 1] = upper.reshape(n_lat, subs, lanes).astype(bf16)
        from_lower = apply(lower, 2 * odd)
        from_upper = apply(upper, 2 * odd + 1)
        made = jnp.where(own, from_upper, from_lower + from_upper)
        fine_out[:, odd] = made.reshape(n_lat, subs, lanes).astype(bf16)
        coarse_made = jnp.where(own, from_lower, coarse_made)
    coarse_out[:, 0] = coarse_made.reshape(n_lat, subs, lanes).astype(bf16)


def mix(fine, coarse, weight, local_pairs, first, backward, into):
    n_lat, count, subs, lanes = fine.shape
    pair_dev = weight.shape[0] // 2
    fine_spec = pl.BlockSpec((n_lat, 2, subs, lanes), lambda k, pairs: (0, k, 0, 0))
    coarse_spec = pl.BlockSpec((n_lat, 1, subs, lanes), lambda k, pairs: (0, k + first, 0, 0))
    body, extra, alias = filled(
        functools.partial(mix_body, pair_dev, first, backward), into, 4, 1
    )
    return call(
        body,
        "mix_back" if backward else "mix",
        2 * count * n_lat * subs * 8 * PADDED * PADDED,
        2 * weight.size * count // pair_dev + 12 * fine.size,
        grid_spec=pltpu.PrefetchScalarGridSpec(
            num_scalar_prefetch=1,
            grid=(count // 2,),
            in_specs=[
                fine_spec,
                coarse_spec,
                pl.BlockSpec((4,) + weight.shape[1:], lambda k, pairs: (k + first, 0, 0, 0)),
            ]
            + extra,
            out_specs=[
                fine_spec,
                coarse_spec,
                pl.BlockSpec((4, n_lat, subs, lanes), lambda k, pairs: (k, 0, 0, 0)),
            ],
        ),
        out_shape=[
            jax.ShapeDtypeStruct(fine.shape, bf16),
            jax.ShapeDtypeStruct(coarse.shape, bf16),
            jax.ShapeDtypeStruct((2 * count, n_lat, subs, lanes), bf16),
        ],
        input_output_aliases=alias,
    )(local_pairs, fine, coarse, weight, *([] if into is None else [into]))


def mix_grad_body(n_parts, *refs):
    values, grads, out = refs[:n_parts], refs[n_parts : 2 * n_parts], refs[2 * n_parts]
    gather = lambda parts: jnp.concatenate([flat(part[0]) for part in parts], axis=0)
    value_real, value_imag = [v.astype(bf16) for v in split_parts(gather(values), WIDE)]
    grad_real, grad_imag = [v.astype(bf16) for v in split_parts(gather(grads), C)]
    out[0, :, 0, :] = dot(grad_real, value_real, 0, 0) + dot(grad_imag, value_imag, 0, 0)
    out[0, :, 1, :] = dot(grad_imag, value_real, 0, 0) - dot(grad_real, value_imag, 0, 0)


def mix_gradient(values, grads):
    slots = values[0].shape[0]
    shape = values[0].shape[1:]
    spec = pl.BlockSpec((1,) + shape, lambda k: (k, 0, 0, 0))
    rows = len(values) * math.prod(shape[:2])
    return call(
        functools.partial(mix_grad_body, len(values)),
        "mix_gradient",
        8 * slots * rows * C * WIDE,
        slots * (4 * rows * LANES + 8 * C * WIDE),
        grid=(slots,),
        in_specs=[spec] * (2 * len(values)),
        out_specs=pl.BlockSpec((1, C, 2, WIDE), lambda k: (k, 0, 0, 0)),
        out_shape=jax.ShapeDtypeStruct((slots, C, 2, WIDE), f32),
    )(*values, *grads)


def pixel_body(
    synth, state, cotangent, table, gain, bias, up, up_turned, up_bias, down, down_turned,
    down_bias, out, middle_grad, synth_grad, up_grad, down_grad, wide_sums, narrow_sums, held,
    wide_held, narrow_held,
):
    step = pl.program_id(0)

    @pl.when(step == 0)
    def _():
        held[...] = jnp.zeros_like(held)
        up_grad[...] = jnp.zeros_like(up_grad)
        down_grad[...] = jnp.zeros_like(down_grad)
        wide_held[...] = jnp.zeros_like(wide_held)
        narrow_held[...] = jnp.zeros_like(narrow_held)

    real, imag = split_parts(flat(synth[:, 0]), C)
    stacked = jnp.concatenate([real, imag], axis=0).astype(bf16)
    middle = state[0][:, 0, :] + dot(stacked, table[...], 0, 0)
    xhat, scale = norm_stats(middle)
    normed_low = (xhat * gain[...] + bias[...]).astype(bf16)
    pre_act = dot(up_turned[...], normed_low, 1, 0) + up_bias[...]
    share = 0.5 * (1.0 + lax.erf(pre_act * math.sqrt(0.5)))
    density = jnp.exp(-0.5 * pre_act * pre_act) * (1.0 / math.sqrt(2.0 * math.pi))
    hidden_low = (pre_act * share).astype(bf16)
    slope = share + pre_act * density
    out[0] = (middle + dot(down_turned[...], hidden_low, 1, 0) + down_bias[...])[:, None, :]
    grad = cotangent[0][:, 0, :]
    grad_low = grad.astype(bf16)
    pre_grad = dot(down[...], grad_low, 1, 0) * slope
    pre_low = pre_grad.astype(bf16)
    wide_held[...] += pre_grad
    down_grad[...] += dot(grad_low, hidden_low, 1, 1)
    up_grad[...] += dot(normed_low, pre_low, 1, 1)
    normed_grad = dot(up[...], pre_low, 1, 0)
    narrow_held[0] += normed_grad * xhat
    narrow_held[1] += normed_grad
    narrow_held[2] += grad
    scaled = normed_grad * gain[...]
    total = grad + scale * (
        scaled
        - jnp.mean(scaled, axis=0, keepdims=True)
        - xhat * jnp.mean(scaled * xhat, axis=0, keepdims=True)
    )
    middle_grad[0] = total
    held[:C] = total
    result = dot(table[...], held[...].astype(bf16), 1, 1)
    rows = result.shape[0] // 2
    joined = join_parts(result[:rows], result[rows:], C)
    synth_grad[:, 0] = joined.reshape(synth_grad.shape[0], synth_grad.shape[2], LANES).astype(bf16)

    @pl.when(step == pl.num_programs(0) - 1)
    def _():
        wide_sums[...] = jnp.sum(wide_held[...], axis=1, keepdims=True)
        narrow_sums[...] = jnp.sum(narrow_held[...], axis=2, keepdims=True)


def pixels(synth, state, cotangent, table, params, first, into):
    n_lat, count, subs, lanes = synth.shape
    points = state.shape[3]
    hidden = params[2].shape[1]
    row_spec = pl.BlockSpec((1, C, 1, points), lambda r: (r + first, 0, 0, 0))
    const = lambda array: pl.BlockSpec(array.shape, lambda r: (0,) * array.ndim)
    row_out = lambda shape: pl.BlockSpec((1,) + shape, lambda r: (r,) + (0,) * len(shape))
    wave = pl.BlockSpec((n_lat, 1, subs, lanes), lambda r: (0, r, 0, 0))
    whole = lambda shape: pl.BlockSpec(shape, lambda r: (0,) * len(shape))
    shaped = lambda shape, kind=f32: jax.ShapeDtypeStruct(shape, kind)
    body, extra, alias = filled(pixel_body, into, 4 + len(params))
    return call(
        body,
        "feed_forward",
        2 * count * points * (6 * C * hidden + 2 * table.shape[0] * PADDED),
        count * (4 * C * points * 4 + 4 * n_lat * subs * lanes),
        grid=(count,),
        in_specs=[wave, row_spec, row_spec, const(table)] + [const(p) for p in params] + extra,
        input_output_aliases=alias,
        out_specs=[
            row_spec,
            row_out((C, points)),
            wave,
            whole((C, hidden)),
            whole((C, hidden)),
            whole((hidden, 1)),
            whole((3, C, 1)),
        ],
        out_shape=[
            shaped(state.shape),
            shaped((count, C, points)),
            shaped(synth.shape, bf16),
            shaped((C, hidden)),
            shaped((C, hidden)),
            shaped((hidden, 1)),
            shaped((3, C, 1)),
        ],
        scratch_shapes=[
            pltpu.VMEM((PADDED, points), f32),
            pltpu.VMEM((hidden, points), f32),
            pltpu.VMEM((3, C, points), f32),
        ],
    )(synth, state, cotangent, table, *params, *([] if into is None else [into]))


def final_body(wave, state, middle_grad, table, gain, out, sums, held):
    step = pl.program_id(0)

    @pl.when(step == 0)
    def _():
        held[...] = jnp.zeros_like(held)

    real, imag = split_parts(flat(wave[:, 0]), C)
    stacked = jnp.concatenate([real, imag], axis=0).astype(bf16)
    spread_grad = dot(stacked, table[...], 0, 0)
    xhat, scale = norm_stats(state[0][:, 0, :])
    held[0] += spread_grad * xhat
    held[1] += spread_grad
    scaled = spread_grad * gain[...]
    out[0] = (
        middle_grad[0]
        + scale
        * (
            scaled
            - jnp.mean(scaled, axis=0, keepdims=True)
            - xhat * jnp.mean(scaled * xhat, axis=0, keepdims=True)
        )
    )[:, None, :]

    @pl.when(step == pl.num_programs(0) - 1)
    def _():
        sums[...] = jnp.sum(held[...], axis=2, keepdims=True)


def finish(wave, state, middle_grad, table, gain, first, into):
    n_lat, count, subs, lanes = wave.shape
    points = state.shape[3]
    body, extra, alias = filled(final_body, into, 5)
    return call(
        body,
        "first_norm_back",
        2 * count * points * table.shape[0] * PADDED,
        count * (3 * C * points * 4 + 2 * n_lat * subs * lanes),
        grid=(count,),
        in_specs=[
            pl.BlockSpec((n_lat, 1, subs, lanes), lambda r: (0, r, 0, 0)),
            pl.BlockSpec((1, C, 1, points), lambda r: (r + first, 0, 0, 0)),
            pl.BlockSpec((1, C, points), lambda r: (r, 0, 0)),
            pl.BlockSpec(table.shape, lambda r: (0, 0)),
            pl.BlockSpec((C, 1), lambda r: (0, 0)),
        ]
        + extra,
        input_output_aliases=alias,
        out_specs=[
            pl.BlockSpec((1, C, 1, points), lambda r: (r + first, 0, 0, 0)),
            pl.BlockSpec((2, C, 1), lambda r: (0, 0, 0)),
        ],
        out_shape=[
            jax.ShapeDtypeStruct(state.shape, f32),
            jax.ShapeDtypeStruct((2, C, 1), f32),
        ],
        scratch_shapes=[pltpu.VMEM((2, C, points), f32)],
    )(wave, state, middle_grad, table, gain, *([] if into is None else [into]))


def part_rows_body(paired, out):
    turned = paired[0][:, 0, :].T
    count = turned.shape[0] // 2
    for half in range(2):
        out[half] = turned[half * count : (half + 1) * count][:, None, :]


def part_rows(paired):
    pairs, points = paired.shape[0], paired.shape[3] // 2
    return call(
        part_rows_body,
        "part_rows",
        0,
        8 * paired.size,
        grid=(pairs,),
        in_specs=[pl.BlockSpec((1, C, 1, 2 * points), lambda r: (r, 0, 0, 0))],
        out_specs=pl.BlockSpec((2, points, 1, C), lambda r: (r, 0, 0, 0)),
        out_shape=jax.ShapeDtypeStruct((2 * pairs, points, 1, C), f32),
    )(paired)


def fourier_tables(orders, live, points, lon_count):
    phase = (orders * points % lon_count).astype(f32) * (2.0 * math.pi / lon_count)
    kept = live.astype(f32)
    cosine, sine = jnp.cos(phase) * kept, -jnp.sin(phase) * kept
    doubling = jnp.where(orders == 0, 1.0, 2.0).astype(f32)
    forward = jnp.concatenate([cosine / lon_count, sine / lon_count], axis=0)
    inverse = jnp.concatenate([cosine * doubling, sine * doubling], axis=0)
    return forward.astype(bf16), inverse.astype(bf16)


def order_rows(n_lat, pair_dev, subs):
    index = jnp.arange(n_lat * subs, dtype=jnp.int32)[:, None]
    return index // subs, index % subs


def fine_fourier(n_lat, pair_dev, subs, lon_count):
    device, sub = order_rows(n_lat, pair_dev, subs)
    kind = device * pair_dev + sub // 2
    member = sub % 2
    live = (sub < 2 * pair_dev) & jnp.where(
        member == 0, kind <= LB // 2, (kind >= 1) & (kind <= LB // 2 - 1)
    )
    orders = jnp.where(live, jnp.where(member == 0, kind, LB - kind), 0)
    points = jnp.arange(lon_count, dtype=jnp.int32)[None, :]
    return fourier_tables(orders, live, points, lon_count)


def coarse_fourier(n_lat, pair_dev, subs, lon_count):
    device, sub = order_rows(n_lat, pair_dev, subs)
    order = device * pair_dev + sub % pair_dev
    points = jnp.arange(2 * lon_count, dtype=jnp.int32)[None, :]
    live = (sub < 2 * pair_dev) & (order < LA) & (sub // pair_dev == points // lon_count)
    orders = jnp.where((sub < 2 * pair_dev) & (order < LA), order, 0)
    return fourier_tables(orders, live, points % lon_count, lon_count)


class Line:
    def __init__(self):
        self.before = self.last = None
        self.work, self.later = [], []
        self.aside = None

    def swap(self, values):
        waits = self.work + ([] if self.last is None else [self.last])
        if waits:
            values = lax.optimization_barrier((values, waits))[0]
        self.before = self.last
        self.last = lax.all_to_all(values, "lat", split_axis=0, concat_axis=0, tiled=True)
        self.work, self.later = self.later, []
        self.step_aside()
        return self.last

    def step_aside(self):
        if self.aside is not None:
            next(self.aside, None)

    def hold(self, values):
        if self.before is None:
            return values
        return lax.optimization_barrier((values, self.before))[0]

    def keep(self, values):
        self.work.append(values)
        return values

    def keep_later(self, values):
        self.later.append(values)
        return values


def partners(count, step):
    if count & (count - 1) == 0:
        return [(k, k ^ step) for k in range(count)], lambda rank: jnp.bitwise_xor(rank, step)
    return [(k, (k + step) % count) for k in range(count)], lambda rank: (rank + step) % count


def share_slots(members, n_chan, step):
    share = members.shape[0] // n_chan
    route, find = partners(n_chan, step)
    block = lax.dynamic_slice_in_dim(members, find(lax.axis_index("chan")) * share, share)
    return lax.ppermute(block, "chan", route) if step else block


def sum_over(values, sizes):
    for axis, size in sizes:
        if size & (size - 1):
            values = lax.psum(values, axis)
            continue
        step = 1
        while step < size:
            values = values + lax.ppermute(values, axis, partners(size, step)[0])
            step *= 2
    return values


def add_dense(arrays, axes, line, result):
    columns = max(array.shape[1] for array in arrays)
    heights = [array.shape[0] for array in arrays]
    steps = [
        (axis, 2**k) for axis, size in axes for k in range(size.bit_length() - 1)
    ]
    rows = -(-sum(heights) // (8 * 2 ** len(steps))) * 8 * 2 ** len(steps)
    wide = [jnp.pad(a, ((0, 0), (0, columns - a.shape[1]))) for a in arrays]
    held = jnp.pad(jnp.concatenate(wide, axis=0), ((0, rows - sum(heights)), (0, 0)))
    sizes = dict(axes)
    odd = lambda axis, step: (lax.axis_index(axis) // step) % 2 == 1
    for axis, step in steps:
        low, high = jnp.split(line.hold(held), 2, axis=0)
        upper = odd(axis, step)
        other = lax.ppermute(jnp.where(upper, low, high), axis, partners(sizes[axis], step)[0])
        held = line.keep_later(jnp.where(upper, high, low) + other)
        yield
    held = held.astype(bf16)
    for axis, step in reversed(steps):
        if (axis, step) == steps[1]:
            yield
        held = line.hold(held)
        upper = odd(axis, step)
        other = lax.ppermute(held, axis, partners(sizes[axis], step)[0])
        held = jnp.concatenate(
            [jnp.where(upper, other, held), jnp.where(upper, held, other)], axis=0
        )
        line.keep_later(held)
        yield
    begin = 0
    for array, height in zip(arrays, heights):
        result.append(held[begin : begin + height, : array.shape[1]].astype(f32))
        begin += height


def shards(
    n_lat, n_chan, coarse_state, fine_state, coarse_noise, fine_noise, coarse_rows, fine_rows,
    pair_slots, first_gain, first_bias, mix_weight, second_gain, second_bias, up_weight, up_bias,
    down_weight, down_bias, coarse_cotangent, fine_cotangent,
):
    pair_dev = mix_weight.shape[0] // 2
    subs = -(-2 * pair_dev // 8) * 8
    lat_rank = lax.axis_index("lat")
    fine_dev, fine_points = fine_state.shape[1], fine_state.shape[2]
    coarse_dev, coarse_points = coarse_state.shape[1], coarse_state.shape[2]
    coarse_two = coarse_dev // 2
    column = lambda vector: vector[:, None]

    def fine_in(values):
        return values.transpose(1, 3, 0, 2)

    def coarse_in(values):
        paired = values[0].reshape(coarse_two, 2 * coarse_points, values.shape[3])
        return paired.transpose(0, 2, 1)[:, :, None, :]

    def fine_back(values):
        return values.transpose(2, 0, 3, 1)

    def coarse_back(values):
        return part_rows(values).transpose(2, 0, 1, 3)

    line = Line()
    row_cuts = [(fine_dev + 1) // 2, fine_dev // 2] if fine_dev >= 8 else [fine_dev]
    row_starts = [sum(row_cuts[:k]) for k in range(len(row_cuts))]
    n_chunks = 2 if pair_dev % 4 == 0 else 1
    chunk_pairs = pair_dev // n_chunks
    chunk_range = range(n_chunks)

    fine_x = fine_in(fine_state)
    fine_noise_in = fine_noise[0].transpose(0, 2, 1)
    fine_forward, fine_inverse = fine_fourier(n_lat, pair_dev, subs, fine_points)
    gain_one, bias_one = column(first_gain), column(first_bias)
    fine_four = []
    for start, count in zip(row_starts, row_cuts):
        made = spread(fine_x, fine_noise_in, gain_one, bias_one, fine_forward, n_lat, start, count)
        fine_four.append(line.swap(line.keep(made)))
    coarse_x = coarse_in(coarse_state)
    coarse_forward, coarse_inverse = coarse_fourier(n_lat, pair_dev, subs, coarse_points)
    coarse_noise_in = coarse_in(coarse_noise)[:, :, 0, :]
    coarse_four = line.swap(
        spread(coarse_x, coarse_noise_in, gain_one, bias_one, coarse_forward, n_lat, 0, coarse_two)
    )

    wide = -(-pair_dev // 8) * 8
    classes = lat_rank * pair_dev + jnp.arange(wide, dtype=jnp.int32)
    classes = jnp.where(jnp.arange(wide) < pair_dev, classes, LB).astype(jnp.int32)
    coarse_order = coarse_rows.reshape(-1, 2).T.reshape(-1)
    by_device = fine_rows.reshape(n_lat, fine_dev)
    fine_order = jnp.concatenate(
        [by_device[:, a : a + c].reshape(-1) for a, c in zip(row_starts, row_cuts)]
    )
    fine_plain, fine_quad = legendre_tables(fine_order, pair_slots, classes, LB, True)
    coarse_plain, coarse_quad = legendre_tables(coarse_order, pair_slots, classes, LA, False)
    turn = lambda table, chunks=n_chunks: by_class(table, n_lat, pair_dev, chunks)

    def fine_tables(parts):
        first, near, far = [turn(part) for part in parts]
        table_a = jnp.concatenate([first, near], axis=1)
        return [table_a, far], [table_a.transpose(0, 2, 1), far.transpose(0, 2, 1)]

    fine_quad_in, fine_quad_out = fine_tables(fine_quad)
    fine_plain_in, fine_plain_out = fine_tables(fine_plain)
    coarse_quad_in = turn(coarse_quad[0], 1)
    coarse_plain_in = turn(coarse_plain[0], 1)
    coarse_quad_out = coarse_quad_in.transpose(0, 2, 1)
    coarse_plain_out = coarse_plain_in.transpose(0, 2, 1)
    local_pairs = lax.dynamic_slice_in_dim(pair_slots, lat_rank * pair_dev, pair_dev)
    weight = mix_weight.transpose(0, 1, 3, 2)

    fine_degrees = [[n_lat, chunk_pairs, subs, LANES]] * n_chunks
    coarse_degrees = [[n_lat, pair_dev // 2, subs, LANES]]
    fine_waves = [[n_lat, count, subs, LANES] for count in row_cuts]
    coarse_waves = [[n_lat, coarse_two, subs, LANES]]

    def spectral(coarse_chunk, fine_chunks, in_tables, out_tables, backward, aside):
        fine_made = lane_call(
            functools.partial(to_degrees_fine_body, pair_dev), "rows_to_degrees",
            line.hold(fine_chunks), in_tables[1], fine_degrees,
        )
        line.keep(fine_made)
        arrived, mixed, shared = [], [], []

        def mix_chunk(k):
            fine, coarse = line.hold((arrived[k], arrived_coarse))
            made = mix(
                fine, coarse, weight, local_pairs, k * chunk_pairs // 2, backward,
                mixed[-1][1] if mixed else None,
            )
            mixed.append(line.keep(made))

        def share_next(count=1):
            members = joined_rows([made[2] for made in mixed])
            for step in range(len(shared), min(len(shared) + count, n_chan)):
                shared.append(line.keep(share_slots(line.hold(members), n_chan, step)))

        arrived.append(line.swap(fine_made[0]))
        coarse_made = lane_call(
            functools.partial(to_degrees_coarse_body, pair_dev), "rows_to_degrees",
            [line.hold(coarse_chunk)], [in_tables[0]], coarse_degrees,
        )[0]
        arrived_coarse = line.swap(line.keep(coarse_made))
        for k in range(1, n_chunks):
            arrived.append(line.swap(fine_made[k]))
            mix_chunk(k - 1)
        if n_chunks == 1:
            mix_chunk(0)
        fine_back = []
        for k in range(n_chunks - 1):
            fine_back.append(line.swap(mixed[k][0]))
            mix_chunk(k + 1)
        arrived_coarse = line.swap(mixed[-1][1])
        share_next(2)
        fine_back.append(line.swap(mixed[-1][0]))
        share_next()
        coarse_made = lane_call(
            functools.partial(to_orders_coarse_body, pair_dev), "degrees_to_rows",
            [line.hold(arrived_coarse)], [out_tables[0]], coarse_waves,
        )[0]
        coarse_end = line.swap(line.keep(coarse_made))
        share_next(n_chan)
        fine_made = lane_call(
            functools.partial(to_orders_fine_body, pair_dev), "degrees_to_rows",
            line.hold(fine_back), out_tables[1], fine_waves,
        )
        line.keep(fine_made)
        fine_end = []
        for k, made in enumerate(fine_made):
            fine_end.append(line.swap(made))
            aside(k, coarse_end, fine_end, shared)
        return fine_end, shared

    params = [
        column(second_gain), column(second_bias), up_weight, up_weight.T, column(up_bias),
        down_weight, down_weight.T, column(down_bias),
    ]
    coarse_g, fine_g = coarse_in(coarse_cotangent), fine_in(fine_cotangent)
    coarse_made, fine_made = [], []

    def fine_pixels(k, synth):
        into = fine_made[-1][0] if fine_made else None
        made = pixels(
            line.hold(synth), fine_x, fine_g, fine_inverse, params, row_starts[k], into
        )
        fine_made.append(line.keep(made))

    def forward_aside(k, coarse_end, fine_end, shared):
        if k == 0:
            made = pixels(
                line.hold(coarse_end), coarse_x, coarse_g, coarse_inverse, params, 0, None
            )
            coarse_made.extend(line.keep(made))
        else:
            if k == 1:
                coarse_made[0] = line.keep(coarse_back(line.hold(coarse_made[0])))
            fine_pixels(k - 1, fine_end[k - 1])

    fine_synth, values = spectral(
        coarse_four, fine_four, (coarse_quad_in, fine_quad_in), (coarse_plain_out, fine_plain_out),
        False, forward_aside,
    )
    if len(row_cuts) == 1:
        fine_pixels(0, fine_synth[0])
    fine_sgrad = []
    for k in range(len(row_cuts)):
        fine_sgrad.append(line.swap(fine_made[k][2]))
        if k + 1 < len(row_cuts):
            fine_pixels(k + 1, fine_synth[k + 1])
    axes = (("chan", n_chan), ("lat", n_lat))
    hidden = up_bias.shape[0]
    total = coarse_made[3:]
    for made in fine_made:
        total = [x + y for x, y in zip(total, made[3:])]
    narrow = jnp.concatenate([total[2][:, 0], total[3].reshape(-1)])
    narrow = jnp.pad(narrow, (0, -narrow.shape[0] % hidden)).reshape(-1, hidden)
    dense = []
    line.aside = add_dense([line.hold(total[0]), total[1], narrow], axes, line, dense)
    line.step_aside()
    coarse_sgrad = line.swap(coarse_made[2])
    if len(row_cuts) == 1:
        coarse_made[0] = coarse_back(coarse_made[0])
    ends, mix_grads = [], []

    def backward_aside(k, coarse_end, fine_end, shared):
        if k == 0:
            mix_grads.append(line.keep(mix_gradient(values, line.hold(shared))))
            made = finish(
                line.hold(coarse_end), coarse_x, coarse_made[1], coarse_forward, gain_one, 0, None
            )
        else:
            if k == 1:
                ends[0][0] = line.keep(coarse_back(line.hold(ends[0][0])))
            into = ends[-1][0] if k > 1 else None
            made = finish(
                line.hold(fine_end[k - 1]), fine_x, fine_made[k - 1][1], fine_forward, gain_one,
                row_starts[k - 1], into,
            )
        ends.append(list(line.keep(made)))

    fine_fgrad, grads = spectral(
        coarse_sgrad, fine_sgrad, (coarse_plain_in, fine_plain_in), (coarse_quad_out, fine_quad_out),
        True, backward_aside,
    )
    for unused in line.aside:
        pass
    up_grad, down_grad, narrow = dense
    narrow = narrow.reshape(-1)
    narrow_sums = narrow[hidden : hidden + 3 * C].reshape(3, C)
    if len(row_cuts) == 1:
        ends[0][0] = coarse_back(ends[0][0])
    into = ends[-1][0] if len(row_cuts) > 1 else None
    last_wave = lax.optimization_barrier((fine_fgrad[-1], line.work + line.later))[0]
    ends.append(
        finish(
            last_wave, fine_x, fine_made[-1][1], fine_forward, gain_one, row_starts[-1], into
        )
    )
    mix_grad = mix_grads[0].transpose(0, 2, 3, 1)
    sums = sum(end[1] for end in ends)
    first_sums = sum_over(sums[:, :, 0], axes)
    return (
        coarse_made[0],
        fine_back(fine_made[-1][0]),
        ends[0][0],
        fine_back(ends[-1][0]),
        first_sums[0],
        first_sums[1],
        mix_grad,
        narrow_sums[0],
        narrow_sums[1],
        up_grad,
        narrow[:hidden],
        down_grad.T,
        narrow_sums[2],
    )


def solution(mesh):
    pixel = P("chan", "lat", None, None)
    slots = P("lat", None, None, None)
    return jax.shard_map(
        functools.partial(shards, mesh.shape["lat"], mesh.shape["chan"]),
        mesh=mesh,
        in_specs=(pixel,) * 4 + (P(),) * 5 + (slots,) + (P(),) * 6 + (pixel,) * 2,
        out_specs=(pixel,) * 4 + (P(),) * 2 + (P(("lat", "chan"), None, None, None),) + (P(),) * 6,
        check_vma=False,
    )
```

```python
import functools
import math

import jax
import jax.numpy as jnp
from jax import lax
from jax.experimental import pallas as pl
from jax.experimental.pallas import tpu as pltpu
from jax.sharding import PartitionSpec as P

C = 641
NOISE = 8
WIDE = C + NOISE
LA = 90
LB = 180

TILE = 128
MAIN = C // TILE * TILE
HALF = TILE // 2
WHOLE = 2 * MAIN
LANES = WHOLE + TILE
PADDED = MAIN + TILE

epsilon = 1e-05
noise_scale = 1.0 / 262144.0
bf16 = jnp.bfloat16
f32 = jnp.float32
VMEM_LIMIT = 60 * 2**20


def call(body, name, flops, moved, **options):
    if "grid_spec" not in options:
        options.setdefault("scratch_shapes", [])
    return pl.pallas_call(
        body,
        compiler_params=pltpu.CompilerParams(vmem_limit_bytes=VMEM_LIMIT),
        cost_estimate=pl.CostEstimate(flops=int(flops), bytes_accessed=int(moved), transcendentals=0),
        name=name,
        **options,
    )


def filled(body, into, position, *outputs):
    if into is None:
        return body, [], {}
    count = len(outputs)

    def skipping(*refs):
        body(*refs[:position], *refs[position + count :])

    alias = {position + k: output for k, output in enumerate(outputs)}
    return skipping, [pl.BlockSpec(memory_space=pl.ANY)] * count, alias


def dot(left, right, left_dim, right_dim):
    return lax.dot_general(
        left, right, (((left_dim,), (right_dim,)), ((), ())), preferred_element_type=f32
    )


def join_parts(real, imag, count):
    tail = real[:, MAIN:] + pltpu.roll(imag[:, MAIN:], HALF, 1)
    return jnp.concatenate([real[:, :MAIN], imag[:, :MAIN], tail], axis=1)


def join_narrow(real, imag):
    lane = lax.broadcasted_iota(jnp.int32, (real.shape[0], TILE), 1)
    tail = jnp.where(
        lane == 0, real[:, MAIN:C], jnp.where(lane == HALF, imag[:, MAIN:C], 0.0)
    )
    return jnp.concatenate([real[:, :MAIN], imag[:, :MAIN], tail], axis=1)


def split_parts(joined, count):
    tail = joined[:, 2 * MAIN :]
    real = jnp.concatenate([joined[:, :MAIN], tail], axis=1)[:, :count]
    imag = jnp.concatenate(
        [joined[:, MAIN : 2 * MAIN], pltpu.roll(tail, HALF, 1)], axis=1
    )[:, :count]
    return real, imag


def packing(rows, width):
    share = HALF // width
    return share, -(-rows // share)


def eights(rows, subs):
    return rows * (subs // 8) + 1


def packed_group(tail, group, subs):
    count = subs // 8
    tiles = [tail[:, :, (group * count + k) * TILE :][:, :, :TILE] for k in range(count)]
    return jnp.stack(tiles, axis=1).reshape(-1, TILE)


def unpacked(group_tile, place, width):
    turned = pltpu.roll(group_tile, (TILE - place * width) % TILE, 1)
    lane = lax.broadcasted_iota(jnp.int32, turned.shape, 1)
    return jnp.where(lane % HALF < width, turned, 0.0)


def last_eight(groups, n_lat, subs):
    count = subs // 8
    tiles = []
    for group in groups:
        split = group.reshape(n_lat, count, 8, TILE)
        tiles += [split[:, k] for k in range(count)]
    blank = jnp.zeros((n_lat, 8, TILE), f32)
    return jnp.concatenate(tiles + [blank] * (WHOLE // TILE - len(tiles)), axis=2)


def flat(block):
    return block.astype(f32).reshape(-1, block.shape[-1])


def joined_rows(parts):
    return parts[0] if len(parts) == 1 else jnp.concatenate(parts, axis=0)


def norm_stats(values):
    centered = values - jnp.mean(values, axis=0, keepdims=True)
    variance = jnp.mean(centered * centered, axis=0, keepdims=True)
    scale = lax.rsqrt(variance + epsilon)
    return centered * scale, scale


def spread_body(state, noise, gain, bias, table, out, held, tails):
    step, last = pl.program_id(0), pl.num_programs(0) - 1
    n_lat, count, unused, lanes = out.shape
    width = WIDE - MAIN
    share = HALF // width

    @pl.when(step == 0)
    def _():
        held[...] = jnp.zeros_like(held)
        tails[...] = jnp.zeros_like(tails)

    @pl.when(step < last)
    def _():
        xhat, unused = norm_stats(state[0][:, 0, :])
        held[:C] = xhat * gain[...] + bias[...]
        held[C:WIDE] = ((noise[0].astype(f32) + 0.5) * noise_scale - 0.5) * math.sqrt(12.0)
        result = dot(table[...], held[...].astype(bf16), 1, 1)
        rows = result.shape[0] // 2
        joined = join_parts(result[:rows], result[rows:], WIDE)
        out[...] = joined[:, :WHOLE].reshape(out.shape).astype(bf16)
        tails[step // share] += pltpu.roll(joined[:, WHOLE:], step % share * width, 1)

    @pl.when(step == last)
    def _():
        groups = [tails[k] for k in range(tails.shape[0])]
        out[:, 0] = last_eight(groups, n_lat, 8 * count).astype(bf16)


def spread(state, noise, gain, bias, table, n_lat, first, count):
    points = state.shape[3]
    subs = table.shape[0] // (2 * n_lat)
    const = lambda r: (0, 0)
    row = lambda r: jnp.minimum(r, count - 1) + first
    return call(
        spread_body,
        "norm_and_dft",
        2 * count * table.shape[0] * points * PADDED,
        count * (C * points * 4 + n_lat * subs * LANES * 2),
        grid=(count + 1,),
        in_specs=[
            pl.BlockSpec((1, C, 1, points), lambda r: (row(r), 0, 0, 0)),
            pl.BlockSpec((1, NOISE, points), lambda r: (row(r), 0, 0)),
            pl.BlockSpec((C, 1), const),
            pl.BlockSpec((C, 1), const),
            pl.BlockSpec(table.shape, const),
        ],
        out_specs=pl.BlockSpec((n_lat, subs // 8, 8, WHOLE), lambda r: (0, r, 0, 0)),
        out_shape=jax.ShapeDtypeStruct((n_lat, eights(count, subs), 8, WHOLE), bf16),
        scratch_shapes=[
            pltpu.VMEM((PADDED, points), f32),
            pltpu.VMEM((packing(count, WIDE - MAIN)[1], n_lat * subs, TILE), f32),
        ],
    )(state, noise, gain, bias, table)


def legendre_body(total, pairs, order_a, order_b, diag_a, diag_b, cosine, classes, *refs):
    two = order_b is not None
    outs, (held_a, held_b) = refs[: 3 if two else 1], (refs[3:] if two else (refs[1], None))

    def advance(degree, order, diagonal, previous, earlier):
        real = degree.astype(f32)
        grow = jnp.sqrt(
            (4.0 * real * real - 1.0) / jnp.maximum(real * real - order * order, 1.0)
        )
        damp = jnp.sqrt(
            jnp.maximum((real - 1.0) * (real - 1.0) - order * order, 0.0)
            / jnp.maximum(4.0 * (real - 1.0) * (real - 1.0) - 1.0, 1.0)
        )
        grown = grow * (cosine[...] * previous - damp * earlier)
        return jnp.where(real == order, diagonal, jnp.where(real > order, grown, 0.0))

    def step(degree, carry):
        now_a = advance(degree, order_a[...], diag_a[...], carry[0], carry[1])
        held_a[degree] = now_a
        if not two:
            return (now_a, carry[0])
        now_b = advance(degree, order_b[...], diag_b[...], carry[2], carry[3])
        held_b[degree] = now_b
        return (now_a, carry[0], now_b, carry[2])

    zero = diag_a[...] * 0.0
    lax.fori_loop(0, total, step, (zero,) * (4 if two else 2))

    def pick(slot, unused):
        pair = pairs[slot]
        safe = jnp.maximum(pair, 0)
        live = jnp.where(pair >= 0, 1.0, 0.0)
        low = classes[...] <= pair
        near = held_a[safe] * live
        if two:
            far = held_a[LB - 1 - safe] * live
            outs[0][slot] = jnp.where(low, near, far)
            outs[1][slot] = jnp.where(low, far, 0.0)
            outs[2][slot] = jnp.where(low, 0.0, held_b[LB - 1 - safe] * live)
        else:
            outs[0][slot] = jnp.where(low, near, 0.0)
        return unused

    lax.fori_loop(0, pairs.shape[0], pick, 0)


def diagonal_values(orders, live, sines):
    order_real = orders.astype(f32)[:, None]
    log_start = 0.5 * jnp.log((2.0 * order_real + 1.0) / (4.0 * math.pi))
    log_start = log_start + 0.5 * (
        lax.lgamma(2.0 * order_real + 1.0)
        - 2.0 * order_real * math.log(2.0)
        - 2.0 * lax.lgamma(order_real + 1.0)
    )
    diagonal = jnp.exp(log_start + order_real * jnp.log(sines)[None, :])
    return jnp.where(live[:, None], diagonal, 0.0)


def legendre_tables(row_table, pair_slots, classes, total, two):
    slots, rows, wide = pair_slots.shape[0], row_table.shape[0], classes.shape[0]
    occupied = (row_table >= 0).astype(f32)
    colatitude = math.pi * (jnp.maximum(row_table, 0).astype(f32) + 0.5) / total
    sines = jnp.sin(colatitude)
    cosine = jnp.broadcast_to(jnp.cos(colatitude)[None, :], (wide, rows))
    spread_out = lambda v: jnp.broadcast_to(v.astype(f32)[:, None], (wide, rows))
    top = LB // 2 if two else LA - 1
    order_a = jnp.where(classes <= top, classes, 0)
    diag_a = diagonal_values(order_a, classes <= top, sines)
    live_b = (classes >= 1) & (classes <= LB // 2 - 1)
    order_b = jnp.where(live_b, LB - classes, 0)
    diag_b = diagonal_values(order_b, live_b, sines)
    class_wide = jnp.broadcast_to(classes[:, None], (wide, rows))
    if two:
        arrays = [spread_out(order_a), spread_out(order_b), diag_a, diag_b, cosine, class_wide]
        body = functools.partial(legendre_body, total)
    else:
        arrays = [spread_out(order_a), diag_a, cosine, class_wide]

        def body(pairs, order, diagonal, cosines, class_ref, *refs):
            legendre_body(total, pairs, order, None, diagonal, None, cosines, class_ref, *refs)

    shape = jax.ShapeDtypeStruct((slots, wide, rows), f32)
    count = 3 if two else 1
    tables = call(
        body,
        "legendre_tables",
        total * wide * rows * 40,
        count * slots * wide * rows * 4,
        in_specs=[pl.BlockSpec(memory_space=pltpu.SMEM)]
        + [pl.BlockSpec(memory_space=pltpu.VMEM)] * len(arrays),
        out_specs=[pl.BlockSpec(memory_space=pltpu.VMEM)] * count,
        out_shape=[shape] * count,
        scratch_shapes=[pltpu.VMEM((total, wide, rows), f32)] * (2 if two else 1),
    )(pair_slots, *arrays)
    plain = [table * occupied for table in tables]
    weight = sines * occupied * (2.0 * math.pi * math.pi / total)
    return plain, [table * weight for table in plain]


def by_class(table, n_lat, pair_dev, n_chunks):
    split = table.reshape(n_lat, n_chunks, pair_dev // (2 * n_chunks), 2, *table.shape[1:])
    moved = split.transpose(4, 3, 1, 0, 2, 5)[:pair_dev]
    return moved.reshape(pair_dev, n_lat * pair_dev, table.shape[2]).astype(bf16)


def to_degrees_fine(pair_dev, subs, tables, held, results):
    table_a, table_b = tables
    half = sum(result.shape[0] for result in results) // (2 * subs)

    def order_rows(sub):
        parts = [keep[pl.ds(sub, keep.shape[0] // subs, stride=subs), :] for keep in held]
        return joined_rows(parts).astype(bf16)

    for index in range(pair_dev):
        from_a = dot(table_a[index], order_rows(2 * index), 1, 0)
        from_b = dot(table_b[index], order_rows(2 * index + 1), 1, 0)
        first, second = from_a[: 2 * half], from_a[2 * half :] + from_b
        begin = 0
        for odd in range(2):
            start = odd * subs + index
            for result in results:
                count = result.shape[0] // (2 * subs)
                rows = slice(begin, begin + count)
                begin += count
                result[pl.ds(start + (1 - odd) * pair_dev, count, stride=2 * subs), :] = first[rows]
                result[pl.ds(start + odd * pair_dev, count, stride=2 * subs), :] = second[rows]


def to_orders_fine(pair_dev, subs, tables, held, results):
    table_a, table_b = tables
    for index in range(pair_dev):
        first, second = [], []
        for odd in range(2):
            start = odd * subs + index
            for keep in held:
                count = keep.shape[0] // (2 * subs)
                first.append(keep[pl.ds(start + (1 - odd) * pair_dev, count, stride=2 * subs), :])
                second.append(keep[pl.ds(start + odd * pair_dev, count, stride=2 * subs), :])
        second = joined_rows(second)
        both = joined_rows(first + [second]).astype(bf16)
        made = (dot(table_a[index], both, 1, 0), dot(table_b[index], second.astype(bf16), 1, 0))
        for member in range(2):
            begin = 0
            for result in results:
                rows = result.shape[0] // subs
                result[pl.ds(2 * index + member, rows, stride=subs), :] = made[member][
                    begin : begin + rows
                ]
                begin += rows


def coarse_either_way(pair_dev, subs, tables, held, results):
    (keep,), (result,), (table,) = held, results, tables
    before, after = keep.shape[0] // subs, result.shape[0] // subs
    for index in range(pair_dev):
        taken = joined_rows(
            [keep[pl.ds(odd * pair_dev + index, before, stride=subs), :] for odd in range(2)]
        ).astype(bf16)
        made = dot(table[index], taken, 1, 0)
        for odd in range(2):
            result[pl.ds(odd * pair_dev + index, after, stride=subs), :] = made[
                odd * after : (odd + 1) * after
            ]


def lane_body(work, subs, width, n_in, n_tables, n_out, *refs):
    cuts = [n_in, n_in, n_tables, n_out, n_in, n_out, n_out]
    mains, tails, tables, outs, held, results, packed = [
        refs[sum(cuts[:k]) : sum(cuts[: k + 1])] for k in range(len(cuts))
    ]
    step = pl.program_id(0)
    n_lat, per = mains[0].shape[0], subs // 8

    @pl.when(step == 0)
    def _():
        for tail, keep in zip(tails, held):
            rows = keep.shape[0] // (n_lat * subs)
            share, groups = packing(rows, width)
            whole = tail[:, 0].astype(f32)
            for group in range(groups):
                tile = packed_group(whole, group, subs)
                for row in range(group * share, min(rows, (group + 1) * share)):
                    own = unpacked(tile, row % share, width)
                    for device in range(n_lat):
                        keep[pl.ds((device * rows + row) * subs, subs), :] = own[
                            device * subs : (device + 1) * subs
                        ]
        for result in results:
            result[...] = jnp.zeros_like(result)

    @pl.when(step > 0)
    def _():
        for main, keep in zip(mains, held):
            keep[...] = flat(main[:, : main.shape[1] - 1])

    work(subs, tables, held, results)

    @pl.when(step == 0)
    def _():
        for result, pack in zip(results, packed):
            rows = result.shape[0] // (n_lat * subs)
            share, groups = packing(rows, width)
            pack[...] = jnp.zeros_like(pack)
            made = result[...].reshape(n_lat, rows, subs, TILE)
            for group in range(groups):
                total = jnp.zeros((n_lat * subs, TILE), f32)
                for row in range(group * share, min(rows, (group + 1) * share)):
                    own = made[:, row].reshape(n_lat * subs, TILE)
                    total = total + pltpu.roll(own, row % share * width, 1)
                split = total.reshape(n_lat, per, 8, TILE)
                for k in range(per):
                    pack[group * per + k] = split[:, k]

    @pl.when(step > 0)
    def _():
        for out, result, pack in zip(outs, results, packed):
            count = out.shape[1] - 1
            out[:, :count] = result[...].reshape(n_lat, count, 8, TILE).astype(bf16)
            out[:, count] = pack[step - 1].astype(bf16)


def lane_call(work, name, inputs, tables, rows_out, subs, width):
    n_lat = inputs[0].shape[0]
    outs = [(n_lat, eights(rows, subs), 8, WHOLE) for rows in rows_out]
    rows_in = [(a.shape[1] - 1) * 8 // subs for a in inputs]
    tiled = lambda shape: pl.BlockSpec(
        tuple(shape[:3]) + (TILE,), lambda t: (0, 0, 0, jnp.maximum(t - 1, 0))
    )
    tail = lambda shape: pl.BlockSpec(
        (shape[0], 1, 8, WHOLE), lambda t, last=shape[1] - 1: (0, last, 0, 0)
    )
    whole = lambda shape: pl.BlockSpec(shape, lambda t: (0, 0, 0))
    held = lambda rows: pltpu.VMEM((n_lat * rows * subs, TILE), f32)
    moved = sum(2 * math.prod(s) for s in [a.shape for a in inputs] + outs)
    flops = sum(2 * math.prod(t.shape) for t in tables) * LANES
    return call(
        functools.partial(lane_body, work, subs, width, len(inputs), len(tables), len(outs)),
        name,
        flops,
        moved,
        grid=(WHOLE // TILE + 1,),
        in_specs=[tiled(a.shape) for a in inputs]
        + [tail(a.shape) for a in inputs]
        + [whole(t.shape) for t in tables],
        out_specs=[tiled(shape) for shape in outs],
        out_shape=[jax.ShapeDtypeStruct(shape, bf16) for shape in outs],
        scratch_shapes=[held(rows) for rows in rows_in]
        + [held(rows) for rows in rows_out]
        + [pltpu.VMEM((WHOLE // TILE, n_lat, 8, TILE), f32) for unused in outs],
    )(*inputs, *inputs, *tables)


def mix_body(
    pair_dev, subs, first, ends, backward, pairs, fine, fine_tail, coarse, coarse_tail, weight,
    carried, fine_out, coarse_out, members, carry, fine_held, coarse_held,
):
    step, last = pl.program_id(0), pl.num_programs(0) - 1
    n_lat, per = fine.shape[0], subs // 8
    rows = n_lat * subs
    width = (C if backward else WIDE) - MAIN
    count = C if backward else WIDE

    @pl.when(step == 0)
    def _():
        fine_held[...] = jnp.zeros_like(fine_held)
        coarse_held[...] = carried[...]

    def apply(values, slot):
        real, imag = split_parts(values, count)
        stacked = jnp.concatenate([real, imag], axis=0).astype(bf16)
        by_real = dot(stacked, weight[slot, 0], 1, 0 if backward else 1)
        by_imag = dot(stacked, weight[slot, 1], 1, 0 if backward else 1)
        if backward:
            out_real = by_real[:rows] + by_imag[rows:]
            out_imag = by_real[rows:] - by_imag[:rows]
        else:
            out_real = by_real[:rows] - by_imag[rows:]
            out_imag = by_imag[:rows] + by_real[rows:]
        return join_narrow(out_real[:, :C], out_imag[:, :C])

    @pl.when(step < last)
    def _():
        row = lax.broadcasted_iota(jnp.int32, (rows, 1), 0)
        sub = row % subs
        group = sub // pair_dev
        order_class = row // subs * pair_dev + sub % pair_dev
        share = HALF // width

        def packed_at(tail, place):
            whole = tail[:, 0].astype(f32)
            groups = packing(WHOLE // TILE // per * share, width)[1]
            tile = packed_group(whole, 0, subs)
            for index in range(1, groups):
                tile = jnp.where(place // share == index, packed_group(whole, index, subs), tile)
            return unpacked(tile, place % share, width)

        coarse_rows = jnp.concatenate(
            [flat(coarse[...]), packed_at(coarse_tail, step + first)], axis=1
        )
        coarse_made = jnp.zeros((rows, LANES), f32)
        for odd in range(2):
            pair = pairs[2 * (step + first) + odd]
            own = group == odd
            low = order_class <= pair
            fine_rows = jnp.concatenate(
                [
                    flat(fine[:, odd * per : (odd + 1) * per]),
                    packed_at(fine_tail, 2 * step + odd),
                ],
                axis=1,
            )
            lower = jnp.where(own, coarse_rows, jnp.where(low, fine_rows, 0.0))
            upper = jnp.where(own | ~low, fine_rows, 0.0)
            members[2 * odd] = lower.reshape(n_lat, subs, LANES).astype(bf16)
            members[2 * odd + 1] = upper.reshape(n_lat, subs, LANES).astype(bf16)
            from_lower = apply(lower, 2 * odd)
            from_upper = apply(upper, 2 * odd + 1)
            made = jnp.where(own, from_upper, from_lower + from_upper)
            fine_out[:, odd * per : (odd + 1) * per] = (
                made[:, :WHOLE].reshape(n_lat, per, 8, WHOLE).astype(bf16)
            )
            fine_held[...] += pltpu.roll(made[:, WHOLE:], 2 * step + odd, 1)
            coarse_made = jnp.where(own, from_lower, coarse_made)
        coarse_out[...] = coarse_made[:, :WHOLE].reshape(coarse_out.shape).astype(bf16)
        coarse_held[...] += pltpu.roll(coarse_made[:, WHOLE:], step + first, 1)

    @pl.when(step == last)
    def _():
        fine_out[:, 0] = last_eight([fine_held[...]], n_lat, subs).astype(bf16)
        carry[...] = coarse_held[...]
        if ends:
            coarse_out[:, 0] = last_eight([coarse_held[...]], n_lat, subs).astype(bf16)


def mix(fine, coarse, weight, local_pairs, subs, first, ends, backward, into, carried):
    n_lat, per = fine.shape[0], subs // 8
    count = (fine.shape[1] - 1) // per
    pair_dev = weight.shape[0] // 2
    turns = count // 2
    inside = lambda k: jnp.minimum(k, turns - 1)
    rows = lambda height, place: pl.BlockSpec(
        (n_lat, height, 8, WHOLE), lambda k, pairs: (0, place(k), 0, 0)
    )
    tail = lambda array: rows(1, lambda k: array.shape[1] - 1)
    whole = pl.BlockSpec((n_lat * subs, TILE), lambda k, pairs: (0, 0))
    body, extra, alias = filled(
        functools.partial(mix_body, pair_dev, subs, first, ends, backward), into, 7, 1
    )
    coarse_place = (lambda k: k + first) if ends else (lambda k: inside(k) + first)
    wave = lambda array: jax.ShapeDtypeStruct(array.shape, bf16)
    return call(
        body,
        "mix_back" if backward else "mix",
        2 * count * n_lat * subs * 8 * PADDED * PADDED,
        2 * weight.size * count // pair_dev + 12 * fine.size,
        grid_spec=pltpu.PrefetchScalarGridSpec(
            num_scalar_prefetch=1,
            grid=(turns + 1,),
            in_specs=[
                rows(2 * per, inside),
                tail(fine),
                rows(per, lambda k: inside(k) + first),
                tail(coarse),
                pl.BlockSpec(
                    (4,) + weight.shape[1:], lambda k, pairs: (inside(k) + first, 0, 0, 0)
                ),
                whole,
            ]
            + extra,
            out_specs=[
                rows(2 * per, lambda k: k),
                rows(per, coarse_place),
                pl.BlockSpec((4, n_lat, subs, LANES), lambda k, pairs: (inside(k), 0, 0, 0)),
                whole,
            ],
            scratch_shapes=[pltpu.VMEM((n_lat * subs, TILE), f32)] * 2,
        ),
        out_shape=[
            wave(fine),
            wave(coarse),
            jax.ShapeDtypeStruct((2 * count, n_lat, subs, LANES), bf16),
            jax.ShapeDtypeStruct((n_lat * subs, TILE), f32),
        ],
        input_output_aliases=alias,
    )(local_pairs, fine, fine, coarse, coarse, weight, carried, *([] if into is None else [into]))


def mix_grad_body(n_parts, *refs):
    values, grads, out = refs[:n_parts], refs[n_parts : 2 * n_parts], refs[2 * n_parts]
    gather = lambda parts: jnp.concatenate([flat(part[0]) for part in parts], axis=0)
    value_real, value_imag = [v.astype(bf16) for v in split_parts(gather(values), WIDE)]
    grad_real, grad_imag = [v.astype(bf16) for v in split_parts(gather(grads), C)]
    out[0, :, 0, :] = dot(grad_real, value_real, 0, 0) + dot(grad_imag, value_imag, 0, 0)
    out[0, :, 1, :] = dot(grad_imag, value_real, 0, 0) - dot(grad_real, value_imag, 0, 0)


def mix_gradient(values, grads):
    slots = values[0].shape[0]
    shape = values[0].shape[1:]
    spec = pl.BlockSpec((1,) + shape, lambda k: (k, 0, 0, 0))
    rows = len(values) * math.prod(shape[:2])
    return call(
        functools.partial(mix_grad_body, len(values)),
        "mix_gradient",
        8 * slots * rows * C * WIDE,
        slots * (4 * rows * LANES + 8 * C * WIDE),
        grid=(slots,),
        in_specs=[spec] * (2 * len(values)),
        out_specs=pl.BlockSpec((1, C, 2, WIDE), lambda k: (k, 0, 0, 0)),
        out_shape=jax.ShapeDtypeStruct((slots, C, 2, WIDE), f32),
    )(*values, *grads)


def pixel_body(
    synth, tail, state, cotangent, table, gain, bias, up, up_turned, up_bias, down, down_turned,
    down_bias, out, middle_grad, synth_grad, up_grad, down_grad, wide_sums, narrow_sums, held,
    wide_held, narrow_held, tails,
):
    step, last = pl.program_id(0), pl.num_programs(0) - 1
    n_lat, per = synth.shape[:2]
    subs = 8 * per

    @pl.when(step == 0)
    def _():
        held[...] = jnp.zeros_like(held)
        up_grad[...] = jnp.zeros_like(up_grad)
        down_grad[...] = jnp.zeros_like(down_grad)
        wide_held[...] = jnp.zeros_like(wide_held)
        narrow_held[...] = jnp.zeros_like(narrow_held)
        tails[...] = jnp.zeros_like(tails)

    @pl.when(step < last)
    def _():
        own = unpacked(packed_group(tail[:, 0].astype(f32), 0, subs), step, C - MAIN)
        real, imag = split_parts(jnp.concatenate([flat(synth[...]), own], axis=1), C)
        stacked = jnp.concatenate([real, imag], axis=0).astype(bf16)
        middle = state[0][:, 0, :] + dot(stacked, table[...], 0, 0)
        xhat, scale = norm_stats(middle)
        normed_low = (xhat * gain[...] + bias[...]).astype(bf16)
        pre_act = dot(up_turned[...], normed_low, 1, 0) + up_bias[...]
        share = 0.5 * (1.0 + lax.erf(pre_act * math.sqrt(0.5)))
        density = jnp.exp(-0.5 * pre_act * pre_act) * (1.0 / math.sqrt(2.0 * math.pi))
        hidden_low = (pre_act * share).astype(bf16)
        slope = share + pre_act * density
        out[0] = (middle + dot(down_turned[...], hidden_low, 1, 0) + down_bias[...])[:, None, :]
        grad = cotangent[0][:, 0, :]
        grad_low = grad.astype(bf16)
        pre_grad = dot(down[...], grad_low, 1, 0) * slope
        pre_low = pre_grad.astype(bf16)
        wide_held[...] += pre_grad
        down_grad[...] += dot(grad_low, hidden_low, 1, 1)
        up_grad[...] += dot(normed_low, pre_low, 1, 1)
        normed_grad = dot(up[...], pre_low, 1, 0)
        narrow_held[0] += normed_grad * xhat
        narrow_held[1] += normed_grad
        narrow_held[2] += grad
        scaled = normed_grad * gain[...]
        total = grad + scale * (
            scaled
            - jnp.mean(scaled, axis=0, keepdims=True)
            - xhat * jnp.mean(scaled * xhat, axis=0, keepdims=True)
        )
        middle_grad[0] = total
        held[:C] = total
        result = dot(table[...], held[...].astype(bf16), 1, 1)
        rows = result.shape[0] // 2
        joined = join_parts(result[:rows], result[rows:], C)
        synth_grad[...] = joined[:, :WHOLE].reshape(synth_grad.shape).astype(bf16)
        tails[...] += pltpu.roll(joined[:, WHOLE:], step, 1)

    @pl.when(step == last)
    def _():
        synth_grad[:, 0] = last_eight([tails[...]], n_lat, subs).astype(bf16)
        wide_sums[...] = jnp.sum(wide_held[...], axis=1, keepdims=True)
        narrow_sums[...] = jnp.sum(narrow_held[...], axis=2, keepdims=True)


def pixels(synth, state, cotangent, table, params, first, into):
    n_lat, subs = synth.shape[0], table.shape[0] // (2 * synth.shape[0])
    per = subs // 8
    count = (synth.shape[1] - 1) // per
    row = lambda r: jnp.minimum(r, count - 1)
    points = state.shape[3]
    hidden = params[2].shape[1]
    row_spec = pl.BlockSpec((1, C, 1, points), lambda r: (row(r) + first, 0, 0, 0))
    const = lambda array: pl.BlockSpec(array.shape, lambda r: (0,) * array.ndim)
    wave = lambda place: pl.BlockSpec((n_lat, per, 8, WHOLE), lambda r: (0, place(r), 0, 0))
    tail = pl.BlockSpec((n_lat, 1, 8, WHOLE), lambda r: (0, count * per, 0, 0))
    whole = lambda shape: pl.BlockSpec(shape, lambda r: (0,) * len(shape))
    shaped = lambda shape, kind=f32: jax.ShapeDtypeStruct(shape, kind)
    body, extra, alias = filled(pixel_body, into, 5 + len(params), 0, 1)
    return call(
        body,
        "feed_forward",
        2 * count * points * (6 * C * hidden + 2 * table.shape[0] * PADDED),
        count * (4 * C * points * 4 + 4 * n_lat * subs * LANES),
        grid=(count + 1,),
        in_specs=[wave(row), tail, row_spec, row_spec, const(table)] + [const(p) for p in params] + extra,
        input_output_aliases=alias,
        out_specs=[
            row_spec,
            pl.BlockSpec((1, C, points), lambda r: (row(r) + first, 0, 0)),
            wave(lambda r: r),
            whole((C, hidden)),
            whole((C, hidden)),
            whole((hidden, 1)),
            whole((3, C, 1)),
        ],
        out_shape=[
            shaped(state.shape),
            shaped((state.shape[0], C, points)),
            shaped(synth.shape, bf16),
            shaped((C, hidden)),
            shaped((C, hidden)),
            shaped((hidden, 1)),
            shaped((3, C, 1)),
        ],
        scratch_shapes=[
            pltpu.VMEM((PADDED, points), f32),
            pltpu.VMEM((hidden, points), f32),
            pltpu.VMEM((3, C, points), f32),
            pltpu.VMEM((n_lat * subs, TILE), f32),
        ],
    )(synth, synth, state, cotangent, table, *params, *([] if into is None else into))


def final_body(wave, tail, state, middle_grad, table, gain, out, sums, held):
    step = pl.program_id(0)

    @pl.when(step == 0)
    def _():
        held[...] = jnp.zeros_like(held)

    own = unpacked(packed_group(tail[:, 0].astype(f32), 0, 8 * wave.shape[1]), step, C - MAIN)
    real, imag = split_parts(jnp.concatenate([flat(wave[...]), own], axis=1), C)
    stacked = jnp.concatenate([real, imag], axis=0).astype(bf16)
    spread_grad = dot(stacked, table[...], 0, 0)
    xhat, scale = norm_stats(state[0][:, 0, :])
    held[0] += spread_grad * xhat
    held[1] += spread_grad
    scaled = spread_grad * gain[...]
    out[0] = (
        middle_grad[0]
        + scale
        * (
            scaled
            - jnp.mean(scaled, axis=0, keepdims=True)
            - xhat * jnp.mean(scaled * xhat, axis=0, keepdims=True)
        )
    )[:, None, :]

    @pl.when(step == pl.num_programs(0) - 1)
    def _():
        sums[...] = jnp.sum(held[...], axis=2, keepdims=True)


def finish(wave, state, middle_grad, table, gain, first, into):
    n_lat, subs = wave.shape[0], table.shape[0] // (2 * wave.shape[0])
    per = subs // 8
    count = (wave.shape[1] - 1) // per
    points = state.shape[3]
    body, extra, alias = filled(final_body, into, 6, 0)
    return call(
        body,
        "first_norm_back",
        2 * count * points * table.shape[0] * PADDED,
        count * (3 * C * points * 4 + 2 * n_lat * subs * LANES),
        grid=(count,),
        in_specs=[
            pl.BlockSpec((n_lat, per, 8, WHOLE), lambda r: (0, r, 0, 0)),
            pl.BlockSpec((n_lat, 1, 8, WHOLE), lambda r: (0, count * per, 0, 0)),
            pl.BlockSpec((1, C, 1, points), lambda r: (r + first, 0, 0, 0)),
            pl.BlockSpec((1, C, points), lambda r: (r + first, 0, 0)),
            pl.BlockSpec(table.shape, lambda r: (0, 0)),
            pl.BlockSpec((C, 1), lambda r: (0, 0)),
        ]
        + extra,
        input_output_aliases=alias,
        out_specs=[
            pl.BlockSpec((1, C, 1, points), lambda r: (r + first, 0, 0, 0)),
            pl.BlockSpec((2, C, 1), lambda r: (0, 0, 0)),
        ],
        out_shape=[
            jax.ShapeDtypeStruct(state.shape, f32),
            jax.ShapeDtypeStruct((2, C, 1), f32),
        ],
        scratch_shapes=[pltpu.VMEM((2, C, points), f32)],
    )(wave, wave, state, middle_grad, table, gain, *([] if into is None else [into]))


def part_rows_body(paired, out):
    turned = paired[0][:, 0, :].T
    count = turned.shape[0] // 2
    for half in range(2):
        out[half] = turned[half * count : (half + 1) * count][:, None, :]


def part_rows(paired):
    pairs, points = paired.shape[0], paired.shape[3] // 2
    return call(
        part_rows_body,
        "part_rows",
        0,
        8 * paired.size,
        grid=(pairs,),
        in_specs=[pl.BlockSpec((1, C, 1, 2 * points), lambda r: (r, 0, 0, 0))],
        out_specs=pl.BlockSpec((2, points, 1, C), lambda r: (r, 0, 0, 0)),
        out_shape=jax.ShapeDtypeStruct((2 * pairs, points, 1, C), f32),
    )(paired)


def fourier_tables(orders, live, points, lon_count):
    phase = (orders * points % lon_count).astype(f32) * (2.0 * math.pi / lon_count)
    kept = live.astype(f32)
    cosine, sine = jnp.cos(phase) * kept, -jnp.sin(phase) * kept
    doubling = jnp.where(orders == 0, 1.0, 2.0).astype(f32)
    forward = jnp.concatenate([cosine / lon_count, sine / lon_count], axis=0)
    inverse = jnp.concatenate([cosine * doubling, sine * doubling], axis=0)
    return forward.astype(bf16), inverse.astype(bf16)


def order_rows(n_lat, pair_dev, subs):
    index = jnp.arange(n_lat * subs, dtype=jnp.int32)[:, None]
    return index // subs, index % subs


def fine_fourier(n_lat, pair_dev, subs, lon_count):
    device, sub = order_rows(n_lat, pair_dev, subs)
    kind = device * pair_dev + sub // 2
    member = sub % 2
    live = (sub < 2 * pair_dev) & jnp.where(
        member == 0, kind <= LB // 2, (kind >= 1) & (kind <= LB // 2 - 1)
    )
    orders = jnp.where(live, jnp.where(member == 0, kind, LB - kind), 0)
    points = jnp.arange(lon_count, dtype=jnp.int32)[None, :]
    return fourier_tables(orders, live, points, lon_count)


def coarse_fourier(n_lat, pair_dev, subs, lon_count):
    device, sub = order_rows(n_lat, pair_dev, subs)
    order = device * pair_dev + sub % pair_dev
    points = jnp.arange(2 * lon_count, dtype=jnp.int32)[None, :]
    live = (sub < 2 * pair_dev) & (order < LA) & (sub // pair_dev == points // lon_count)
    orders = jnp.where((sub < 2 * pair_dev) & (order < LA), order, 0)
    return fourier_tables(orders, live, points % lon_count, lon_count)


class Line:
    def __init__(self):
        self.before = self.last = None
        self.work, self.later = [], []
        self.aside = None

    def swap(self, values):
        waits = self.work + ([] if self.last is None else [self.last])
        if waits:
            values = lax.optimization_barrier((values, waits))[0]
        self.before = self.last
        self.last = lax.all_to_all(values, "lat", split_axis=0, concat_axis=0, tiled=True)
        self.work, self.later = self.later, []
        self.step_aside()
        return self.last

    def step_aside(self):
        if self.aside is not None:
            next(self.aside, None)

    def hold(self, values):
        if self.before is None:
            return values
        return lax.optimization_barrier((values, self.before))[0]

    def keep(self, values):
        self.work.append(values)
        return values

    def keep_later(self, values):
        self.later.append(values)
        return values


def partners(count, step):
    if count & (count - 1) == 0:
        return [(k, k ^ step) for k in range(count)], lambda rank: jnp.bitwise_xor(rank, step)
    return [(k, (k + step) % count) for k in range(count)], lambda rank: (rank + step) % count


def share_slots(members, n_chan, step):
    share = members.shape[0] // n_chan
    route, find = partners(n_chan, step)
    block = lax.dynamic_slice_in_dim(members, find(lax.axis_index("chan")) * share, share)
    return lax.ppermute(block, "chan", route) if step else block


def sum_over(values, sizes):
    for axis, size in sizes:
        if size & (size - 1):
            values = lax.psum(values, axis)
            continue
        step = 1
        while step < size:
            values = values + lax.ppermute(values, axis, partners(size, step)[0])
            step *= 2
    return values


def add_dense(arrays, axes, line, result):
    columns = max(array.shape[1] for array in arrays)
    heights = [array.shape[0] for array in arrays]
    steps = [
        (axis, 2**k) for axis, size in axes for k in range(size.bit_length() - 1)
    ]
    rows = -(-sum(heights) // (8 * 2 ** len(steps))) * 8 * 2 ** len(steps)
    wide = [jnp.pad(a, ((0, 0), (0, columns - a.shape[1]))) for a in arrays]
    held = jnp.pad(jnp.concatenate(wide, axis=0), ((0, rows - sum(heights)), (0, 0)))
    sizes = dict(axes)
    odd = lambda axis, step: (lax.axis_index(axis) // step) % 2 == 1
    for axis, step in steps:
        low, high = jnp.split(line.hold(held), 2, axis=0)
        upper = odd(axis, step)
        other = lax.ppermute(jnp.where(upper, low, high), axis, partners(sizes[axis], step)[0])
        held = line.keep_later(jnp.where(upper, high, low) + other)
        yield
    held = held.astype(bf16)
    for axis, step in reversed(steps):
        if (axis, step) == steps[1]:
            yield
        held = line.hold(held)
        upper = odd(axis, step)
        other = lax.ppermute(held, axis, partners(sizes[axis], step)[0])
        held = jnp.concatenate(
            [jnp.where(upper, other, held), jnp.where(upper, held, other)], axis=0
        )
        line.keep_later(held)
        yield
    begin = 0
    for array, height in zip(arrays, heights):
        result.append(held[begin : begin + height, : array.shape[1]].astype(f32))
        begin += height


def shards(
    n_lat, n_chan, coarse_state, fine_state, coarse_noise, fine_noise, coarse_rows, fine_rows,
    pair_slots, first_gain, first_bias, mix_weight, second_gain, second_bias, up_weight, up_bias,
    down_weight, down_bias, coarse_cotangent, fine_cotangent,
):
    pair_dev = mix_weight.shape[0] // 2
    subs = -(-2 * pair_dev // 8) * 8
    lat_rank = lax.axis_index("lat")
    fine_dev, fine_points = fine_state.shape[1], fine_state.shape[2]
    coarse_dev, coarse_points = coarse_state.shape[1], coarse_state.shape[2]
    coarse_two = coarse_dev // 2
    column = lambda vector: vector[:, None]

    def fine_in(values):
        return values.transpose(1, 3, 0, 2)

    def coarse_in(values):
        paired = values[0].reshape(coarse_two, 2 * coarse_points, values.shape[3])
        return paired.transpose(0, 2, 1)[:, :, None, :]

    def fine_back(values):
        return values.transpose(2, 0, 3, 1)

    def coarse_back(values):
        return part_rows(values).transpose(2, 0, 1, 3)

    line = Line()
    row_cuts = [(fine_dev + 1) // 2, fine_dev // 2] if fine_dev >= 8 else [fine_dev]
    row_starts = [sum(row_cuts[:k]) for k in range(len(row_cuts))]
    outer_cuts = [fine_dev // 4 + 1, fine_dev - fine_dev // 4 - 1] if fine_dev >= 8 else [fine_dev]
    outer_starts = [sum(outer_cuts[:k]) for k in range(len(outer_cuts))]
    n_chunks = 2 if pair_dev % 4 == 0 else 1
    chunk_pairs = pair_dev // n_chunks
    chunk_range = range(n_chunks)

    fine_x = fine_in(fine_state)
    fine_noise_in = fine_noise[0].transpose(0, 2, 1)
    fine_forward, fine_inverse = fine_fourier(n_lat, pair_dev, subs, fine_points)
    gain_one, bias_one = column(first_gain), column(first_bias)
    fine_four = []
    for start, count in zip(outer_starts, outer_cuts):
        made = spread(fine_x, fine_noise_in, gain_one, bias_one, fine_forward, n_lat, start, count)
        fine_four.append(line.swap(line.keep(made)))
    coarse_x = coarse_in(coarse_state)
    coarse_forward, coarse_inverse = coarse_fourier(n_lat, pair_dev, subs, coarse_points)
    coarse_noise_in = coarse_in(coarse_noise)[:, :, 0, :]
    coarse_four = line.swap(
        spread(coarse_x, coarse_noise_in, gain_one, bias_one, coarse_forward, n_lat, 0, coarse_two)
    )

    wide = -(-pair_dev // 8) * 8
    classes = lat_rank * pair_dev + jnp.arange(wide, dtype=jnp.int32)
    classes = jnp.where(jnp.arange(wide) < pair_dev, classes, LB).astype(jnp.int32)
    coarse_order = coarse_rows.reshape(-1, 2).T.reshape(-1)
    by_device = fine_rows.reshape(n_lat, fine_dev)
    in_order = lambda starts, cuts: jnp.concatenate(
        [by_device[:, a : a + c].reshape(-1) for a, c in zip(starts, cuts)]
    )
    unused, fine_quad = legendre_tables(
        in_order(outer_starts, outer_cuts), pair_slots, classes, LB, True
    )
    fine_plain, unused = legendre_tables(
        in_order(row_starts, row_cuts), pair_slots, classes, LB, True
    )
    coarse_plain, coarse_quad = legendre_tables(coarse_order, pair_slots, classes, LA, False)
    turn = lambda table, chunks=n_chunks: by_class(table, n_lat, pair_dev, chunks)

    def fine_tables(parts):
        first, near, far = [turn(part) for part in parts]
        table_a = jnp.concatenate([first, near], axis=1)
        return [table_a, far], [table_a.transpose(0, 2, 1), far.transpose(0, 2, 1)]

    fine_quad_in, fine_quad_out = fine_tables(fine_quad)
    fine_plain_in, fine_plain_out = fine_tables(fine_plain)
    coarse_quad_in = turn(coarse_quad[0], 1)
    coarse_plain_in = turn(coarse_plain[0], 1)
    coarse_quad_out = coarse_quad_in.transpose(0, 2, 1)
    coarse_plain_out = coarse_plain_in.transpose(0, 2, 1)
    local_pairs = lax.dynamic_slice_in_dim(pair_slots, lat_rank * pair_dev, pair_dev)
    weight = mix_weight.transpose(0, 1, 3, 2)

    fine_work = functools.partial(to_degrees_fine, pair_dev)
    fine_back_work = functools.partial(to_orders_fine, pair_dev)
    coarse_work = functools.partial(coarse_either_way, pair_dev)

    def spectral(coarse_chunk, fine_chunks, in_tables, out_tables, cuts, backward, aside):
        wide = (C if backward else WIDE) - MAIN
        fine_made = lane_call(
            fine_work, "rows_to_degrees", line.hold(fine_chunks), in_tables[1],
            [chunk_pairs] * n_chunks, subs, wide,
        )
        line.keep(fine_made)
        arrived, mixed, shared = [], [], []

        def mix_chunk(k):
            fine, coarse = line.hold((arrived[k], arrived_coarse))
            carried = mixed[-1][3] if mixed else jnp.zeros((n_lat * subs, TILE), f32)
            made = mix(
                fine, coarse, weight, local_pairs, subs, k * chunk_pairs // 2, k == n_chunks - 1,
                backward, mixed[-1][1] if mixed else None, carried,
            )
            mixed.append(line.keep(made))

        def share_next(count=1):
            members = joined_rows([made[2] for made in mixed])
            for step in range(len(shared), min(len(shared) + count, n_chan)):
                shared.append(line.keep(share_slots(line.hold(members), n_chan, step)))

        arrived.append(line.swap(fine_made[0]))
        coarse_made = lane_call(
            coarse_work, "rows_to_degrees", [line.hold(coarse_chunk)], [in_tables[0]],
            [pair_dev // 2], subs, wide,
        )[0]
        arrived_coarse = line.swap(line.keep(coarse_made))
        for k in range(1, n_chunks):
            arrived.append(line.swap(fine_made[k]))
            mix_chunk(k - 1)
        if n_chunks == 1:
            mix_chunk(0)
        fine_back = []
        for k in range(n_chunks - 1):
            fine_back.append(line.swap(mixed[k][0]))
            mix_chunk(k + 1)
        arrived_coarse = line.swap(mixed[-1][1])
        share_next(2)
        fine_back.append(line.swap(mixed[-1][0]))
        share_next()
        coarse_made = lane_call(
            coarse_work, "degrees_to_rows", [line.hold(arrived_coarse)], [out_tables[0]],
            [coarse_two], subs, C - MAIN,
        )[0]
        coarse_end = line.swap(line.keep(coarse_made))
        share_next(n_chan)
        fine_made = lane_call(
            fine_back_work, "degrees_to_rows", line.hold(fine_back), out_tables[1],
            cuts, subs, C - MAIN,
        )
        line.keep(fine_made)
        fine_end = [None] * len(cuts)
        order = list(range(len(cuts)))
        if backward:
            order.reverse()
        for k, place in enumerate(order):
            fine_end[place] = line.swap(fine_made[place])
            aside(k, coarse_end, fine_end, shared)
        return fine_end, shared

    params = [
        column(second_gain), column(second_bias), up_weight, up_weight.T, column(up_bias),
        down_weight, down_weight.T, column(down_bias),
    ]
    coarse_g, fine_g = coarse_in(coarse_cotangent), fine_in(fine_cotangent)
    coarse_made, fine_made = [], []

    def fine_pixels(k, synth):
        into = fine_made[-1][:2] if fine_made else None
        made = pixels(
            line.hold(synth), fine_x, fine_g, fine_inverse, params, row_starts[k], into
        )
        fine_made.append(line.keep(made))

    def forward_aside(k, coarse_end, fine_end, shared):
        if k == 0:
            made = pixels(
                line.hold(coarse_end), coarse_x, coarse_g, coarse_inverse, params, 0, None
            )
            coarse_made.extend(line.keep(made))
        else:
            if k == 1:
                coarse_made[0] = line.keep(coarse_back(line.hold(coarse_made[0])))
            fine_pixels(k - 1, fine_end[k - 1])

    fine_synth, values = spectral(
        coarse_four, fine_four, (coarse_quad_in, fine_quad_in), (coarse_plain_out, fine_plain_out),
        row_cuts, False, forward_aside,
    )
    if len(row_cuts) == 1:
        fine_pixels(0, fine_synth[0])
    fine_sgrad = []
    for k in range(len(row_cuts)):
        fine_sgrad.append(line.swap(fine_made[k][2]))
        if k + 1 < len(row_cuts):
            fine_pixels(k + 1, fine_synth[k + 1])
    axes = (("chan", n_chan), ("lat", n_lat))
    hidden = up_bias.shape[0]
    total = coarse_made[3:]
    for made in fine_made:
        total = [x + y for x, y in zip(total, made[3:])]
    narrow = jnp.concatenate([total[2][:, 0], total[3].reshape(-1)])
    narrow = jnp.pad(narrow, (0, -narrow.shape[0] % hidden)).reshape(-1, hidden)
    dense = []
    line.aside = add_dense([line.hold(total[0]), total[1], narrow], axes, line, dense)
    line.step_aside()
    coarse_sgrad = line.swap(coarse_made[2])
    if len(row_cuts) == 1:
        coarse_made[0] = coarse_back(coarse_made[0])
    ends, mix_grads = [], []

    def finish_fine(place, wave):
        into = ends[-1][0] if len(ends) > 1 else None
        return finish(
            wave, fine_x, fine_made[-1][1], fine_forward, gain_one, outer_starts[place], into
        )

    def backward_aside(k, coarse_end, fine_end, shared):
        if k == 0:
            mix_grads.append(line.keep(mix_gradient(values, line.hold(shared))))
            made = finish(
                line.hold(coarse_end), coarse_x, coarse_made[1], coarse_forward, gain_one, 0, None
            )
        else:
            if k == 1:
                ends[0][0] = line.keep(coarse_back(line.hold(ends[0][0])))
            made = finish_fine(len(outer_cuts) - k, line.hold(fine_end[-k]))
        ends.append(list(line.keep(made)))

    fine_fgrad, grads = spectral(
        coarse_sgrad, fine_sgrad, (coarse_plain_in, fine_plain_in), (coarse_quad_out, fine_quad_out),
        outer_cuts, True, backward_aside,
    )
    for unused in line.aside:
        pass
    up_grad, down_grad, narrow = dense
    narrow = narrow.reshape(-1)
    narrow_sums = narrow[hidden : hidden + 3 * C].reshape(3, C)
    if len(row_cuts) == 1:
        ends[0][0] = coarse_back(ends[0][0])
    last_wave = lax.optimization_barrier((fine_fgrad[0], line.work + line.later))[0]
    ends.append(finish_fine(0, last_wave))
    mix_grad = mix_grads[0].transpose(0, 2, 3, 1)
    sums = sum(end[1] for end in ends)
    first_sums = sum_over(sums[:, :, 0], axes)
    return (
        coarse_made[0],
        fine_back(fine_made[-1][0]),
        ends[0][0],
        fine_back(ends[-1][0]),
        first_sums[0],
        first_sums[1],
        mix_grad,
        narrow_sums[0],
        narrow_sums[1],
        up_grad,
        narrow[:hidden],
        down_grad.T,
        narrow_sums[2],
    )


def solution(mesh):
    pixel = P("chan", "lat", None, None)
    slots = P("lat", None, None, None)
    return jax.shard_map(
        functools.partial(shards, mesh.shape["lat"], mesh.shape["chan"]),
        mesh=mesh,
        in_specs=(pixel,) * 4 + (P(),) * 5 + (slots,) + (P(),) * 6 + (pixel,) * 2,
        out_specs=(pixel,) * 4 + (P(),) * 2 + (P(("lat", "chan"), None, None, None),) + (P(),) * 6,
        check_vma=False,
    )
```

```python
import functools
import math

import jax
import jax.numpy as jnp
from jax import lax
from jax.experimental import pallas as pl
from jax.experimental.pallas import tpu as pltpu
from jax.sharding import PartitionSpec as P

C = 641
NOISE = 8
WIDE = C + NOISE
LA = 90
LB = 180

TILE = 128
MAIN = C // TILE * TILE
HALF = TILE // 2
WHOLE = 2 * MAIN
LANES = WHOLE + TILE
PADDED = MAIN + TILE

epsilon = 1e-05
noise_scale = 1.0 / 262144.0
bf16 = jnp.bfloat16
f32 = jnp.float32
VMEM_LIMIT = 60 * 2**20


def call(body, name, flops, moved, **options):
    if "grid_spec" not in options:
        options.setdefault("scratch_shapes", [])
    return pl.pallas_call(
        body,
        compiler_params=pltpu.CompilerParams(vmem_limit_bytes=VMEM_LIMIT),
        cost_estimate=pl.CostEstimate(flops=int(flops), bytes_accessed=int(moved), transcendentals=0),
        name=name,
        **options,
    )


def filled(body, into, position, *outputs):
    if into is None:
        return body, [], {}
    count = len(outputs)

    def skipping(*refs):
        body(*refs[:position], *refs[position + count :])

    alias = {position + k: output for k, output in enumerate(outputs)}
    return skipping, [pl.BlockSpec(memory_space=pl.ANY)] * count, alias


def dot(left, right, left_dim, right_dim):
    return lax.dot_general(
        left, right, (((left_dim,), (right_dim,)), ((), ())), preferred_element_type=f32
    )


def join_parts(real, imag, count):
    tail = real[:, MAIN:] + pltpu.roll(imag[:, MAIN:], HALF, 1)
    return jnp.concatenate([real[:, :MAIN], imag[:, :MAIN], tail], axis=1)


def join_narrow(real, imag):
    lane = lax.broadcasted_iota(jnp.int32, (real.shape[0], TILE), 1)
    tail = jnp.where(
        lane == 0, real[:, MAIN:C], jnp.where(lane == HALF, imag[:, MAIN:C], 0.0)
    )
    return jnp.concatenate([real[:, :MAIN], imag[:, :MAIN], tail], axis=1)


def split_parts(joined, count):
    tail = joined[:, 2 * MAIN :]
    real = jnp.concatenate([joined[:, :MAIN], tail], axis=1)[:, :count]
    imag = jnp.concatenate(
        [joined[:, MAIN : 2 * MAIN], pltpu.roll(tail, HALF, 1)], axis=1
    )[:, :count]
    return real, imag


def packing(rows, width):
    share = HALF // width
    return share, -(-rows // share)


def eights(rows, subs):
    return rows * (subs // 8) + 1


def packed_group(tail, group, subs):
    count = subs // 8
    tiles = [tail[:, :, (group * count + k) * TILE :][:, :, :TILE] for k in range(count)]
    return jnp.stack(tiles, axis=1).reshape(-1, TILE)


def unpacked(group_tile, place, width):
    turned = pltpu.roll(group_tile, (TILE - place * width) % TILE, 1)
    lane = lax.broadcasted_iota(jnp.int32, turned.shape, 1)
    return jnp.where(lane % HALF < width, turned, 0.0)


def last_eight(groups, n_lat, subs):
    count = subs // 8
    tiles = []
    for group in groups:
        split = group.reshape(n_lat, count, 8, TILE)
        tiles += [split[:, k] for k in range(count)]
    blank = jnp.zeros((n_lat, 8, TILE), f32)
    return jnp.concatenate(tiles + [blank] * (WHOLE // TILE - len(tiles)), axis=2)


def flat(block):
    return block.astype(f32).reshape(-1, block.shape[-1])


def joined_rows(parts):
    return parts[0] if len(parts) == 1 else jnp.concatenate(parts, axis=0)


def norm_stats(values):
    centered = values - jnp.mean(values, axis=0, keepdims=True)
    variance = jnp.mean(centered * centered, axis=0, keepdims=True)
    scale = lax.rsqrt(variance + epsilon)
    return centered * scale, scale


def spread_body(state, noise, gain, bias, table, out, held, tails):
    step, last = pl.program_id(0), pl.num_programs(0) - 1
    n_lat, count, unused, lanes = out.shape
    width = WIDE - MAIN
    share = HALF // width

    @pl.when(step == 0)
    def _():
        held[...] = jnp.zeros_like(held)
        tails[...] = jnp.zeros_like(tails)

    @pl.when(step < last)
    def _():
        xhat, unused = norm_stats(state[0][:, 0, :])
        held[:C] = xhat * gain[...] + bias[...]
        held[C:WIDE] = ((noise[0].astype(f32) + 0.5) * noise_scale - 0.5) * math.sqrt(12.0)
        result = dot(table[...], held[...].astype(bf16), 1, 1)
        rows = result.shape[0] // 2
        joined = join_parts(result[:rows], result[rows:], WIDE)
        out[...] = joined[:, :WHOLE].reshape(out.shape).astype(bf16)
        tails[step // share] += pltpu.roll(joined[:, WHOLE:], step % share * width, 1)

    @pl.when(step == last)
    def _():
        groups = [tails[k] for k in range(tails.shape[0])]
        out[:, 0] = last_eight(groups, n_lat, 8 * count).astype(bf16)


def spread(state, noise, gain, bias, table, n_lat, first, count):
    points = state.shape[3]
    subs = table.shape[0] // (2 * n_lat)
    const = lambda r: (0, 0)
    row = lambda r: jnp.minimum(r, count - 1) + first
    return call(
        spread_body,
        "norm_and_dft",
        2 * count * table.shape[0] * points * PADDED,
        count * (C * points * 4 + n_lat * subs * LANES * 2),
        grid=(count + 1,),
        in_specs=[
            pl.BlockSpec((1, C, 1, points), lambda r: (row(r), 0, 0, 0)),
            pl.BlockSpec((1, NOISE, points), lambda r: (row(r), 0, 0)),
            pl.BlockSpec((C, 1), const),
            pl.BlockSpec((C, 1), const),
            pl.BlockSpec(table.shape, const),
        ],
        out_specs=pl.BlockSpec((n_lat, subs // 8, 8, WHOLE), lambda r: (0, r, 0, 0)),
        out_shape=jax.ShapeDtypeStruct((n_lat, eights(count, subs), 8, WHOLE), bf16),
        scratch_shapes=[
            pltpu.VMEM((PADDED, points), f32),
            pltpu.VMEM((packing(count, WIDE - MAIN)[1], n_lat * subs, TILE), f32),
        ],
    )(state, noise, gain, bias, table)


def legendre_body(total, pairs, order_a, order_b, diag_a, diag_b, cosine, classes, *refs):
    two = order_b is not None
    outs, (held_a, held_b) = refs[: 3 if two else 1], (refs[3:] if two else (refs[1], None))

    def advance(degree, order, diagonal, previous, earlier):
        real = degree.astype(f32)
        grow = jnp.sqrt(
            (4.0 * real * real - 1.0) / jnp.maximum(real * real - order * order, 1.0)
        )
        damp = jnp.sqrt(
            jnp.maximum((real - 1.0) * (real - 1.0) - order * order, 0.0)
            / jnp.maximum(4.0 * (real - 1.0) * (real - 1.0) - 1.0, 1.0)
        )
        grown = grow * (cosine[...] * previous - damp * earlier)
        return jnp.where(real == order, diagonal, jnp.where(real > order, grown, 0.0))

    def step(degree, carry):
        now_a = advance(degree, order_a[...], diag_a[...], carry[0], carry[1])
        held_a[degree] = now_a
        if not two:
            return (now_a, carry[0])
        now_b = advance(degree, order_b[...], diag_b[...], carry[2], carry[3])
        held_b[degree] = now_b
        return (now_a, carry[0], now_b, carry[2])

    zero = diag_a[...] * 0.0
    lax.fori_loop(0, total, step, (zero,) * (4 if two else 2))

    def pick(slot, unused):
        pair = pairs[slot]
        safe = jnp.maximum(pair, 0)
        live = jnp.where(pair >= 0, 1.0, 0.0)
        low = classes[...] <= pair
        near = held_a[safe] * live
        if two:
            far = held_a[LB - 1 - safe] * live
            outs[0][slot] = jnp.where(low, near, far)
            outs[1][slot] = jnp.where(low, far, 0.0)
            outs[2][slot] = jnp.where(low, 0.0, held_b[LB - 1 - safe] * live)
        else:
            outs[0][slot] = jnp.where(low, near, 0.0)
        return unused

    lax.fori_loop(0, pairs.shape[0], pick, 0)


def diagonal_values(orders, live, sines):
    order_real = orders.astype(f32)[:, None]
    log_start = 0.5 * jnp.log((2.0 * order_real + 1.0) / (4.0 * math.pi))
    log_start = log_start + 0.5 * (
        lax.lgamma(2.0 * order_real + 1.0)
        - 2.0 * order_real * math.log(2.0)
        - 2.0 * lax.lgamma(order_real + 1.0)
    )
    diagonal = jnp.exp(log_start + order_real * jnp.log(sines)[None, :])
    return jnp.where(live[:, None], diagonal, 0.0)


def legendre_tables(row_table, pair_slots, classes, total, two):
    slots, rows, wide = pair_slots.shape[0], row_table.shape[0], classes.shape[0]
    occupied = (row_table >= 0).astype(f32)
    colatitude = math.pi * (jnp.maximum(row_table, 0).astype(f32) + 0.5) / total
    sines = jnp.sin(colatitude)
    cosine = jnp.broadcast_to(jnp.cos(colatitude)[None, :], (wide, rows))
    spread_out = lambda v: jnp.broadcast_to(v.astype(f32)[:, None], (wide, rows))
    top = LB // 2 if two else LA - 1
    order_a = jnp.where(classes <= top, classes, 0)
    diag_a = diagonal_values(order_a, classes <= top, sines)
    live_b = (classes >= 1) & (classes <= LB // 2 - 1)
    order_b = jnp.where(live_b, LB - classes, 0)
    diag_b = diagonal_values(order_b, live_b, sines)
    class_wide = jnp.broadcast_to(classes[:, None], (wide, rows))
    if two:
        arrays = [spread_out(order_a), spread_out(order_b), diag_a, diag_b, cosine, class_wide]
        body = functools.partial(legendre_body, total)
    else:
        arrays = [spread_out(order_a), diag_a, cosine, class_wide]

        def body(pairs, order, diagonal, cosines, class_ref, *refs):
            legendre_body(total, pairs, order, None, diagonal, None, cosines, class_ref, *refs)

    shape = jax.ShapeDtypeStruct((slots, wide, rows), f32)
    count = 3 if two else 1
    tables = call(
        body,
        "legendre_tables",
        total * wide * rows * 40,
        count * slots * wide * rows * 4,
        in_specs=[pl.BlockSpec(memory_space=pltpu.SMEM)]
        + [pl.BlockSpec(memory_space=pltpu.VMEM)] * len(arrays),
        out_specs=[pl.BlockSpec(memory_space=pltpu.VMEM)] * count,
        out_shape=[shape] * count,
        scratch_shapes=[pltpu.VMEM((total, wide, rows), f32)] * (2 if two else 1),
    )(pair_slots, *arrays)
    plain = [table * occupied for table in tables]
    weight = sines * occupied * (2.0 * math.pi * math.pi / total)
    return plain, [table * weight for table in plain]


def by_class(table, n_lat, pair_dev, n_chunks):
    split = table.reshape(n_lat, n_chunks, pair_dev // (2 * n_chunks), 2, *table.shape[1:])
    moved = split.transpose(4, 3, 1, 0, 2, 5)[:pair_dev]
    return moved.reshape(pair_dev, n_lat * pair_dev, table.shape[2]).astype(bf16)


def to_degrees_fine(pair_dev, subs, tables, held, results):
    table_a, table_b = tables
    half = sum(result.shape[0] for result in results) // (2 * subs)

    def order_rows(sub):
        parts = [keep[pl.ds(sub, keep.shape[0] // subs, stride=subs), :] for keep in held]
        return joined_rows(parts).astype(bf16)

    for index in range(pair_dev):
        from_a = dot(table_a[index], order_rows(2 * index), 1, 0)
        from_b = dot(table_b[index], order_rows(2 * index + 1), 1, 0)
        first, second = from_a[: 2 * half], from_a[2 * half :] + from_b
        begin = 0
        for odd in range(2):
            start = odd * subs + index
            for result in results:
                count = result.shape[0] // (2 * subs)
                rows = slice(begin, begin + count)
                begin += count
                result[pl.ds(start + (1 - odd) * pair_dev, count, stride=2 * subs), :] = first[rows]
                result[pl.ds(start + odd * pair_dev, count, stride=2 * subs), :] = second[rows]


def to_orders_fine(pair_dev, subs, tables, held, results):
    table_a, table_b = tables
    for index in range(pair_dev):
        first, second = [], []
        for odd in range(2):
            start = odd * subs + index
            for keep in held:
                count = keep.shape[0] // (2 * subs)
                first.append(keep[pl.ds(start + (1 - odd) * pair_dev, count, stride=2 * subs), :])
                second.append(keep[pl.ds(start + odd * pair_dev, count, stride=2 * subs), :])
        second = joined_rows(second)
        both = joined_rows(first + [second]).astype(bf16)
        made = (dot(table_a[index], both, 1, 0), dot(table_b[index], second.astype(bf16), 1, 0))
        for member in range(2):
            begin = 0
            for result in results:
                rows = result.shape[0] // subs
                result[pl.ds(2 * index + member, rows, stride=subs), :] = made[member][
                    begin : begin + rows
                ]
                begin += rows


def coarse_either_way(pair_dev, subs, tables, held, results):
    (keep,), (result,), (table,) = held, results, tables
    before, after = keep.shape[0] // subs, result.shape[0] // subs
    for index in range(pair_dev):
        taken = joined_rows(
            [keep[pl.ds(odd * pair_dev + index, before, stride=subs), :] for odd in range(2)]
        ).astype(bf16)
        made = dot(table[index], taken, 1, 0)
        for odd in range(2):
            result[pl.ds(odd * pair_dev + index, after, stride=subs), :] = made[
                odd * after : (odd + 1) * after
            ]


def lane_body(work, subs, width, n_in, n_tables, n_out, *refs):
    cuts = [n_in, n_in, n_tables, n_out, n_in, n_out, n_out]
    mains, tails, tables, outs, held, results, packed = [
        refs[sum(cuts[:k]) : sum(cuts[: k + 1])] for k in range(len(cuts))
    ]
    step = pl.program_id(0)
    n_lat, per = mains[0].shape[0], subs // 8

    @pl.when(step == 0)
    def _():
        for tail, keep in zip(tails, held):
            rows = keep.shape[0] // (n_lat * subs)
            share, groups = packing(rows, width)
            whole = tail[:, 0].astype(f32)
            for group in range(groups):
                tile = packed_group(whole, group, subs)
                for row in range(group * share, min(rows, (group + 1) * share)):
                    own = unpacked(tile, row % share, width)
                    for device in range(n_lat):
                        keep[pl.ds((device * rows + row) * subs, subs), :] = own[
                            device * subs : (device + 1) * subs
                        ]
        for result in results:
            result[...] = jnp.zeros_like(result)

    @pl.when(step > 0)
    def _():
        for main, keep in zip(mains, held):
            keep[...] = flat(main[:, : main.shape[1] - 1])

    work(subs, tables, held, results)

    @pl.when(step == 0)
    def _():
        for result, pack in zip(results, packed):
            rows = result.shape[0] // (n_lat * subs)
            share, groups = packing(rows, width)
            pack[...] = jnp.zeros_like(pack)
            made = result[...].reshape(n_lat, rows, subs, TILE)
            for group in range(groups):
                total = jnp.zeros((n_lat * subs, TILE), f32)
                for row in range(group * share, min(rows, (group + 1) * share)):
                    own = made[:, row].reshape(n_lat * subs, TILE)
                    total = total + pltpu.roll(own, row % share * width, 1)
                split = total.reshape(n_lat, per, 8, TILE)
                for k in range(per):
                    pack[group * per + k] = split[:, k]

    @pl.when(step > 0)
    def _():
        for out, result, pack in zip(outs, results, packed):
            count = out.shape[1] - 1
            out[:, :count] = result[...].reshape(n_lat, count, 8, TILE).astype(bf16)
            out[:, count] = pack[step - 1].astype(bf16)


def lane_call(work, name, inputs, tables, rows_out, subs, width):
    n_lat = inputs[0].shape[0]
    outs = [(n_lat, eights(rows, subs), 8, WHOLE) for rows in rows_out]
    rows_in = [(a.shape[1] - 1) * 8 // subs for a in inputs]
    tiled = lambda shape: pl.BlockSpec(
        tuple(shape[:3]) + (TILE,), lambda t: (0, 0, 0, jnp.maximum(t - 1, 0))
    )
    tail = lambda shape: pl.BlockSpec(
        (shape[0], 1, 8, WHOLE), lambda t, last=shape[1] - 1: (0, last, 0, 0)
    )
    whole = lambda shape: pl.BlockSpec(shape, lambda t: (0, 0, 0))
    held = lambda rows: pltpu.VMEM((n_lat * rows * subs, TILE), f32)
    moved = sum(2 * math.prod(s) for s in [a.shape for a in inputs] + outs)
    flops = sum(2 * math.prod(t.shape) for t in tables) * LANES
    return call(
        functools.partial(lane_body, work, subs, width, len(inputs), len(tables), len(outs)),
        name,
        flops,
        moved,
        grid=(WHOLE // TILE + 1,),
        in_specs=[tiled(a.shape) for a in inputs]
        + [tail(a.shape) for a in inputs]
        + [whole(t.shape) for t in tables],
        out_specs=[tiled(shape) for shape in outs],
        out_shape=[jax.ShapeDtypeStruct(shape, bf16) for shape in outs],
        scratch_shapes=[held(rows) for rows in rows_in]
        + [held(rows) for rows in rows_out]
        + [pltpu.VMEM((WHOLE // TILE, n_lat, 8, TILE), f32) for unused in outs],
    )(*inputs, *inputs, *tables)


def mix_body(
    pair_dev, subs, first, ends, backward, pairs, fine, fine_tail, coarse, coarse_tail, weight,
    carried, fine_out, coarse_out, members, carry, fine_held, coarse_held,
):
    step, last = pl.program_id(0), pl.num_programs(0) - 1
    n_lat, per = fine.shape[0], subs // 8
    rows = n_lat * subs
    width = (C if backward else WIDE) - MAIN
    count = C if backward else WIDE

    @pl.when(step == 0)
    def _():
        fine_held[...] = jnp.zeros_like(fine_held)
        coarse_held[...] = carried[...]

    def apply(values, slot):
        real, imag = split_parts(values, count)
        stacked = jnp.concatenate([real, imag], axis=0).astype(bf16)
        by_real = dot(stacked, weight[slot, 0], 1, 0 if backward else 1)
        by_imag = dot(stacked, weight[slot, 1], 1, 0 if backward else 1)
        if backward:
            out_real = by_real[:rows] + by_imag[rows:]
            out_imag = by_real[rows:] - by_imag[:rows]
        else:
            out_real = by_real[:rows] - by_imag[rows:]
            out_imag = by_imag[:rows] + by_real[rows:]
        return join_narrow(out_real[:, :C], out_imag[:, :C])

    @pl.when(step < last)
    def _():
        row = lax.broadcasted_iota(jnp.int32, (rows, 1), 0)
        sub = row % subs
        group = sub // pair_dev
        order_class = row // subs * pair_dev + sub % pair_dev
        share = HALF // width

        def packed_at(tail, place):
            whole = tail[:, 0].astype(f32)
            groups = packing(WHOLE // TILE // per * share, width)[1]
            tile = packed_group(whole, 0, subs)
            for index in range(1, groups):
                tile = jnp.where(place // share == index, packed_group(whole, index, subs), tile)
            return unpacked(tile, place % share, width)

        coarse_rows = jnp.concatenate(
            [flat(coarse[...]), packed_at(coarse_tail, step + first)], axis=1
        )
        coarse_made = jnp.zeros((rows, LANES), f32)
        for odd in range(2):
            pair = pairs[2 * (step + first) + odd]
            own = group == odd
            low = order_class <= pair
            fine_rows = jnp.concatenate(
                [
                    flat(fine[:, odd * per : (odd + 1) * per]),
                    packed_at(fine_tail, 2 * step + odd),
                ],
                axis=1,
            )
            lower = jnp.where(own, coarse_rows, jnp.where(low, fine_rows, 0.0))
            upper = jnp.where(own | ~low, fine_rows, 0.0)
            members[2 * odd] = lower.reshape(n_lat, subs, LANES).astype(bf16)
            members[2 * odd + 1] = upper.reshape(n_lat, subs, LANES).astype(bf16)
            from_lower = apply(lower, 2 * odd)
            from_upper = apply(upper, 2 * odd + 1)
            made = jnp.where(own, from_upper, from_lower + from_upper)
            fine_out[:, odd * per : (odd + 1) * per] = (
                made[:, :WHOLE].reshape(n_lat, per, 8, WHOLE).astype(bf16)
            )
            fine_held[...] += pltpu.roll(made[:, WHOLE:], 2 * step + odd, 1)
            coarse_made = jnp.where(own, from_lower, coarse_made)
        coarse_out[...] = coarse_made[:, :WHOLE].reshape(coarse_out.shape).astype(bf16)
        coarse_held[...] += pltpu.roll(coarse_made[:, WHOLE:], step + first, 1)

    @pl.when(step == last)
    def _():
        fine_out[:, 0] = last_eight([fine_held[...]], n_lat, subs).astype(bf16)
        carry[...] = coarse_held[...]
        if ends:
            coarse_out[:, 0] = last_eight([coarse_held[...]], n_lat, subs).astype(bf16)


def mix(fine, coarse, weight, local_pairs, subs, first, ends, backward, into, carried):
    n_lat, per = fine.shape[0], subs // 8
    count = (fine.shape[1] - 1) // per
    pair_dev = weight.shape[0] // 2
    turns = count // 2
    inside = lambda k: jnp.minimum(k, turns - 1)
    rows = lambda height, place: pl.BlockSpec(
        (n_lat, height, 8, WHOLE), lambda k, pairs: (0, place(k), 0, 0)
    )
    tail = lambda array: rows(1, lambda k: array.shape[1] - 1)
    whole = pl.BlockSpec((n_lat * subs, TILE), lambda k, pairs: (0, 0))
    body, extra, alias = filled(
        functools.partial(mix_body, pair_dev, subs, first, ends, backward), into, 7, 1
    )
    coarse_place = (lambda k: k + first) if ends else (lambda k: inside(k) + first)
    wave = lambda array: jax.ShapeDtypeStruct(array.shape, bf16)
    return call(
        body,
        "mix_back" if backward else "mix",
        2 * count * n_lat * subs * 8 * PADDED * PADDED,
        2 * weight.size * count // pair_dev + 12 * fine.size,
        grid_spec=pltpu.PrefetchScalarGridSpec(
            num_scalar_prefetch=1,
            grid=(turns + 1,),
            in_specs=[
                rows(2 * per, inside),
                tail(fine),
                rows(per, lambda k: inside(k) + first),
                tail(coarse),
                pl.BlockSpec(
                    (4,) + weight.shape[1:], lambda k, pairs: (inside(k) + first, 0, 0, 0)
                ),
                whole,
            ]
            + extra,
            out_specs=[
                rows(2 * per, lambda k: k),
                rows(per, coarse_place),
                pl.BlockSpec((4, n_lat, subs, LANES), lambda k, pairs: (inside(k), 0, 0, 0)),
                whole,
            ],
            scratch_shapes=[pltpu.VMEM((n_lat * subs, TILE), f32)] * 2,
        ),
        out_shape=[
            wave(fine),
            wave(coarse),
            jax.ShapeDtypeStruct((2 * count, n_lat, subs, LANES), bf16),
            jax.ShapeDtypeStruct((n_lat * subs, TILE), f32),
        ],
        input_output_aliases=alias,
    )(local_pairs, fine, fine, coarse, coarse, weight, carried, *([] if into is None else [into]))


def mix_grad_body(n_parts, *refs):
    values, grads, out = refs[:n_parts], refs[n_parts : 2 * n_parts], refs[2 * n_parts]
    gather = lambda parts: jnp.concatenate([flat(part[0]) for part in parts], axis=0)
    value_real, value_imag = [v.astype(bf16) for v in split_parts(gather(values), WIDE)]
    grad_real, grad_imag = [v.astype(bf16) for v in split_parts(gather(grads), C)]
    out[0, :, 0, :] = dot(grad_real, value_real, 0, 0) + dot(grad_imag, value_imag, 0, 0)
    out[0, :, 1, :] = dot(grad_imag, value_real, 0, 0) - dot(grad_real, value_imag, 0, 0)


def mix_gradient(values, grads):
    slots = values[0].shape[0]
    shape = values[0].shape[1:]
    spec = pl.BlockSpec((1,) + shape, lambda k: (k, 0, 0, 0))
    rows = len(values) * math.prod(shape[:2])
    return call(
        functools.partial(mix_grad_body, len(values)),
        "mix_gradient",
        8 * slots * rows * C * WIDE,
        slots * (4 * rows * LANES + 8 * C * WIDE),
        grid=(slots,),
        in_specs=[spec] * (2 * len(values)),
        out_specs=pl.BlockSpec((1, C, 2, WIDE), lambda k: (k, 0, 0, 0)),
        out_shape=jax.ShapeDtypeStruct((slots, C, 2, WIDE), f32),
    )(*values, *grads)


def pixel_body(
    synth, tail, state, cotangent, table, gain, bias, up, up_turned, up_bias, down, down_turned,
    down_bias, out, middle_grad, synth_grad, dense, wide_sums, narrow_sums, held,
    wide_held, narrow_held, tails,
):
    step, last = pl.program_id(0), pl.num_programs(0) - 1
    n_lat, per = synth.shape[:2]
    subs = 8 * per

    @pl.when(step == 0)
    def _():
        held[...] = jnp.zeros_like(held)
        dense[...] = jnp.zeros_like(dense)
        wide_held[...] = jnp.zeros_like(wide_held)
        narrow_held[...] = jnp.zeros_like(narrow_held)
        tails[...] = jnp.zeros_like(tails)

    @pl.when(step < last)
    def _():
        own = unpacked(packed_group(tail[:, 0].astype(f32), 0, subs), step, C - MAIN)
        real, imag = split_parts(jnp.concatenate([flat(synth[...]), own], axis=1), C)
        stacked = jnp.concatenate([real, imag], axis=0).astype(bf16)
        middle = state[0][:, 0, :] + dot(stacked, table[...], 0, 0)
        xhat, scale = norm_stats(middle)
        normed_low = (xhat * gain[...] + bias[...]).astype(bf16)
        pre_act = dot(up_turned[...], normed_low, 1, 0) + up_bias[...]
        share = 0.5 * (1.0 + lax.erf(pre_act * math.sqrt(0.5)))
        density = jnp.exp(-0.5 * pre_act * pre_act) * (1.0 / math.sqrt(2.0 * math.pi))
        hidden_low = (pre_act * share).astype(bf16)
        slope = share + pre_act * density
        out[0] = (middle + dot(down_turned[...], hidden_low, 1, 0) + down_bias[...])[:, None, :]
        grad = cotangent[0][:, 0, :]
        grad_low = grad.astype(bf16)
        pre_grad = dot(down[...], grad_low, 1, 0) * slope
        pre_low = pre_grad.astype(bf16)
        wide_held[...] += pre_grad
        dense[1, :C] += dot(grad_low, hidden_low, 1, 1)
        dense[0, :C] += dot(normed_low, pre_low, 1, 1)
        normed_grad = dot(up[...], pre_low, 1, 0)
        narrow_held[0] += normed_grad * xhat
        narrow_held[1] += normed_grad
        narrow_held[2] += grad
        scaled = normed_grad * gain[...]
        total = grad + scale * (
            scaled
            - jnp.mean(scaled, axis=0, keepdims=True)
            - xhat * jnp.mean(scaled * xhat, axis=0, keepdims=True)
        )
        middle_grad[0] = total
        held[:C] = total
        result = dot(table[...], held[...].astype(bf16), 1, 1)
        rows = result.shape[0] // 2
        joined = join_parts(result[:rows], result[rows:], C)
        synth_grad[...] = joined[:, :WHOLE].reshape(synth_grad.shape).astype(bf16)
        tails[...] += pltpu.roll(joined[:, WHOLE:], step, 1)

    @pl.when(step == last)
    def _():
        synth_grad[:, 0] = last_eight([tails[...]], n_lat, subs).astype(bf16)
        wide_sums[...] = jnp.sum(wide_held[...], axis=1, keepdims=True)
        narrow_sums[...] = jnp.sum(narrow_held[...], axis=2, keepdims=True)


def pixels(synth, state, cotangent, table, params, first, into, dense_rows):
    n_lat, subs = synth.shape[0], table.shape[0] // (2 * synth.shape[0])
    per = subs // 8
    count = (synth.shape[1] - 1) // per
    row = lambda r: jnp.minimum(r, count - 1)
    points = state.shape[3]
    hidden = params[2].shape[1]
    row_spec = pl.BlockSpec((1, C, 1, points), lambda r: (row(r) + first, 0, 0, 0))
    const = lambda array: pl.BlockSpec(array.shape, lambda r: (0,) * array.ndim)
    wave = lambda place: pl.BlockSpec((n_lat, per, 8, WHOLE), lambda r: (0, place(r), 0, 0))
    tail = pl.BlockSpec((n_lat, 1, 8, WHOLE), lambda r: (0, count * per, 0, 0))
    whole = lambda shape: pl.BlockSpec(shape, lambda r: (0,) * len(shape))
    shaped = lambda shape, kind=f32: jax.ShapeDtypeStruct(shape, kind)
    body, extra, alias = filled(pixel_body, into, 5 + len(params), 0, 1)
    return call(
        body,
        "feed_forward",
        2 * count * points * (6 * C * hidden + 2 * table.shape[0] * PADDED),
        count * (4 * C * points * 4 + 4 * n_lat * subs * LANES),
        grid=(count + 1,),
        in_specs=[wave(row), tail, row_spec, row_spec, const(table)] + [const(p) for p in params] + extra,
        input_output_aliases=alias,
        out_specs=[
            row_spec,
            pl.BlockSpec((1, C, points), lambda r: (row(r) + first, 0, 0)),
            wave(lambda r: r),
            whole((2, dense_rows, hidden)),
            whole((hidden, 1)),
            whole((3, C, 1)),
        ],
        out_shape=[
            shaped(state.shape),
            shaped((state.shape[0], C, points)),
            shaped(synth.shape, bf16),
            shaped((2, dense_rows, hidden)),
            shaped((hidden, 1)),
            shaped((3, C, 1)),
        ],
        scratch_shapes=[
            pltpu.VMEM((PADDED, points), f32),
            pltpu.VMEM((hidden, points), f32),
            pltpu.VMEM((3, C, points), f32),
            pltpu.VMEM((n_lat * subs, TILE), f32),
        ],
    )(synth, synth, state, cotangent, table, *params, *([] if into is None else into))


def final_body(wave, tail, state, middle_grad, table, gain, out, sums, held):
    step = pl.program_id(0)

    @pl.when(step == 0)
    def _():
        held[...] = jnp.zeros_like(held)

    own = unpacked(packed_group(tail[:, 0].astype(f32), 0, 8 * wave.shape[1]), step, C - MAIN)
    real, imag = split_parts(jnp.concatenate([flat(wave[...]), own], axis=1), C)
    stacked = jnp.concatenate([real, imag], axis=0).astype(bf16)
    spread_grad = dot(stacked, table[...], 0, 0)
    xhat, scale = norm_stats(state[0][:, 0, :])
    held[0] += spread_grad * xhat
    held[1] += spread_grad
    scaled = spread_grad * gain[...]
    out[0] = (
        middle_grad[0]
        + scale
        * (
            scaled
            - jnp.mean(scaled, axis=0, keepdims=True)
            - xhat * jnp.mean(scaled * xhat, axis=0, keepdims=True)
        )
    )[:, None, :]

    @pl.when(step == pl.num_programs(0) - 1)
    def _():
        sums[...] = jnp.sum(held[...], axis=2, keepdims=True)


def finish(wave, state, middle_grad, table, gain, first, into):
    n_lat, subs = wave.shape[0], table.shape[0] // (2 * wave.shape[0])
    per = subs // 8
    count = (wave.shape[1] - 1) // per
    points = state.shape[3]
    body, extra, alias = filled(final_body, into, 6, 0)
    return call(
        body,
        "first_norm_back",
        2 * count * points * table.shape[0] * PADDED,
        count * (3 * C * points * 4 + 2 * n_lat * subs * LANES),
        grid=(count,),
        in_specs=[
            pl.BlockSpec((n_lat, per, 8, WHOLE), lambda r: (0, r, 0, 0)),
            pl.BlockSpec((n_lat, 1, 8, WHOLE), lambda r: (0, count * per, 0, 0)),
            pl.BlockSpec((1, C, 1, points), lambda r: (r + first, 0, 0, 0)),
            pl.BlockSpec((1, C, points), lambda r: (r + first, 0, 0)),
            pl.BlockSpec(table.shape, lambda r: (0, 0)),
            pl.BlockSpec((C, 1), lambda r: (0, 0)),
        ]
        + extra,
        input_output_aliases=alias,
        out_specs=[
            pl.BlockSpec((1, C, 1, points), lambda r: (r + first, 0, 0, 0)),
            pl.BlockSpec((2, C, 1), lambda r: (0, 0, 0)),
        ],
        out_shape=[
            jax.ShapeDtypeStruct(state.shape, f32),
            jax.ShapeDtypeStruct((2, C, 1), f32),
        ],
        scratch_shapes=[pltpu.VMEM((2, C, points), f32)],
    )(wave, wave, state, middle_grad, table, gain, *([] if into is None else [into]))


def part_rows_body(paired, out):
    turned = paired[0][:, 0, :].T
    count = turned.shape[0] // 2
    for half in range(2):
        out[half] = turned[half * count : (half + 1) * count][:, None, :]


def part_rows(paired):
    pairs, points = paired.shape[0], paired.shape[3] // 2
    return call(
        part_rows_body,
        "part_rows",
        0,
        8 * paired.size,
        grid=(pairs,),
        in_specs=[pl.BlockSpec((1, C, 1, 2 * points), lambda r: (r, 0, 0, 0))],
        out_specs=pl.BlockSpec((2, points, 1, C), lambda r: (r, 0, 0, 0)),
        out_shape=jax.ShapeDtypeStruct((2 * pairs, points, 1, C), f32),
    )(paired)


def fourier_tables(orders, live, points, lon_count):
    phase = (orders * points % lon_count).astype(f32) * (2.0 * math.pi / lon_count)
    kept = live.astype(f32)
    cosine, sine = jnp.cos(phase) * kept, -jnp.sin(phase) * kept
    doubling = jnp.where(orders == 0, 1.0, 2.0).astype(f32)
    forward = jnp.concatenate([cosine / lon_count, sine / lon_count], axis=0)
    inverse = jnp.concatenate([cosine * doubling, sine * doubling], axis=0)
    return forward.astype(bf16), inverse.astype(bf16)


def order_rows(n_lat, pair_dev, subs):
    index = jnp.arange(n_lat * subs, dtype=jnp.int32)[:, None]
    return index // subs, index % subs


def fine_fourier(n_lat, pair_dev, subs, lon_count):
    device, sub = order_rows(n_lat, pair_dev, subs)
    kind = device * pair_dev + sub // 2
    member = sub % 2
    live = (sub < 2 * pair_dev) & jnp.where(
        member == 0, kind <= LB // 2, (kind >= 1) & (kind <= LB // 2 - 1)
    )
    orders = jnp.where(live, jnp.where(member == 0, kind, LB - kind), 0)
    points = jnp.arange(lon_count, dtype=jnp.int32)[None, :]
    return fourier_tables(orders, live, points, lon_count)


def coarse_fourier(n_lat, pair_dev, subs, lon_count):
    device, sub = order_rows(n_lat, pair_dev, subs)
    order = device * pair_dev + sub % pair_dev
    points = jnp.arange(2 * lon_count, dtype=jnp.int32)[None, :]
    live = (sub < 2 * pair_dev) & (order < LA) & (sub // pair_dev == points // lon_count)
    orders = jnp.where((sub < 2 * pair_dev) & (order < LA), order, 0)
    return fourier_tables(orders, live, points % lon_count, lon_count)


class Line:
    def __init__(self):
        self.before = self.last = None
        self.work, self.later = [], []
        self.aside = None

    def swap(self, values):
        self.step_aside()
        waits = self.work + ([] if self.last is None else [self.last])
        if waits:
            values = lax.optimization_barrier((values, waits))[0]
        self.before = self.last
        self.last = lax.all_to_all(values, "lat", split_axis=0, concat_axis=0, tiled=True)
        self.work, self.later = self.later, []
        return self.last

    def step_aside(self):
        if self.aside is not None:
            next(self.aside, None)

    def hold(self, values):
        if self.before is None:
            return values
        return lax.optimization_barrier((values, self.before))[0]

    def after_work(self, values):
        return lax.optimization_barrier((values, self.work))[0] if self.work else values

    def keep(self, values):
        self.work.append(values)
        return values

    def keep_later(self, values):
        self.later.append(values)
        return values


def partners(count, step):
    if count & (count - 1) == 0:
        return [(k, k ^ step) for k in range(count)], lambda rank: jnp.bitwise_xor(rank, step)
    return [(k, (k + step) % count) for k in range(count)], lambda rank: (rank + step) % count


def share_slots(members, n_chan, step):
    share = members.shape[0] // n_chan
    route, find = partners(n_chan, step)
    block = lax.dynamic_slice_in_dim(members, find(lax.axis_index("chan")) * share, share)
    return lax.ppermute(block, "chan", route) if step else block


def sum_over(values, sizes):
    for axis, size in sizes:
        if size & (size - 1):
            values = lax.psum(values, axis)
            continue
        step = 1
        while step < size:
            values = values + lax.ppermute(values, axis, partners(size, step)[0])
            step *= 2
    return values


def add_dense(array, n_lat, n_chan, line, result):
    shape, columns = array.shape, array.shape[2]
    sizes = {"chan": n_chan, "lat": n_lat}
    pairs = [("chan", 2**k) for k in range(n_chan.bit_length() - 1)] + [("lat", 1)]
    others = n_lat // 2
    held = array.reshape(-1, columns)
    odd = lambda axis, step: (lax.axis_index(axis) // step) % 2 == 1
    group = lax.axis_index("lat") // 2

    def halve(held, axis, step):
        low, high = jnp.split(line.hold(held), 2, axis=0)
        upper = odd(axis, step)
        other = lax.ppermute(jnp.where(upper, low, high), axis, partners(sizes[axis], step)[0])
        return line.keep(jnp.where(upper, high, low) + other)

    def double(held, axis, step):
        upper = odd(axis, step)
        other = lax.ppermute(line.hold(held), axis, partners(sizes[axis], step)[0])
        return line.keep_later(
            jnp.concatenate([jnp.where(upper, other, held), jnp.where(upper, held, other)], axis=0)
        )

    for axis, step in pairs[:-1]:
        held = halve(held, axis, step)
    yield
    yield
    held = halve(held, *pairs[-1])
    yield
    pieces = line.hold(held).reshape(others, -1, columns)
    own = lax.dynamic_index_in_dim(pieces, group, 0, False)
    for step in range(1, others):
        block = lax.dynamic_index_in_dim(pieces, jnp.bitwise_xor(group, step), 0, False)
        block = lax.ppermute(block.astype(bf16), "lat", partners(n_lat, 2 * step)[0])
        own = own + block.astype(f32)
    own = line.keep_later(own).astype(bf16)
    yield
    yield
    yield
    own = line.hold(own)
    held = jnp.zeros((others,) + own.shape, bf16)
    for step in range(others):
        block = lax.ppermute(own, "lat", partners(n_lat, 2 * step)[0]) if step else own
        held = lax.dynamic_update_index_in_dim(held, block, jnp.bitwise_xor(group, step), 0)
    held = line.keep_later(held).reshape(-1, columns)
    yield
    yield
    yield
    for axis, step in reversed(pairs[1:]):
        held = double(held, axis, step)
    yield
    held = double(held, *pairs[0])
    result.append(held.astype(f32).reshape(shape))


def shards(
    n_lat, n_chan, coarse_state, fine_state, coarse_noise, fine_noise, coarse_rows, fine_rows,
    pair_slots, first_gain, first_bias, mix_weight, second_gain, second_bias, up_weight, up_bias,
    down_weight, down_bias, coarse_cotangent, fine_cotangent,
):
    pair_dev = mix_weight.shape[0] // 2
    subs = -(-2 * pair_dev // 8) * 8
    lat_rank = lax.axis_index("lat")
    fine_dev, fine_points = fine_state.shape[1], fine_state.shape[2]
    coarse_dev, coarse_points = coarse_state.shape[1], coarse_state.shape[2]
    coarse_two = coarse_dev // 2
    column = lambda vector: vector[:, None]

    def fine_in(values):
        return values.transpose(1, 3, 0, 2)

    def coarse_in(values):
        paired = values[0].reshape(coarse_two, 2 * coarse_points, values.shape[3])
        return paired.transpose(0, 2, 1)[:, :, None, :]

    def fine_back(values):
        return values.transpose(2, 0, 3, 1)

    def coarse_back(values):
        return part_rows(values).transpose(2, 0, 1, 3)

    line = Line()
    dense_unit = 4 * n_lat * n_chan
    dense_rows = -(-(C + 3) // dense_unit) * dense_unit
    row_cuts = [(fine_dev + 1) // 2, fine_dev // 2] if fine_dev >= 8 else [fine_dev]
    row_starts = [sum(row_cuts[:k]) for k in range(len(row_cuts))]
    outer_cuts = [fine_dev // 4 + 1, fine_dev - fine_dev // 4 - 1] if fine_dev >= 8 else [fine_dev]
    outer_starts = [sum(outer_cuts[:k]) for k in range(len(outer_cuts))]
    n_chunks = 2 if pair_dev % 4 == 0 else 1
    chunk_pairs = pair_dev // n_chunks
    chunk_range = range(n_chunks)

    fine_x = fine_in(fine_state)
    fine_noise_in = fine_noise[0].transpose(0, 2, 1)
    fine_forward, fine_inverse = fine_fourier(n_lat, pair_dev, subs, fine_points)
    gain_one, bias_one = column(first_gain), column(first_bias)
    fine_four = []
    for start, count in zip(outer_starts, outer_cuts):
        made = spread(fine_x, fine_noise_in, gain_one, bias_one, fine_forward, n_lat, start, count)
        fine_four.append(line.swap(line.keep(made)))
    coarse_x = coarse_in(coarse_state)
    coarse_forward, coarse_inverse = coarse_fourier(n_lat, pair_dev, subs, coarse_points)
    coarse_noise_in = coarse_in(coarse_noise)[:, :, 0, :]
    coarse_four = line.swap(
        spread(coarse_x, coarse_noise_in, gain_one, bias_one, coarse_forward, n_lat, 0, coarse_two)
    )

    wide = -(-pair_dev // 8) * 8
    classes = lat_rank * pair_dev + jnp.arange(wide, dtype=jnp.int32)
    classes = jnp.where(jnp.arange(wide) < pair_dev, classes, LB).astype(jnp.int32)
    coarse_order = coarse_rows.reshape(-1, 2).T.reshape(-1)
    by_device = fine_rows.reshape(n_lat, fine_dev)
    in_order = lambda starts, cuts: jnp.concatenate(
        [by_device[:, a : a + c].reshape(-1) for a, c in zip(starts, cuts)]
    )
    unused, fine_quad = legendre_tables(
        in_order(outer_starts, outer_cuts), pair_slots, classes, LB, True
    )
    fine_plain, unused = legendre_tables(
        in_order(row_starts, row_cuts), pair_slots, classes, LB, True
    )
    coarse_plain, coarse_quad = legendre_tables(coarse_order, pair_slots, classes, LA, False)
    turn = lambda table, chunks=n_chunks: by_class(table, n_lat, pair_dev, chunks)

    def fine_tables(parts):
        first, near, far = [turn(part) for part in parts]
        table_a = jnp.concatenate([first, near], axis=1)
        return [table_a, far], [table_a.transpose(0, 2, 1), far.transpose(0, 2, 1)]

    fine_quad_in, fine_quad_out = fine_tables(fine_quad)
    fine_plain_in, fine_plain_out = fine_tables(fine_plain)
    coarse_quad_in = turn(coarse_quad[0], 1)
    coarse_plain_in = turn(coarse_plain[0], 1)
    coarse_quad_out = coarse_quad_in.transpose(0, 2, 1)
    coarse_plain_out = coarse_plain_in.transpose(0, 2, 1)
    local_pairs = lax.dynamic_slice_in_dim(pair_slots, lat_rank * pair_dev, pair_dev)
    weight = mix_weight.transpose(0, 1, 3, 2)

    fine_work = functools.partial(to_degrees_fine, pair_dev)
    fine_back_work = functools.partial(to_orders_fine, pair_dev)
    coarse_work = functools.partial(coarse_either_way, pair_dev)

    def spectral(coarse_chunk, fine_chunks, in_tables, out_tables, cuts, backward, aside):
        wide = (C if backward else WIDE) - MAIN
        fine_made = lane_call(
            fine_work, "rows_to_degrees", line.hold(fine_chunks), in_tables[1],
            [chunk_pairs] * n_chunks, subs, wide,
        )
        line.keep(fine_made)
        arrived, mixed, shared = [], [], []

        def mix_chunk(k):
            fine, coarse = line.hold((arrived[k], arrived_coarse))
            carried = mixed[-1][3] if mixed else jnp.zeros((n_lat * subs, TILE), f32)
            made = mix(
                fine, coarse, weight, local_pairs, subs, k * chunk_pairs // 2, k == n_chunks - 1,
                backward, mixed[-1][1] if mixed else None, carried,
            )
            mixed.append(line.keep(made))

        def share_next(count=1):
            members = joined_rows([made[2] for made in mixed])
            for step in range(len(shared), min(len(shared) + count, n_chan)):
                shared.append(line.keep_later(share_slots(line.hold(members), n_chan, step)))

        arrived.append(line.swap(fine_made[0]))
        coarse_made = lane_call(
            coarse_work, "rows_to_degrees", [line.hold(coarse_chunk)], [in_tables[0]],
            [pair_dev // 2], subs, wide,
        )[0]
        arrived_coarse = line.swap(line.keep(coarse_made))
        for k in range(1, n_chunks):
            arrived.append(line.swap(fine_made[k]))
            mix_chunk(k - 1)
        if n_chunks == 1:
            mix_chunk(0)
        fine_back = []
        for k in range(n_chunks - 1):
            fine_back.append(line.swap(mixed[k][0]))
            mix_chunk(k + 1)
        arrived_coarse = line.swap(mixed[-1][1])
        share_next(2)
        fine_back.append(line.swap(mixed[-1][0]))
        share_next()
        coarse_made = lane_call(
            coarse_work, "degrees_to_rows", [line.hold(arrived_coarse)], [out_tables[0]],
            [coarse_two], subs, C - MAIN,
        )[0]
        coarse_end = line.swap(line.keep(coarse_made))
        share_next(n_chan)
        fine_made = lane_call(
            fine_back_work, "degrees_to_rows", line.hold(fine_back), out_tables[1],
            cuts, subs, C - MAIN,
        )
        line.keep(fine_made)
        fine_end = [None] * len(cuts)
        order = list(range(len(cuts)))
        if backward:
            order.reverse()
        for k, place in enumerate(order):
            fine_end[place] = line.swap(fine_made[place])
            aside(k, coarse_end, fine_end, shared)
        return fine_end, shared

    params = [
        column(second_gain), column(second_bias), up_weight, up_weight.T, column(up_bias),
        down_weight, down_weight.T, column(down_bias),
    ]
    coarse_g, fine_g = coarse_in(coarse_cotangent), fine_in(fine_cotangent)
    coarse_made, fine_made = [], []

    def fine_pixels(k, synth):
        into = fine_made[-1][:2] if fine_made else None
        made = pixels(
            line.hold(synth), fine_x, fine_g, fine_inverse, params, row_starts[k], into,
            dense_rows,
        )
        fine_made.append(line.keep(made))

    def forward_aside(k, coarse_end, fine_end, shared):
        if k == 0:
            made = pixels(
                line.hold(coarse_end), coarse_x, coarse_g, coarse_inverse, params, 0, None,
                dense_rows,
            )
            coarse_made.extend(line.keep(made))
        else:
            if k == 1:
                coarse_made[0] = line.keep(coarse_back(line.hold(coarse_made[0])))
            fine_pixels(k - 1, fine_end[k - 1])

    fine_synth, values = spectral(
        coarse_four, fine_four, (coarse_quad_in, fine_quad_in), (coarse_plain_out, fine_plain_out),
        row_cuts, False, forward_aside,
    )
    if len(row_cuts) == 1:
        fine_pixels(0, fine_synth[0])
    fine_sgrad = []
    for k in range(len(row_cuts)):
        fine_sgrad.append(line.swap(fine_made[k][2]))
        if k + 1 < len(row_cuts):
            fine_pixels(k + 1, fine_synth[k + 1])
    axes = (("chan", n_chan), ("lat", n_lat))
    hidden = up_bias.shape[0]
    total = coarse_made[3:]
    for made in fine_made:
        total = [x + y for x, y in zip(total, made[3:])]
    narrow = jnp.concatenate([total[1][:, 0], total[2].reshape(-1)])
    narrow = jnp.pad(narrow, (0, 3 * hidden - narrow.shape[0])).reshape(1, 3, hidden)
    stacked = lax.dynamic_update_slice(total[0], narrow, (0, C, 0))
    dense = []
    line.aside = add_dense(line.hold(stacked), n_lat, n_chan, line, dense)
    line.step_aside()
    coarse_sgrad = line.swap(coarse_made[2])
    if len(row_cuts) == 1:
        coarse_made[0] = coarse_back(coarse_made[0])
    ends, mix_grads = [], []

    def finish_fine(place, wave):
        into = ends[-1][0] if len(ends) > 1 else None
        return finish(
            wave, fine_x, fine_made[-1][1], fine_forward, gain_one, outer_starts[place], into
        )

    def backward_aside(k, coarse_end, fine_end, shared):
        if k == 0:
            mix_grads.append(line.keep(mix_gradient(values, line.hold(shared))))
            made = finish(
                line.hold(coarse_end), coarse_x, coarse_made[1], coarse_forward, gain_one, 0, None
            )
        else:
            if k == 1:
                ends[0][0] = line.keep(coarse_back(line.hold(ends[0][0])))
            made = finish_fine(len(outer_cuts) - k, line.hold(fine_end[-k]))
        ends.append(list(line.keep(made)))

    fine_fgrad, grads = spectral(
        coarse_sgrad, fine_sgrad, (coarse_plain_in, fine_plain_in), (coarse_quad_out, fine_quad_out),
        outer_cuts, True, backward_aside,
    )
    for unused in line.aside:
        pass
    up_grad, down_grad = dense[0][0, :C], dense[0][1, :C]
    narrow = dense[0][0, C : C + 3].reshape(-1)
    narrow_sums = narrow[hidden : hidden + 3 * C].reshape(3, C)
    if len(row_cuts) == 1:
        ends[0][0] = coarse_back(ends[0][0])
    last_wave = lax.optimization_barrier((fine_fgrad[0], line.work + line.later))[0]
    ends.append(finish_fine(0, last_wave))
    mix_grad = mix_grads[0].transpose(0, 2, 3, 1)
    sums = sum(end[1] for end in ends)
    first_sums = sum_over(sums[:, :, 0], axes)
    return (
        coarse_made[0],
        fine_back(fine_made[-1][0]),
        ends[0][0],
        fine_back(ends[-1][0]),
        first_sums[0],
        first_sums[1],
        mix_grad,
        narrow_sums[0],
        narrow_sums[1],
        up_grad,
        narrow[:hidden],
        down_grad.T,
        narrow_sums[2],
    )


def solution(mesh):
    pixel = P("chan", "lat", None, None)
    slots = P("lat", None, None, None)
    return jax.shard_map(
        functools.partial(shards, mesh.shape["lat"], mesh.shape["chan"]),
        mesh=mesh,
        in_specs=(pixel,) * 4 + (P(),) * 5 + (slots,) + (P(),) * 6 + (pixel,) * 2,
        out_specs=(pixel,) * 4 + (P(),) * 2 + (P(("lat", "chan"), None, None, None),) + (P(),) * 6,
        check_vma=False,
    )
```

```python
import functools
import math

import jax
import jax.numpy as jnp
from jax import lax
from jax.experimental import pallas as pl
from jax.experimental.pallas import tpu as pltpu
from jax.sharding import PartitionSpec as P

C = 641
NOISE = 8
WIDE = C + NOISE
LA = 90
LB = 180

TILE = 128
MAIN = C // TILE * TILE
HALF = TILE // 2
WHOLE = 2 * MAIN
LANES = WHOLE + TILE
PADDED = MAIN + TILE

epsilon = 1e-05
noise_scale = 1.0 / 262144.0
bf16 = jnp.bfloat16
f32 = jnp.float32
VMEM_LIMIT = 60 * 2**20


def call(body, name, flops, moved, **options):
    if "grid_spec" not in options:
        options.setdefault("scratch_shapes", [])
    return pl.pallas_call(
        body,
        compiler_params=pltpu.CompilerParams(vmem_limit_bytes=VMEM_LIMIT),
        cost_estimate=pl.CostEstimate(flops=int(flops), bytes_accessed=int(moved), transcendentals=0),
        name=name,
        **options,
    )


def filled(body, into, position, *outputs):
    if into is None:
        return body, [], {}
    count = len(outputs)

    def skipping(*refs):
        body(*refs[:position], *refs[position + count :])

    alias = {position + k: output for k, output in enumerate(outputs)}
    return skipping, [pl.BlockSpec(memory_space=pl.ANY)] * count, alias


def dot(left, right, left_dim, right_dim):
    return lax.dot_general(
        left, right, (((left_dim,), (right_dim,)), ((), ())), preferred_element_type=f32
    )


def join_parts(real, imag, count):
    tail = real[:, MAIN:] + pltpu.roll(imag[:, MAIN:], HALF, 1)
    return jnp.concatenate([real[:, :MAIN], imag[:, :MAIN], tail], axis=1)


def join_narrow(real, imag):
    lane = lax.broadcasted_iota(jnp.int32, (real.shape[0], TILE), 1)
    tail = jnp.where(
        lane == 0, real[:, MAIN:C], jnp.where(lane == HALF, imag[:, MAIN:C], 0.0)
    )
    return jnp.concatenate([real[:, :MAIN], imag[:, :MAIN], tail], axis=1)


def split_parts(joined, count):
    tail = joined[:, 2 * MAIN :]
    real = jnp.concatenate([joined[:, :MAIN], tail], axis=1)[:, :count]
    imag = jnp.concatenate(
        [joined[:, MAIN : 2 * MAIN], pltpu.roll(tail, HALF, 1)], axis=1
    )[:, :count]
    return real, imag


def packing(rows, width):
    share = HALF // width
    return share, -(-rows // share)


def eights(rows, subs):
    return rows * (subs // 8) + 1


def packed_group(tail, group, subs):
    count = subs // 8
    tiles = [tail[:, :, (group * count + k) * TILE :][:, :, :TILE] for k in range(count)]
    return jnp.stack(tiles, axis=1).reshape(-1, TILE)


def unpacked(group_tile, place, width):
    turned = pltpu.roll(group_tile, (TILE - place * width) % TILE, 1)
    lane = lax.broadcasted_iota(jnp.int32, turned.shape, 1)
    return jnp.where(lane % HALF < width, turned, 0.0)


def last_eight(groups, n_lat, subs):
    count = subs // 8
    tiles = []
    for group in groups:
        split = group.reshape(n_lat, count, 8, TILE)
        tiles += [split[:, k] for k in range(count)]
    blank = jnp.zeros((n_lat, 8, TILE), f32)
    return jnp.concatenate(tiles + [blank] * (WHOLE // TILE - len(tiles)), axis=2)


def flat(block):
    return block.astype(f32).reshape(-1, block.shape[-1])


def joined_rows(parts):
    return parts[0] if len(parts) == 1 else jnp.concatenate(parts, axis=0)


def norm_stats(values):
    centered = values - jnp.mean(values, axis=0, keepdims=True)
    variance = jnp.mean(centered * centered, axis=0, keepdims=True)
    scale = lax.rsqrt(variance + epsilon)
    return centered * scale, scale


def spread_body(state, noise, gain, bias, table, out, held, tails):
    step, last = pl.program_id(0), pl.num_programs(0) - 1
    n_lat, count, unused, lanes = out.shape
    width = WIDE - MAIN
    share = HALF // width

    @pl.when(step == 0)
    def _():
        held[...] = jnp.zeros_like(held)
        tails[...] = jnp.zeros_like(tails)

    @pl.when(step < last)
    def _():
        xhat, unused = norm_stats(state[0][:, 0, :])
        held[:C] = xhat * gain[...] + bias[...]
        held[C:WIDE] = ((noise[0].astype(f32) + 0.5) * noise_scale - 0.5) * math.sqrt(12.0)
        result = dot(table[...], held[...].astype(bf16), 1, 1)
        rows = result.shape[0] // 2
        joined = join_parts(result[:rows], result[rows:], WIDE)
        out[...] = joined[:, :WHOLE].reshape(out.shape).astype(bf16)
        tails[step // share] += pltpu.roll(joined[:, WHOLE:], step % share * width, 1)

    @pl.when(step == last)
    def _():
        groups = [tails[k] for k in range(tails.shape[0])]
        out[:, 0] = last_eight(groups, n_lat, 8 * count).astype(bf16)


def spread(state, noise, gain, bias, table, n_lat, first, count):
    points = state.shape[3]
    subs = table.shape[0] // (2 * n_lat)
    const = lambda r: (0, 0)
    row = lambda r: jnp.minimum(r, count - 1) + first
    return call(
        spread_body,
        "norm_and_dft",
        2 * count * table.shape[0] * points * PADDED,
        count * (C * points * 4 + n_lat * subs * LANES * 2),
        grid=(count + 1,),
        in_specs=[
            pl.BlockSpec((1, C, 1, points), lambda r: (row(r), 0, 0, 0)),
            pl.BlockSpec((1, NOISE, points), lambda r: (row(r), 0, 0)),
            pl.BlockSpec((C, 1), const),
            pl.BlockSpec((C, 1), const),
            pl.BlockSpec(table.shape, const),
        ],
        out_specs=pl.BlockSpec((n_lat, subs // 8, 8, WHOLE), lambda r: (0, r, 0, 0)),
        out_shape=jax.ShapeDtypeStruct((n_lat, eights(count, subs), 8, WHOLE), bf16),
        scratch_shapes=[
            pltpu.VMEM((PADDED, points), f32),
            pltpu.VMEM((packing(count, WIDE - MAIN)[1], n_lat * subs, TILE), f32),
        ],
    )(state, noise, gain, bias, table)


def legendre_body(total, pairs, order_a, order_b, diag_a, diag_b, cosine, classes, *refs):
    two = order_b is not None
    outs, (held_a, held_b) = refs[: 3 if two else 1], (refs[3:] if two else (refs[1], None))

    def advance(degree, order, diagonal, previous, earlier):
        real = degree.astype(f32)
        grow = jnp.sqrt(
            (4.0 * real * real - 1.0) / jnp.maximum(real * real - order * order, 1.0)
        )
        damp = jnp.sqrt(
            jnp.maximum((real - 1.0) * (real - 1.0) - order * order, 0.0)
            / jnp.maximum(4.0 * (real - 1.0) * (real - 1.0) - 1.0, 1.0)
        )
        grown = grow * (cosine[...] * previous - damp * earlier)
        return jnp.where(real == order, diagonal, jnp.where(real > order, grown, 0.0))

    def step(degree, carry):
        now_a = advance(degree, order_a[...], diag_a[...], carry[0], carry[1])
        held_a[degree] = now_a
        if not two:
            return (now_a, carry[0])
        now_b = advance(degree, order_b[...], diag_b[...], carry[2], carry[3])
        held_b[degree] = now_b
        return (now_a, carry[0], now_b, carry[2])

    zero = diag_a[...] * 0.0
    lax.fori_loop(0, total, step, (zero,) * (4 if two else 2))

    def pick(slot, unused):
        pair = pairs[slot]
        safe = jnp.maximum(pair, 0)
        live = jnp.where(pair >= 0, 1.0, 0.0)
        low = classes[...] <= pair
        near = held_a[safe] * live
        if two:
            far = held_a[LB - 1 - safe] * live
            outs[0][slot] = jnp.where(low, near, far)
            outs[1][slot] = jnp.where(low, far, 0.0)
            outs[2][slot] = jnp.where(low, 0.0, held_b[LB - 1 - safe] * live)
        else:
            outs[0][slot] = jnp.where(low, near, 0.0)
        return unused

    lax.fori_loop(0, pairs.shape[0], pick, 0)


def diagonal_values(orders, live, sines):
    order_real = orders.astype(f32)[:, None]
    log_start = 0.5 * jnp.log((2.0 * order_real + 1.0) / (4.0 * math.pi))
    log_start = log_start + 0.5 * (
        lax.lgamma(2.0 * order_real + 1.0)
        - 2.0 * order_real * math.log(2.0)
        - 2.0 * lax.lgamma(order_real + 1.0)
    )
    diagonal = jnp.exp(log_start + order_real * jnp.log(sines)[None, :])
    return jnp.where(live[:, None], diagonal, 0.0)


def legendre_tables(row_table, pair_slots, classes, total, two):
    slots, rows, wide = pair_slots.shape[0], row_table.shape[0], classes.shape[0]
    occupied = (row_table >= 0).astype(f32)
    colatitude = math.pi * (jnp.maximum(row_table, 0).astype(f32) + 0.5) / total
    sines = jnp.sin(colatitude)
    cosine = jnp.broadcast_to(jnp.cos(colatitude)[None, :], (wide, rows))
    spread_out = lambda v: jnp.broadcast_to(v.astype(f32)[:, None], (wide, rows))
    top = LB // 2 if two else LA - 1
    order_a = jnp.where(classes <= top, classes, 0)
    diag_a = diagonal_values(order_a, classes <= top, sines)
    live_b = (classes >= 1) & (classes <= LB // 2 - 1)
    order_b = jnp.where(live_b, LB - classes, 0)
    diag_b = diagonal_values(order_b, live_b, sines)
    class_wide = jnp.broadcast_to(classes[:, None], (wide, rows))
    if two:
        arrays = [spread_out(order_a), spread_out(order_b), diag_a, diag_b, cosine, class_wide]
        body = functools.partial(legendre_body, total)
    else:
        arrays = [spread_out(order_a), diag_a, cosine, class_wide]

        def body(pairs, order, diagonal, cosines, class_ref, *refs):
            legendre_body(total, pairs, order, None, diagonal, None, cosines, class_ref, *refs)

    shape = jax.ShapeDtypeStruct((slots, wide, rows), f32)
    count = 3 if two else 1
    tables = call(
        body,
        "legendre_tables",
        total * wide * rows * 40,
        count * slots * wide * rows * 4,
        in_specs=[pl.BlockSpec(memory_space=pltpu.SMEM)]
        + [pl.BlockSpec(memory_space=pltpu.VMEM)] * len(arrays),
        out_specs=[pl.BlockSpec(memory_space=pltpu.VMEM)] * count,
        out_shape=[shape] * count,
        scratch_shapes=[pltpu.VMEM((total, wide, rows), f32)] * (2 if two else 1),
    )(pair_slots, *arrays)
    plain = [table * occupied for table in tables]
    weight = sines * occupied * (2.0 * math.pi * math.pi / total)
    return plain, [table * weight for table in plain]


def by_class(table, n_lat, pair_dev, n_chunks):
    split = table.reshape(n_lat, n_chunks, pair_dev // (2 * n_chunks), 2, *table.shape[1:])
    moved = split.transpose(4, 3, 1, 0, 2, 5)[:pair_dev]
    return moved.reshape(pair_dev, n_lat * pair_dev, table.shape[2]).astype(bf16)


def to_degrees_fine(pair_dev, subs, tables, held, results):
    table_a, table_b = tables
    half = sum(result.shape[0] for result in results) // (2 * subs)

    def order_rows(sub):
        parts = [keep[pl.ds(sub, keep.shape[0] // subs, stride=subs), :] for keep in held]
        return joined_rows(parts).astype(bf16)

    for index in range(pair_dev):
        from_a = dot(table_a[index], order_rows(2 * index), 1, 0)
        from_b = dot(table_b[index], order_rows(2 * index + 1), 1, 0)
        first, second = from_a[: 2 * half], from_a[2 * half :] + from_b
        begin = 0
        for odd in range(2):
            start = odd * subs + index
            for result in results:
                count = result.shape[0] // (2 * subs)
                rows = slice(begin, begin + count)
                begin += count
                result[pl.ds(start + (1 - odd) * pair_dev, count, stride=2 * subs), :] = first[rows]
                result[pl.ds(start + odd * pair_dev, count, stride=2 * subs), :] = second[rows]


def to_orders_fine(pair_dev, subs, tables, held, results):
    table_a, table_b = tables
    for index in range(pair_dev):
        first, second = [], []
        for odd in range(2):
            start = odd * subs + index
            for keep in held:
                count = keep.shape[0] // (2 * subs)
                first.append(keep[pl.ds(start + (1 - odd) * pair_dev, count, stride=2 * subs), :])
                second.append(keep[pl.ds(start + odd * pair_dev, count, stride=2 * subs), :])
        second = joined_rows(second)
        both = joined_rows(first + [second]).astype(bf16)
        made = (dot(table_a[index], both, 1, 0), dot(table_b[index], second.astype(bf16), 1, 0))
        for member in range(2):
            begin = 0
            for result in results:
                rows = result.shape[0] // subs
                result[pl.ds(2 * index + member, rows, stride=subs), :] = made[member][
                    begin : begin + rows
                ]
                begin += rows


def coarse_either_way(pair_dev, subs, tables, held, results):
    (keep,), (result,), (table,) = held, results, tables
    before, after = keep.shape[0] // subs, result.shape[0] // subs
    for index in range(pair_dev):
        taken = joined_rows(
            [keep[pl.ds(odd * pair_dev + index, before, stride=subs), :] for odd in range(2)]
        ).astype(bf16)
        made = dot(table[index], taken, 1, 0)
        for odd in range(2):
            result[pl.ds(odd * pair_dev + index, after, stride=subs), :] = made[
                odd * after : (odd + 1) * after
            ]


def lane_body(work, subs, width, n_in, n_tables, n_out, *refs):
    cuts = [n_in, n_in, n_tables, n_out, n_in, n_out, n_out]
    mains, tails, tables, outs, held, results, packed = [
        refs[sum(cuts[:k]) : sum(cuts[: k + 1])] for k in range(len(cuts))
    ]
    step = pl.program_id(0)
    n_lat, per = mains[0].shape[0], subs // 8

    @pl.when(step == 0)
    def _():
        for tail, keep in zip(tails, held):
            rows = keep.shape[0] // (n_lat * subs)
            share, groups = packing(rows, width)
            whole = tail[:, 0].astype(f32)
            for group in range(groups):
                tile = packed_group(whole, group, subs)
                for row in range(group * share, min(rows, (group + 1) * share)):
                    own = unpacked(tile, row % share, width)
                    for device in range(n_lat):
                        keep[pl.ds((device * rows + row) * subs, subs), :] = own[
                            device * subs : (device + 1) * subs
                        ]
        for result in results:
            result[...] = jnp.zeros_like(result)

    @pl.when(step > 0)
    def _():
        for main, keep in zip(mains, held):
            keep[...] = flat(main[:, : main.shape[1] - 1])

    work(subs, tables, held, results)

    @pl.when(step == 0)
    def _():
        for result, pack in zip(results, packed):
            rows = result.shape[0] // (n_lat * subs)
            share, groups = packing(rows, width)
            pack[...] = jnp.zeros_like(pack)
            made = result[...].reshape(n_lat, rows, subs, TILE)
            for group in range(groups):
                total = jnp.zeros((n_lat * subs, TILE), f32)
                for row in range(group * share, min(rows, (group + 1) * share)):
                    own = made[:, row].reshape(n_lat * subs, TILE)
                    total = total + pltpu.roll(own, row % share * width, 1)
                split = total.reshape(n_lat, per, 8, TILE)
                for k in range(per):
                    pack[group * per + k] = split[:, k]

    @pl.when(step > 0)
    def _():
        for out, result, pack in zip(outs, results, packed):
            count = out.shape[1] - 1
            out[:, :count] = result[...].reshape(n_lat, count, 8, TILE).astype(bf16)
            out[:, count] = pack[step - 1].astype(bf16)


def lane_call(work, name, inputs, tables, rows_out, subs, width):
    n_lat = inputs[0].shape[0]
    outs = [(n_lat, eights(rows, subs), 8, WHOLE) for rows in rows_out]
    rows_in = [(a.shape[1] - 1) * 8 // subs for a in inputs]
    tiled = lambda shape: pl.BlockSpec(
        tuple(shape[:3]) + (TILE,), lambda t: (0, 0, 0, jnp.maximum(t - 1, 0))
    )
    tail = lambda shape: pl.BlockSpec(
        (shape[0], 1, 8, WHOLE), lambda t, last=shape[1] - 1: (0, last, 0, 0)
    )
    whole = lambda shape: pl.BlockSpec(shape, lambda t: (0, 0, 0))
    held = lambda rows: pltpu.VMEM((n_lat * rows * subs, TILE), f32)
    moved = sum(2 * math.prod(s) for s in [a.shape for a in inputs] + outs)
    flops = sum(2 * math.prod(t.shape) for t in tables) * LANES
    return call(
        functools.partial(lane_body, work, subs, width, len(inputs), len(tables), len(outs)),
        name,
        flops,
        moved,
        grid=(WHOLE // TILE + 1,),
        in_specs=[tiled(a.shape) for a in inputs]
        + [tail(a.shape) for a in inputs]
        + [whole(t.shape) for t in tables],
        out_specs=[tiled(shape) for shape in outs],
        out_shape=[jax.ShapeDtypeStruct(shape, bf16) for shape in outs],
        scratch_shapes=[held(rows) for rows in rows_in]
        + [held(rows) for rows in rows_out]
        + [pltpu.VMEM((WHOLE // TILE, n_lat, 8, TILE), f32) for unused in outs],
    )(*inputs, *inputs, *tables)


def mix_body(
    pair_dev, subs, first, ends, backward, pairs, fine, fine_tail, coarse, coarse_tail, weight,
    carried, fine_out, coarse_out, members, carry, fine_held, coarse_held,
):
    step, last = pl.program_id(0), pl.num_programs(0) - 1
    n_lat, per = fine.shape[0], subs // 8
    rows = n_lat * subs
    width = (C if backward else WIDE) - MAIN
    count = C if backward else WIDE

    @pl.when(step == 0)
    def _():
        fine_held[...] = jnp.zeros_like(fine_held)
        coarse_held[...] = carried[...]

    def apply(values, slot):
        real, imag = split_parts(values, count)
        stacked = jnp.concatenate([real, imag], axis=0).astype(bf16)
        by_real = dot(stacked, weight[slot, 0], 1, 0 if backward else 1)
        by_imag = dot(stacked, weight[slot, 1], 1, 0 if backward else 1)
        if backward:
            out_real = by_real[:rows] + by_imag[rows:]
            out_imag = by_real[rows:] - by_imag[:rows]
        else:
            out_real = by_real[:rows] - by_imag[rows:]
            out_imag = by_imag[:rows] + by_real[rows:]
        return join_narrow(out_real[:, :C], out_imag[:, :C])

    @pl.when(step < last)
    def _():
        row = lax.broadcasted_iota(jnp.int32, (rows, 1), 0)
        sub = row % subs
        group = sub // pair_dev
        order_class = row // subs * pair_dev + sub % pair_dev
        share = HALF // width

        def packed_at(tail, place):
            whole = tail[:, 0].astype(f32)
            groups = packing(WHOLE // TILE // per * share, width)[1]
            tile = packed_group(whole, 0, subs)
            for index in range(1, groups):
                tile = jnp.where(place // share == index, packed_group(whole, index, subs), tile)
            return unpacked(tile, place % share, width)

        coarse_rows = jnp.concatenate(
            [flat(coarse[...]), packed_at(coarse_tail, step + first)], axis=1
        )
        coarse_made = jnp.zeros((rows, LANES), f32)
        for odd in range(2):
            pair = pairs[2 * (step + first) + odd]
            own = group == odd
            low = order_class <= pair
            fine_rows = jnp.concatenate(
                [
                    flat(fine[:, odd * per : (odd + 1) * per]),
                    packed_at(fine_tail, 2 * step + odd),
                ],
                axis=1,
            )
            lower = jnp.where(own, coarse_rows, jnp.where(low, fine_rows, 0.0))
            upper = jnp.where(own | ~low, fine_rows, 0.0)
            members[2 * odd] = lower.reshape(n_lat, subs, LANES).astype(bf16)
            members[2 * odd + 1] = upper.reshape(n_lat, subs, LANES).astype(bf16)
            from_lower = apply(lower, 2 * odd)
            from_upper = apply(upper, 2 * odd + 1)
            made = jnp.where(own, from_upper, from_lower + from_upper)
            fine_out[:, odd * per : (odd + 1) * per] = (
                made[:, :WHOLE].reshape(n_lat, per, 8, WHOLE).astype(bf16)
            )
            fine_held[...] += pltpu.roll(made[:, WHOLE:], 2 * step + odd, 1)
            coarse_made = jnp.where(own, from_lower, coarse_made)
        coarse_out[...] = coarse_made[:, :WHOLE].reshape(coarse_out.shape).astype(bf16)
        coarse_held[...] += pltpu.roll(coarse_made[:, WHOLE:], step + first, 1)

    @pl.when(step == last)
    def _():
        fine_out[:, 0] = last_eight([fine_held[...]], n_lat, subs).astype(bf16)
        carry[...] = coarse_held[...]
        if ends:
            coarse_out[:, 0] = last_eight([coarse_held[...]], n_lat, subs).astype(bf16)


def mix(fine, coarse, weight, local_pairs, subs, first, ends, backward, into, carried):
    n_lat, per = fine.shape[0], subs // 8
    count = (fine.shape[1] - 1) // per
    pair_dev = weight.shape[0] // 2
    turns = count // 2
    inside = lambda k: jnp.minimum(k, turns - 1)
    rows = lambda height, place: pl.BlockSpec(
        (n_lat, height, 8, WHOLE), lambda k, pairs: (0, place(k), 0, 0)
    )
    tail = lambda array: rows(1, lambda k: array.shape[1] - 1)
    whole = pl.BlockSpec((n_lat * subs, TILE), lambda k, pairs: (0, 0))
    body, extra, alias = filled(
        functools.partial(mix_body, pair_dev, subs, first, ends, backward), into, 7, 1
    )
    coarse_place = (lambda k: k + first) if ends else (lambda k: inside(k) + first)
    wave = lambda array: jax.ShapeDtypeStruct(array.shape, bf16)
    return call(
        body,
        "mix_back" if backward else "mix",
        2 * count * n_lat * subs * 8 * PADDED * PADDED,
        2 * weight.size * count // pair_dev + 12 * fine.size,
        grid_spec=pltpu.PrefetchScalarGridSpec(
            num_scalar_prefetch=1,
            grid=(turns + 1,),
            in_specs=[
                rows(2 * per, inside),
                tail(fine),
                rows(per, lambda k: inside(k) + first),
                tail(coarse),
                pl.BlockSpec(
                    (4,) + weight.shape[1:], lambda k, pairs: (inside(k) + first, 0, 0, 0)
                ),
                whole,
            ]
            + extra,
            out_specs=[
                rows(2 * per, lambda k: k),
                rows(per, coarse_place),
                pl.BlockSpec((4, n_lat, subs, LANES), lambda k, pairs: (inside(k), 0, 0, 0)),
                whole,
            ],
            scratch_shapes=[pltpu.VMEM((n_lat * subs, TILE), f32)] * 2,
        ),
        out_shape=[
            wave(fine),
            wave(coarse),
            jax.ShapeDtypeStruct((2 * count, n_lat, subs, LANES), bf16),
            jax.ShapeDtypeStruct((n_lat * subs, TILE), f32),
        ],
        input_output_aliases=alias,
    )(local_pairs, fine, fine, coarse, coarse, weight, carried, *([] if into is None else [into]))


def mix_grad_body(n_parts, *refs):
    values, grads, out = refs[:n_parts], refs[n_parts : 2 * n_parts], refs[2 * n_parts]
    gather = lambda parts: jnp.concatenate([flat(part[0]) for part in parts], axis=0)
    value_real, value_imag = [v.astype(bf16) for v in split_parts(gather(values), WIDE)]
    grad_real, grad_imag = [v.astype(bf16) for v in split_parts(gather(grads), C)]
    out[0, :, 0, :] = dot(grad_real, value_real, 0, 0) + dot(grad_imag, value_imag, 0, 0)
    out[0, :, 1, :] = dot(grad_imag, value_real, 0, 0) - dot(grad_real, value_imag, 0, 0)


def mix_gradient(values, grads):
    slots = values[0].shape[0]
    shape = values[0].shape[1:]
    spec = pl.BlockSpec((1,) + shape, lambda k: (k, 0, 0, 0))
    rows = len(values) * math.prod(shape[:2])
    return call(
        functools.partial(mix_grad_body, len(values)),
        "mix_gradient",
        8 * slots * rows * C * WIDE,
        slots * (4 * rows * LANES + 8 * C * WIDE),
        grid=(slots,),
        in_specs=[spec] * (2 * len(values)),
        out_specs=pl.BlockSpec((1, C, 2, WIDE), lambda k: (k, 0, 0, 0)),
        out_shape=jax.ShapeDtypeStruct((slots, C, 2, WIDE), f32),
    )(*values, *grads)


def pixel_body(
    synth, tail, state, cotangent, table, gain, bias, up, up_turned, up_bias, down, down_turned,
    down_bias, out, middle_grad, synth_grad, dense, wide_sums, narrow_sums, held,
    wide_held, narrow_held, tails,
):
    step, last = pl.program_id(0), pl.num_programs(0) - 1
    n_lat, per = synth.shape[:2]
    subs = 8 * per

    @pl.when(step == 0)
    def _():
        held[...] = jnp.zeros_like(held)
        dense[...] = jnp.zeros_like(dense)
        wide_held[...] = jnp.zeros_like(wide_held)
        narrow_held[...] = jnp.zeros_like(narrow_held)
        tails[...] = jnp.zeros_like(tails)

    @pl.when(step < last)
    def _():
        own = unpacked(packed_group(tail[:, 0].astype(f32), 0, subs), step, C - MAIN)
        real, imag = split_parts(jnp.concatenate([flat(synth[...]), own], axis=1), C)
        stacked = jnp.concatenate([real, imag], axis=0).astype(bf16)
        middle = state[0][:, 0, :] + dot(stacked, table[...], 0, 0)
        xhat, scale = norm_stats(middle)
        normed_low = (xhat * gain[...] + bias[...]).astype(bf16)
        pre_act = dot(up_turned[...], normed_low, 1, 0) + up_bias[...]
        share = 0.5 * (1.0 + lax.erf(pre_act * math.sqrt(0.5)))
        density = jnp.exp(-0.5 * pre_act * pre_act) * (1.0 / math.sqrt(2.0 * math.pi))
        hidden_low = (pre_act * share).astype(bf16)
        slope = share + pre_act * density
        out[0] = (middle + dot(down_turned[...], hidden_low, 1, 0) + down_bias[...])[:, None, :]
        grad = cotangent[0][:, 0, :]
        grad_low = grad.astype(bf16)
        pre_grad = dot(down[...], grad_low, 1, 0) * slope
        pre_low = pre_grad.astype(bf16)
        wide_held[...] += pre_grad
        dense[1, :C] += dot(grad_low, hidden_low, 1, 1)
        dense[0, :C] += dot(normed_low, pre_low, 1, 1)
        normed_grad = dot(up[...], pre_low, 1, 0)
        narrow_held[0] += normed_grad * xhat
        narrow_held[1] += normed_grad
        narrow_held[2] += grad
        scaled = normed_grad * gain[...]
        total = grad + scale * (
            scaled
            - jnp.mean(scaled, axis=0, keepdims=True)
            - xhat * jnp.mean(scaled * xhat, axis=0, keepdims=True)
        )
        middle_grad[0] = total
        held[:C] = total
        result = dot(table[...], held[...].astype(bf16), 1, 1)
        rows = result.shape[0] // 2
        joined = join_parts(result[:rows], result[rows:], C)
        synth_grad[...] = joined[:, :WHOLE].reshape(synth_grad.shape).astype(bf16)
        tails[...] += pltpu.roll(joined[:, WHOLE:], step, 1)

    @pl.when(step == last)
    def _():
        synth_grad[:, 0] = last_eight([tails[...]], n_lat, subs).astype(bf16)
        wide_sums[...] = jnp.sum(wide_held[...], axis=1, keepdims=True)
        narrow_sums[...] = jnp.sum(narrow_held[...], axis=2, keepdims=True)


def pixels(synth, state, cotangent, table, params, first, into, dense_rows):
    n_lat, subs = synth.shape[0], table.shape[0] // (2 * synth.shape[0])
    per = subs // 8
    count = (synth.shape[1] - 1) // per
    row = lambda r: jnp.minimum(r, count - 1)
    points = state.shape[3]
    hidden = params[2].shape[1]
    row_spec = pl.BlockSpec((1, C, 1, points), lambda r: (row(r) + first, 0, 0, 0))
    const = lambda array: pl.BlockSpec(array.shape, lambda r: (0,) * array.ndim)
    wave = lambda place: pl.BlockSpec((n_lat, per, 8, WHOLE), lambda r: (0, place(r), 0, 0))
    tail = pl.BlockSpec((n_lat, 1, 8, WHOLE), lambda r: (0, count * per, 0, 0))
    whole = lambda shape: pl.BlockSpec(shape, lambda r: (0,) * len(shape))
    shaped = lambda shape, kind=f32: jax.ShapeDtypeStruct(shape, kind)
    body, extra, alias = filled(pixel_body, into, 5 + len(params), 0, 1)
    return call(
        body,
        "feed_forward",
        2 * count * points * (6 * C * hidden + 2 * table.shape[0] * PADDED),
        count * (4 * C * points * 4 + 4 * n_lat * subs * LANES),
        grid=(count + 1,),
        in_specs=[wave(row), tail, row_spec, row_spec, const(table)] + [const(p) for p in params] + extra,
        input_output_aliases=alias,
        out_specs=[
            row_spec,
            pl.BlockSpec((1, C, points), lambda r: (row(r) + first, 0, 0)),
            wave(lambda r: r),
            whole((2, dense_rows, hidden)),
            whole((hidden, 1)),
            whole((3, C, 1)),
        ],
        out_shape=[
            shaped(state.shape),
            shaped((state.shape[0], C, points)),
            shaped(synth.shape, bf16),
            shaped((2, dense_rows, hidden)),
            shaped((hidden, 1)),
            shaped((3, C, 1)),
        ],
        scratch_shapes=[
            pltpu.VMEM((PADDED, points), f32),
            pltpu.VMEM((hidden, points), f32),
            pltpu.VMEM((3, C, points), f32),
            pltpu.VMEM((n_lat * subs, TILE), f32),
        ],
    )(synth, synth, state, cotangent, table, *params, *([] if into is None else into))


def final_body(wave, tail, state, middle_grad, table, gain, out, sums, held):
    step = pl.program_id(0)

    @pl.when(step == 0)
    def _():
        held[...] = jnp.zeros_like(held)

    own = unpacked(packed_group(tail[:, 0].astype(f32), 0, 8 * wave.shape[1]), step, C - MAIN)
    real, imag = split_parts(jnp.concatenate([flat(wave[...]), own], axis=1), C)
    stacked = jnp.concatenate([real, imag], axis=0).astype(bf16)
    spread_grad = dot(stacked, table[...], 0, 0)
    xhat, scale = norm_stats(state[0][:, 0, :])
    held[0] += spread_grad * xhat
    held[1] += spread_grad
    scaled = spread_grad * gain[...]
    out[0] = (
        middle_grad[0]
        + scale
        * (
            scaled
            - jnp.mean(scaled, axis=0, keepdims=True)
            - xhat * jnp.mean(scaled * xhat, axis=0, keepdims=True)
        )
    )[:, None, :]

    @pl.when(step == pl.num_programs(0) - 1)
    def _():
        sums[...] = jnp.sum(held[...], axis=2, keepdims=True)


def finish(wave, state, middle_grad, table, gain, first, into):
    n_lat, subs = wave.shape[0], table.shape[0] // (2 * wave.shape[0])
    per = subs // 8
    count = (wave.shape[1] - 1) // per
    points = state.shape[3]
    body, extra, alias = filled(final_body, into, 6, 0)
    return call(
        body,
        "first_norm_back",
        2 * count * points * table.shape[0] * PADDED,
        count * (3 * C * points * 4 + 2 * n_lat * subs * LANES),
        grid=(count,),
        in_specs=[
            pl.BlockSpec((n_lat, per, 8, WHOLE), lambda r: (0, r, 0, 0)),
            pl.BlockSpec((n_lat, 1, 8, WHOLE), lambda r: (0, count * per, 0, 0)),
            pl.BlockSpec((1, C, 1, points), lambda r: (r + first, 0, 0, 0)),
            pl.BlockSpec((1, C, points), lambda r: (r + first, 0, 0)),
            pl.BlockSpec(table.shape, lambda r: (0, 0)),
            pl.BlockSpec((C, 1), lambda r: (0, 0)),
        ]
        + extra,
        input_output_aliases=alias,
        out_specs=[
            pl.BlockSpec((1, C, 1, points), lambda r: (r + first, 0, 0, 0)),
            pl.BlockSpec((2, C, 1), lambda r: (0, 0, 0)),
        ],
        out_shape=[
            jax.ShapeDtypeStruct(state.shape, f32),
            jax.ShapeDtypeStruct((2, C, 1), f32),
        ],
        scratch_shapes=[pltpu.VMEM((2, C, points), f32)],
    )(wave, wave, state, middle_grad, table, gain, *([] if into is None else [into]))


def part_rows_body(paired, out):
    turned = paired[0][:, 0, :].T
    count = turned.shape[0] // 2
    for half in range(2):
        out[half] = turned[half * count : (half + 1) * count][:, None, :]


def part_rows(paired):
    pairs, points = paired.shape[0], paired.shape[3] // 2
    return call(
        part_rows_body,
        "part_rows",
        0,
        8 * paired.size,
        grid=(pairs,),
        in_specs=[pl.BlockSpec((1, C, 1, 2 * points), lambda r: (r, 0, 0, 0))],
        out_specs=pl.BlockSpec((2, points, 1, C), lambda r: (r, 0, 0, 0)),
        out_shape=jax.ShapeDtypeStruct((2 * pairs, points, 1, C), f32),
    )(paired)


def fourier_tables(orders, live, points, lon_count):
    phase = (orders * points % lon_count).astype(f32) * (2.0 * math.pi / lon_count)
    kept = live.astype(f32)
    cosine, sine = jnp.cos(phase) * kept, -jnp.sin(phase) * kept
    doubling = jnp.where(orders == 0, 1.0, 2.0).astype(f32)
    forward = jnp.concatenate([cosine / lon_count, sine / lon_count], axis=0)
    inverse = jnp.concatenate([cosine * doubling, sine * doubling], axis=0)
    return forward.astype(bf16), inverse.astype(bf16)


def order_rows(n_lat, pair_dev, subs):
    index = jnp.arange(n_lat * subs, dtype=jnp.int32)[:, None]
    return index // subs, index % subs


def fine_fourier(n_lat, pair_dev, subs, lon_count):
    device, sub = order_rows(n_lat, pair_dev, subs)
    kind = device * pair_dev + sub // 2
    member = sub % 2
    live = (sub < 2 * pair_dev) & jnp.where(
        member == 0, kind <= LB // 2, (kind >= 1) & (kind <= LB // 2 - 1)
    )
    orders = jnp.where(live, jnp.where(member == 0, kind, LB - kind), 0)
    points = jnp.arange(lon_count, dtype=jnp.int32)[None, :]
    return fourier_tables(orders, live, points, lon_count)


def coarse_fourier(n_lat, pair_dev, subs, lon_count):
    device, sub = order_rows(n_lat, pair_dev, subs)
    order = device * pair_dev + sub % pair_dev
    points = jnp.arange(2 * lon_count, dtype=jnp.int32)[None, :]
    live = (sub < 2 * pair_dev) & (order < LA) & (sub // pair_dev == points // lon_count)
    orders = jnp.where((sub < 2 * pair_dev) & (order < LA), order, 0)
    return fourier_tables(orders, live, points % lon_count, lon_count)


class Line:
    def __init__(self):
        self.before = self.last = None
        self.work, self.later = [], []
        self.aside = None

    def swap(self, values):
        self.step_aside()
        waits = self.work + ([] if self.last is None else [self.last])
        if waits:
            values = lax.optimization_barrier((values, waits))[0]
        self.before = self.last
        self.last = lax.all_to_all(values, "lat", split_axis=0, concat_axis=0, tiled=True)
        self.work, self.later = self.later, []
        return self.last

    def step_aside(self):
        if self.aside is not None:
            next(self.aside, None)

    def hold(self, values):
        if self.before is None:
            return values
        return lax.optimization_barrier((values, self.before))[0]

    def after_work(self, values):
        return lax.optimization_barrier((values, self.work))[0] if self.work else values

    def keep(self, values):
        self.work.append(values)
        return values

    def keep_later(self, values):
        self.later.append(values)
        return values


def partners(count, step):
    if count & (count - 1) == 0:
        return [(k, k ^ step) for k in range(count)], lambda rank: jnp.bitwise_xor(rank, step)
    return [(k, (k + step) % count) for k in range(count)], lambda rank: (rank + step) % count


def share_slots(members, n_chan, step):
    share = members.shape[0] // n_chan
    route, find = partners(n_chan, step)
    block = lax.dynamic_slice_in_dim(members, find(lax.axis_index("chan")) * share, share)
    return lax.ppermute(block, "chan", route) if step else block


def sum_over(values, sizes):
    for axis, size in sizes:
        if size & (size - 1):
            values = lax.psum(values, axis)
            continue
        step = 1
        while step < size:
            values = values + lax.ppermute(values, axis, partners(size, step)[0])
            step *= 2
    return values


def add_dense(array, n_lat, n_chan, line, result):
    shape, columns = array.shape, array.shape[2]
    sizes = {"chan": n_chan, "lat": n_lat}
    pairs = [("chan", 2**k) for k in range(n_chan.bit_length() - 1)] + [("lat", 1)]
    others = n_lat // 2
    held = array.reshape(-1, columns)
    odd = lambda axis, step: (lax.axis_index(axis) // step) % 2 == 1
    group = lax.axis_index("lat") // 2

    def halve(held, axis, step):
        low, high = jnp.split(line.hold(held), 2, axis=0)
        upper = odd(axis, step)
        other = lax.ppermute(jnp.where(upper, low, high), axis, partners(sizes[axis], step)[0])
        return line.keep(jnp.where(upper, high, low) + other)

    def double(held, axis, step):
        upper = odd(axis, step)
        other = lax.ppermute(line.hold(held), axis, partners(sizes[axis], step)[0])
        return line.keep_later(
            jnp.concatenate([jnp.where(upper, other, held), jnp.where(upper, held, other)], axis=0)
        )

    for axis, step in pairs[:-1]:
        held = halve(held, axis, step)
    yield
    yield
    held = halve(held, *pairs[-1])
    yield
    pieces = line.hold(held).reshape(others, -1, columns)
    own = lax.dynamic_index_in_dim(pieces, group, 0, False)
    for step in range(1, others):
        block = lax.dynamic_index_in_dim(pieces, jnp.bitwise_xor(group, step), 0, False)
        block = lax.ppermute(block.astype(bf16), "lat", partners(n_lat, 2 * step)[0])
        own = own + block.astype(f32)
    own = line.keep_later(own).astype(bf16)
    yield
    yield
    yield
    own = line.hold(own)
    held = jnp.zeros((others,) + own.shape, bf16)
    for step in range(others):
        block = lax.ppermute(own, "lat", partners(n_lat, 2 * step)[0]) if step else own
        held = lax.dynamic_update_index_in_dim(held, block, jnp.bitwise_xor(group, step), 0)
    held = line.keep_later(held).reshape(-1, columns)
    yield
    yield
    yield
    for axis, step in reversed(pairs[1:]):
        held = double(held, axis, step)
    yield
    held = double(held, *pairs[0])
    result.append(held.astype(f32).reshape(shape))


def shards(
    n_lat, n_chan, coarse_state, fine_state, coarse_noise, fine_noise, coarse_rows, fine_rows,
    pair_slots, first_gain, first_bias, mix_weight, second_gain, second_bias, up_weight, up_bias,
    down_weight, down_bias, coarse_cotangent, fine_cotangent,
):
    pair_dev = mix_weight.shape[0] // 2
    subs = -(-2 * pair_dev // 8) * 8
    lat_rank = lax.axis_index("lat")
    fine_dev, fine_points = fine_state.shape[1], fine_state.shape[2]
    coarse_dev, coarse_points = coarse_state.shape[1], coarse_state.shape[2]
    coarse_two = coarse_dev // 2
    column = lambda vector: vector[:, None]

    def fine_in(values):
        return values.transpose(1, 3, 0, 2)

    def coarse_in(values):
        paired = values[0].reshape(coarse_two, 2 * coarse_points, values.shape[3])
        return paired.transpose(0, 2, 1)[:, :, None, :]

    def fine_back(values):
        return values.transpose(2, 0, 3, 1)

    def coarse_back(values):
        return part_rows(values).transpose(2, 0, 1, 3)

    line = Line()
    dense_unit = 4 * n_lat * n_chan
    dense_rows = -(-(C + 3) // dense_unit) * dense_unit
    row_cuts = [(fine_dev + 1) // 2, fine_dev // 2] if fine_dev >= 8 else [fine_dev]
    row_starts = [sum(row_cuts[:k]) for k in range(len(row_cuts))]
    outer_cuts = [fine_dev // 4 + 1, fine_dev - fine_dev // 4 - 1] if fine_dev >= 8 else [fine_dev]
    outer_starts = [sum(outer_cuts[:k]) for k in range(len(outer_cuts))]
    n_chunks = 2 if pair_dev % 4 == 0 else 1
    chunk_pairs = pair_dev // n_chunks
    chunk_range = range(n_chunks)

    fine_x = fine_in(fine_state)
    fine_noise_in = fine_noise[0].transpose(0, 2, 1)
    fine_forward, fine_inverse = fine_fourier(n_lat, pair_dev, subs, fine_points)
    gain_one, bias_one = column(first_gain), column(first_bias)
    fine_four = []
    for start, count in zip(outer_starts, outer_cuts):
        made = spread(fine_x, fine_noise_in, gain_one, bias_one, fine_forward, n_lat, start, count)
        fine_four.append(line.swap(line.keep(made)))
    coarse_x = coarse_in(coarse_state)
    coarse_forward, coarse_inverse = coarse_fourier(n_lat, pair_dev, subs, coarse_points)
    coarse_noise_in = coarse_in(coarse_noise)[:, :, 0, :]
    coarse_four = line.swap(
        spread(coarse_x, coarse_noise_in, gain_one, bias_one, coarse_forward, n_lat, 0, coarse_two)
    )

    wide = -(-pair_dev // 8) * 8
    classes = lat_rank * pair_dev + jnp.arange(wide, dtype=jnp.int32)
    classes = jnp.where(jnp.arange(wide) < pair_dev, classes, LB).astype(jnp.int32)
    coarse_order = coarse_rows.reshape(-1, 2).T.reshape(-1)
    by_device = fine_rows.reshape(n_lat, fine_dev)
    in_order = lambda starts, cuts: jnp.concatenate(
        [by_device[:, a : a + c].reshape(-1) for a, c in zip(starts, cuts)]
    )
    unused, fine_quad = legendre_tables(
        in_order(outer_starts, outer_cuts), pair_slots, classes, LB, True
    )
    fine_plain, unused = legendre_tables(
        in_order(row_starts, row_cuts), pair_slots, classes, LB, True
    )
    coarse_plain, coarse_quad = legendre_tables(coarse_order, pair_slots, classes, LA, False)
    turn = lambda table, chunks=n_chunks: by_class(table, n_lat, pair_dev, chunks)

    def fine_tables(parts):
        first, near, far = [turn(part) for part in parts]
        table_a = jnp.concatenate([first, near], axis=1)
        return [table_a, far], [table_a.transpose(0, 2, 1), far.transpose(0, 2, 1)]

    fine_quad_in, fine_quad_out = fine_tables(fine_quad)
    fine_plain_in, fine_plain_out = fine_tables(fine_plain)
    coarse_quad_in = turn(coarse_quad[0], 1)
    coarse_plain_in = turn(coarse_plain[0], 1)
    coarse_quad_out = coarse_quad_in.transpose(0, 2, 1)
    coarse_plain_out = coarse_plain_in.transpose(0, 2, 1)
    local_pairs = lax.dynamic_slice_in_dim(pair_slots, lat_rank * pair_dev, pair_dev)
    weight = mix_weight.transpose(0, 1, 3, 2)

    fine_work = functools.partial(to_degrees_fine, pair_dev)
    fine_back_work = functools.partial(to_orders_fine, pair_dev)
    coarse_work = functools.partial(coarse_either_way, pair_dev)

    def spectral(coarse_chunk, fine_chunks, in_tables, out_tables, cuts, backward, aside):
        wide = (C if backward else WIDE) - MAIN
        fine_made = lane_call(
            fine_work, "rows_to_degrees", line.hold(fine_chunks), in_tables[1],
            [chunk_pairs] * n_chunks, subs, wide,
        )
        line.keep(fine_made)
        arrived, mixed, shared = [], [], []

        def mix_chunk(k):
            fine, coarse = line.hold((arrived[k], arrived_coarse))
            carried = mixed[-1][3] if mixed else jnp.zeros((n_lat * subs, TILE), f32)
            made = mix(
                fine, coarse, weight, local_pairs, subs, k * chunk_pairs // 2, k == n_chunks - 1,
                backward, mixed[-1][1] if mixed else None, carried,
            )
            mixed.append(line.keep(made))

        def share_next(count=1):
            members = joined_rows([made[2] for made in mixed])
            for step in range(len(shared), min(len(shared) + count, n_chan)):
                shared.append(line.keep_later(share_slots(line.hold(members), n_chan, step)))

        arrived.append(line.swap(fine_made[0]))
        coarse_made = lane_call(
            coarse_work, "rows_to_degrees", [line.hold(coarse_chunk)], [in_tables[0]],
            [pair_dev // 2], subs, wide,
        )[0]
        arrived_coarse = line.swap(line.keep(coarse_made))
        line.keep(out_tables)
        for k in range(1, n_chunks):
            arrived.append(line.swap(fine_made[k]))
            mix_chunk(k - 1)
        if n_chunks == 1:
            mix_chunk(0)
        fine_back = []
        for k in range(n_chunks - 1):
            fine_back.append(line.swap(mixed[k][0]))
            mix_chunk(k + 1)
        arrived_coarse = line.swap(mixed[-1][1])
        share_next(2)
        fine_back.append(line.swap(mixed[-1][0]))
        share_next()
        coarse_made = lane_call(
            coarse_work, "degrees_to_rows", [line.hold(arrived_coarse)], [out_tables[0]],
            [coarse_two], subs, C - MAIN,
        )[0]
        coarse_end = line.swap(line.keep(coarse_made))
        share_next(n_chan)
        fine_made = lane_call(
            fine_back_work, "degrees_to_rows", line.hold(fine_back), out_tables[1],
            cuts, subs, C - MAIN,
        )
        line.keep(fine_made)
        fine_end = [None] * len(cuts)
        order = list(range(len(cuts)))
        if backward:
            order.reverse()
        for k, place in enumerate(order):
            fine_end[place] = line.swap(fine_made[place])
            aside(k, coarse_end, fine_end, shared)
        return fine_end, shared

    params = [
        column(second_gain), column(second_bias), up_weight, up_weight.T, column(up_bias),
        down_weight, down_weight.T, column(down_bias),
    ]
    coarse_g, fine_g = coarse_in(coarse_cotangent), fine_in(fine_cotangent)
    coarse_made, fine_made = [], []

    def fine_pixels(k, synth):
        into = fine_made[-1][:2] if fine_made else None
        made = pixels(
            line.hold(synth), fine_x, fine_g, fine_inverse, params, row_starts[k], into,
            dense_rows,
        )
        fine_made.append(line.keep(made))

    def forward_aside(k, coarse_end, fine_end, shared):
        if k == 0:
            made = pixels(
                line.hold(coarse_end), coarse_x, coarse_g, coarse_inverse, params, 0, None,
                dense_rows,
            )
            coarse_made.extend(line.keep(made))
        else:
            fine_pixels(k - 1, fine_end[k - 1])

    fine_synth, values = spectral(
        coarse_four, fine_four, (coarse_quad_in, fine_quad_in), (coarse_plain_out, fine_plain_out),
        row_cuts, False, forward_aside,
    )
    if len(row_cuts) == 1:
        fine_pixels(0, fine_synth[0])
    fine_sgrad = []
    for k in range(len(row_cuts)):
        fine_sgrad.append(line.swap(fine_made[k][2]))
        if k + 1 < len(row_cuts):
            fine_pixels(k + 1, fine_synth[k + 1])
    axes = (("chan", n_chan), ("lat", n_lat))
    hidden = up_bias.shape[0]
    total = coarse_made[3:]
    for made in fine_made:
        total = [x + y for x, y in zip(total, made[3:])]
    narrow = jnp.concatenate([total[1][:, 0], total[2].reshape(-1)])
    narrow = jnp.pad(narrow, (0, 3 * hidden - narrow.shape[0])).reshape(1, 3, hidden)
    stacked = lax.dynamic_update_slice(total[0], narrow, (0, C, 0))
    dense = []
    line.aside = add_dense(line.hold(stacked), n_lat, n_chan, line, dense)
    line.step_aside()
    coarse_sgrad = line.swap(coarse_made[2])
    coarse_made[0] = line.keep(coarse_back(line.hold(coarse_made[0])))
    ends, mix_grads = [], []

    def finish_fine(place, wave):
        into = ends[-1][0] if len(ends) > 1 else None
        return finish(
            wave, fine_x, fine_made[-1][1], fine_forward, gain_one, outer_starts[place], into
        )

    def backward_aside(k, coarse_end, fine_end, shared):
        if k == 0:
            mix_grads.append(line.keep(mix_gradient(values, line.hold(shared))))
            made = finish(
                line.hold(coarse_end), coarse_x, coarse_made[1], coarse_forward, gain_one, 0, None
            )
            made = [coarse_back(made[0]), made[1]]
        else:
            made = finish_fine(len(outer_cuts) - k, line.hold(fine_end[-k]))
        ends.append(list(line.keep(made)))

    fine_fgrad, grads = spectral(
        coarse_sgrad, fine_sgrad, (coarse_plain_in, fine_plain_in), (coarse_quad_out, fine_quad_out),
        outer_cuts, True, backward_aside,
    )
    for unused in line.aside:
        pass
    up_grad, down_grad = line.keep((dense[0][0, :C], dense[0][1, :C]))
    narrow = dense[0][0, C : C + 3].reshape(-1)
    narrow_sums = narrow[hidden : hidden + 3 * C].reshape(3, C)
    last_wave = lax.optimization_barrier((fine_fgrad[0], line.work + line.later))[0]
    ends.append(finish_fine(0, last_wave))
    mix_grad = mix_grads[0].transpose(0, 2, 3, 1)
    sums = sum(end[1] for end in ends)
    first_sums = sum_over(sums[:, :, 0], axes)
    return (
        coarse_made[0],
        fine_back(fine_made[-1][0]),
        ends[0][0],
        fine_back(ends[-1][0]),
        first_sums[0],
        first_sums[1],
        mix_grad,
        narrow_sums[0],
        narrow_sums[1],
        up_grad,
        narrow[:hidden],
        down_grad.T,
        narrow_sums[2],
    )


def solution(mesh):
    pixel = P("chan", "lat", None, None)
    slots = P("lat", None, None, None)
    return jax.shard_map(
        functools.partial(shards, mesh.shape["lat"], mesh.shape["chan"]),
        mesh=mesh,
        in_specs=(pixel,) * 4 + (P(),) * 5 + (slots,) + (P(),) * 6 + (pixel,) * 2,
        out_specs=(pixel,) * 4 + (P(),) * 2 + (P(("lat", "chan"), None, None, None),) + (P(),) * 6,
        check_vma=False,
    )
```

```python
import functools
import math

import jax
import jax.numpy as jnp
from jax import lax
from jax.experimental import pallas as pl
from jax.experimental.pallas import tpu as pltpu
from jax.sharding import PartitionSpec as P

C = 641
NOISE = 8
WIDE = C + NOISE
LA = 90
LB = 180

TILE = 128
MAIN = C // TILE * TILE
HALF = TILE // 2
WHOLE = 2 * MAIN
LANES = WHOLE + TILE
PADDED = MAIN + TILE

epsilon = 1e-05
noise_scale = 1.0 / 262144.0
bf16 = jnp.bfloat16
f32 = jnp.float32
VMEM_LIMIT = 62 * 2**20


def call(body, name, flops, moved, **options):
    if "grid_spec" not in options:
        options.setdefault("scratch_shapes", [])
    return pl.pallas_call(
        body,
        compiler_params=pltpu.CompilerParams(vmem_limit_bytes=VMEM_LIMIT),
        cost_estimate=pl.CostEstimate(flops=int(flops), bytes_accessed=int(moved), transcendentals=0),
        name=name,
        **options,
    )


def filled(body, into, position, *outputs):
    if into is None:
        return body, [], {}
    count = len(outputs)

    def skipping(*refs):
        body(*refs[:position], *refs[position + count :])

    alias = {position + k: output for k, output in enumerate(outputs)}
    return skipping, [pl.BlockSpec(memory_space=pl.ANY)] * count, alias


def dot(left, right, left_dim, right_dim):
    return lax.dot_general(
        left, right, (((left_dim,), (right_dim,)), ((), ())), preferred_element_type=f32
    )


def join_parts(real, imag, count):
    tail = real[:, MAIN:] + pltpu.roll(imag[:, MAIN:], HALF, 1)
    return jnp.concatenate([real[:, :MAIN], imag[:, :MAIN], tail], axis=1)


def join_narrow(real, imag):
    lane = lax.broadcasted_iota(jnp.int32, (real.shape[0], TILE), 1)
    tail = jnp.where(
        lane == 0, real[:, MAIN:C], jnp.where(lane == HALF, imag[:, MAIN:C], 0.0)
    )
    return jnp.concatenate([real[:, :MAIN], imag[:, :MAIN], tail], axis=1)


def split_parts(joined, count):
    tail = joined[:, 2 * MAIN :]
    real = jnp.concatenate([joined[:, :MAIN], tail], axis=1)[:, :count]
    imag = jnp.concatenate(
        [joined[:, MAIN : 2 * MAIN], pltpu.roll(tail, HALF, 1)], axis=1
    )[:, :count]
    return real, imag


def packing(rows, width):
    share = HALF // width
    return share, -(-rows // share)


def eights(rows, subs):
    return rows * (subs // 8) + 1


def packed_group(tail, group, subs):
    count = subs // 8
    tiles = [tail[:, :, (group * count + k) * TILE :][:, :, :TILE] for k in range(count)]
    return jnp.stack(tiles, axis=1).reshape(-1, TILE)


def unpacked(group_tile, place, width):
    turned = pltpu.roll(group_tile, (TILE - place * width) % TILE, 1)
    lane = lax.broadcasted_iota(jnp.int32, turned.shape, 1)
    return jnp.where(lane % HALF < width, turned, 0.0)


def last_eight(groups, n_lat, subs):
    count = subs // 8
    tiles = []
    for group in groups:
        split = group.reshape(n_lat, count, 8, TILE)
        tiles += [split[:, k] for k in range(count)]
    blank = jnp.zeros((n_lat, 8, TILE), f32)
    return jnp.concatenate(tiles + [blank] * (WHOLE // TILE - len(tiles)), axis=2)


def flat(block):
    return block.astype(f32).reshape(-1, block.shape[-1])


def joined_rows(parts):
    return parts[0] if len(parts) == 1 else jnp.concatenate(parts, axis=0)


def norm_stats(values):
    centered = values - jnp.mean(values, axis=0, keepdims=True)
    variance = jnp.mean(centered * centered, axis=0, keepdims=True)
    scale = lax.rsqrt(variance + epsilon)
    return centered * scale, scale


def spread_body(state, noise, gain, bias, table, out, held, tails):
    step, last = pl.program_id(0), pl.num_programs(0) - 1
    n_lat, count, unused, lanes = out.shape
    width = WIDE - MAIN
    share = HALF // width

    @pl.when(step == 0)
    def _():
        held[...] = jnp.zeros_like(held)
        tails[...] = jnp.zeros_like(tails)

    @pl.when(step < last)
    def _():
        xhat, unused = norm_stats(state[0][:, 0, :])
        held[:C] = xhat * gain[...] + bias[...]
        held[C:WIDE] = ((noise[0].astype(f32) + 0.5) * noise_scale - 0.5) * math.sqrt(12.0)
        result = dot(table[...], held[...].astype(bf16), 1, 1)
        rows = result.shape[0] // 2
        joined = join_parts(result[:rows], result[rows:], WIDE)
        out[...] = joined[:, :WHOLE].reshape(out.shape).astype(bf16)
        tails[step // share] += pltpu.roll(joined[:, WHOLE:], step % share * width, 1)

    @pl.when(step == last)
    def _():
        groups = [tails[k] for k in range(tails.shape[0])]
        out[:, 0] = last_eight(groups, n_lat, 8 * count).astype(bf16)


def spread(state, noise, gain, bias, table, n_lat, first, count):
    points = state.shape[3]
    subs = table.shape[0] // (2 * n_lat)
    const = lambda r: (0, 0)
    row = lambda r: jnp.minimum(r, count - 1) + first
    return call(
        spread_body,
        "norm_and_dft",
        2 * count * table.shape[0] * points * PADDED,
        count * (C * points * 4 + n_lat * subs * LANES * 2),
        grid=(count + 1,),
        in_specs=[
            pl.BlockSpec((1, C, 1, points), lambda r: (row(r), 0, 0, 0)),
            pl.BlockSpec((1, NOISE, points), lambda r: (row(r), 0, 0)),
            pl.BlockSpec((C, 1), const),
            pl.BlockSpec((C, 1), const),
            pl.BlockSpec(table.shape, const),
        ],
        out_specs=pl.BlockSpec((n_lat, subs // 8, 8, WHOLE), lambda r: (0, r, 0, 0)),
        out_shape=jax.ShapeDtypeStruct((n_lat, eights(count, subs), 8, WHOLE), bf16),
        scratch_shapes=[
            pltpu.VMEM((PADDED, points), f32),
            pltpu.VMEM((packing(count, WIDE - MAIN)[1], n_lat * subs, TILE), f32),
        ],
    )(state, noise, gain, bias, table)


def legendre_body(total, pairs, order_a, order_b, diag_a, diag_b, cosine, classes, *refs):
    two = order_b is not None
    outs, (held_a, held_b) = refs[: 3 if two else 1], (refs[3:] if two else (refs[1], None))

    def advance(degree, order, diagonal, previous, earlier):
        real = degree.astype(f32)
        grow = jnp.sqrt(
            (4.0 * real * real - 1.0) / jnp.maximum(real * real - order * order, 1.0)
        )
        damp = jnp.sqrt(
            jnp.maximum((real - 1.0) * (real - 1.0) - order * order, 0.0)
            / jnp.maximum(4.0 * (real - 1.0) * (real - 1.0) - 1.0, 1.0)
        )
        grown = grow * (cosine[...] * previous - damp * earlier)
        return jnp.where(real == order, diagonal, jnp.where(real > order, grown, 0.0))

    def step(degree, carry):
        now_a = advance(degree, order_a[...], diag_a[...], carry[0], carry[1])
        held_a[degree] = now_a
        if not two:
            return (now_a, carry[0])
        now_b = advance(degree, order_b[...], diag_b[...], carry[2], carry[3])
        held_b[degree] = now_b
        return (now_a, carry[0], now_b, carry[2])

    zero = diag_a[...] * 0.0
    lax.fori_loop(0, total, step, (zero,) * (4 if two else 2))

    def pick(slot, unused):
        pair = pairs[slot]
        safe = jnp.maximum(pair, 0)
        live = jnp.where(pair >= 0, 1.0, 0.0)
        low = classes[...] <= pair
        near = held_a[safe] * live
        if two:
            far = held_a[LB - 1 - safe] * live
            outs[0][slot] = jnp.where(low, near, far)
            outs[1][slot] = jnp.where(low, far, 0.0)
            outs[2][slot] = jnp.where(low, 0.0, held_b[LB - 1 - safe] * live)
        else:
            outs[0][slot] = jnp.where(low, near, 0.0)
        return unused

    lax.fori_loop(0, pairs.shape[0], pick, 0)


def diagonal_values(orders, live, sines):
    order_real = orders.astype(f32)[:, None]
    log_start = 0.5 * jnp.log((2.0 * order_real + 1.0) / (4.0 * math.pi))
    log_start = log_start + 0.5 * (
        lax.lgamma(2.0 * order_real + 1.0)
        - 2.0 * order_real * math.log(2.0)
        - 2.0 * lax.lgamma(order_real + 1.0)
    )
    diagonal = jnp.exp(log_start + order_real * jnp.log(sines)[None, :])
    return jnp.where(live[:, None], diagonal, 0.0)


def legendre_tables(row_table, pair_slots, classes, total, two):
    slots, rows, wide = pair_slots.shape[0], row_table.shape[0], classes.shape[0]
    occupied = (row_table >= 0).astype(f32)
    colatitude = math.pi * (jnp.maximum(row_table, 0).astype(f32) + 0.5) / total
    sines = jnp.sin(colatitude)
    cosine = jnp.broadcast_to(jnp.cos(colatitude)[None, :], (wide, rows))
    spread_out = lambda v: jnp.broadcast_to(v.astype(f32)[:, None], (wide, rows))
    top = LB // 2 if two else LA - 1
    order_a = jnp.where(classes <= top, classes, 0)
    diag_a = diagonal_values(order_a, classes <= top, sines)
    live_b = (classes >= 1) & (classes <= LB // 2 - 1)
    order_b = jnp.where(live_b, LB - classes, 0)
    diag_b = diagonal_values(order_b, live_b, sines)
    class_wide = jnp.broadcast_to(classes[:, None], (wide, rows))
    if two:
        arrays = [spread_out(order_a), spread_out(order_b), diag_a, diag_b, cosine, class_wide]
        body = functools.partial(legendre_body, total)
    else:
        arrays = [spread_out(order_a), diag_a, cosine, class_wide]

        def body(pairs, order, diagonal, cosines, class_ref, *refs):
            legendre_body(total, pairs, order, None, diagonal, None, cosines, class_ref, *refs)

    shape = jax.ShapeDtypeStruct((slots, wide, rows), f32)
    count = 3 if two else 1
    tables = call(
        body,
        "legendre_tables",
        total * wide * rows * 40,
        count * slots * wide * rows * 4,
        in_specs=[pl.BlockSpec(memory_space=pltpu.SMEM)]
        + [pl.BlockSpec(memory_space=pltpu.VMEM)] * len(arrays),
        out_specs=[pl.BlockSpec(memory_space=pltpu.VMEM)] * count,
        out_shape=[shape] * count,
        scratch_shapes=[pltpu.VMEM((total, wide, rows), f32)] * (2 if two else 1),
    )(pair_slots, *arrays)
    plain = [table * occupied for table in tables]
    weight = sines * occupied * (2.0 * math.pi * math.pi / total)
    return plain, [table * weight for table in plain]


def by_class(table, n_lat, pair_dev, n_chunks):
    split = table.reshape(n_lat, n_chunks, pair_dev // (2 * n_chunks), 2, *table.shape[1:])
    moved = split.transpose(4, 3, 1, 0, 2, 5)[:pair_dev]
    return moved.reshape(pair_dev, n_lat * pair_dev, table.shape[2]).astype(bf16)


def to_degrees_fine(pair_dev, subs, tables, held, results):
    table_a, table_b = tables
    half = sum(result.shape[0] for result in results) // (2 * subs)

    def order_rows(sub):
        parts = [keep[pl.ds(sub, keep.shape[0] // subs, stride=subs), :] for keep in held]
        return joined_rows(parts).astype(bf16)

    for index in range(pair_dev):
        from_a = dot(table_a[index], order_rows(2 * index), 1, 0)
        from_b = dot(table_b[index], order_rows(2 * index + 1), 1, 0)
        first, second = from_a[: 2 * half], from_a[2 * half :] + from_b
        begin = 0
        for odd in range(2):
            start = odd * subs + index
            for result in results:
                count = result.shape[0] // (2 * subs)
                rows = slice(begin, begin + count)
                begin += count
                result[pl.ds(start + (1 - odd) * pair_dev, count, stride=2 * subs), :] = first[rows]
                result[pl.ds(start + odd * pair_dev, count, stride=2 * subs), :] = second[rows]


def to_orders_fine(pair_dev, subs, tables, held, results):
    table_a, table_b = tables
    for index in range(pair_dev):
        first, second = [], []
        for odd in range(2):
            start = odd * subs + index
            for keep in held:
                count = keep.shape[0] // (2 * subs)
                first.append(keep[pl.ds(start + (1 - odd) * pair_dev, count, stride=2 * subs), :])
                second.append(keep[pl.ds(start + odd * pair_dev, count, stride=2 * subs), :])
        second = joined_rows(second)
        both = joined_rows(first + [second]).astype(bf16)
        made = (dot(table_a[index], both, 1, 0), dot(table_b[index], second.astype(bf16), 1, 0))
        for member in range(2):
            begin = 0
            for result in results:
                rows = result.shape[0] // subs
                result[pl.ds(2 * index + member, rows, stride=subs), :] = made[member][
                    begin : begin + rows
                ]
                begin += rows


def coarse_either_way(pair_dev, subs, tables, held, results):
    (keep,), (result,), (table,) = held, results, tables
    before, after = keep.shape[0] // subs, result.shape[0] // subs
    for index in range(pair_dev):
        taken = joined_rows(
            [keep[pl.ds(odd * pair_dev + index, before, stride=subs), :] for odd in range(2)]
        ).astype(bf16)
        made = dot(table[index], taken, 1, 0)
        for odd in range(2):
            result[pl.ds(odd * pair_dev + index, after, stride=subs), :] = made[
                odd * after : (odd + 1) * after
            ]


def lane_body(work, subs, width, n_in, n_tables, n_out, *refs):
    cuts = [n_in, n_in, n_tables, n_out, n_in, n_out, n_out]
    mains, tails, tables, outs, held, results, packed = [
        refs[sum(cuts[:k]) : sum(cuts[: k + 1])] for k in range(len(cuts))
    ]
    step = pl.program_id(0)
    n_lat, per = mains[0].shape[0], subs // 8

    @pl.when(step == 0)
    def _():
        for tail, keep in zip(tails, held):
            rows = keep.shape[0] // (n_lat * subs)
            share, groups = packing(rows, width)
            whole = tail[:, 0].astype(f32)
            for group in range(groups):
                tile = packed_group(whole, group, subs)
                for row in range(group * share, min(rows, (group + 1) * share)):
                    own = unpacked(tile, row % share, width)
                    for device in range(n_lat):
                        keep[pl.ds((device * rows + row) * subs, subs), :] = own[
                            device * subs : (device + 1) * subs
                        ]
        for result in results:
            result[...] = jnp.zeros_like(result)

    @pl.when(step > 0)
    def _():
        for main, keep in zip(mains, held):
            keep[...] = flat(main[:, : main.shape[1] - 1])

    work(subs, tables, held, results)

    @pl.when(step == 0)
    def _():
        for result, pack in zip(results, packed):
            rows = result.shape[0] // (n_lat * subs)
            share, groups = packing(rows, width)
            pack[...] = jnp.zeros_like(pack)
            made = result[...].reshape(n_lat, rows, subs, TILE)
            for group in range(groups):
                total = jnp.zeros((n_lat * subs, TILE), f32)
                for row in range(group * share, min(rows, (group + 1) * share)):
                    own = made[:, row].reshape(n_lat * subs, TILE)
                    total = total + pltpu.roll(own, row % share * width, 1)
                split = total.reshape(n_lat, per, 8, TILE)
                for k in range(per):
                    pack[group * per + k] = split[:, k]

    @pl.when(step > 0)
    def _():
        for out, result, pack in zip(outs, results, packed):
            count = out.shape[1] - 1
            out[:, :count] = result[...].reshape(n_lat, count, 8, TILE).astype(bf16)
            out[:, count] = pack[step - 1].astype(bf16)


def lane_call(work, name, inputs, tables, rows_out, subs, width):
    n_lat = inputs[0].shape[0]
    outs = [(n_lat, eights(rows, subs), 8, WHOLE) for rows in rows_out]
    rows_in = [(a.shape[1] - 1) * 8 // subs for a in inputs]
    tiled = lambda shape: pl.BlockSpec(
        tuple(shape[:3]) + (TILE,), lambda t: (0, 0, 0, jnp.maximum(t - 1, 0))
    )
    tail = lambda shape: pl.BlockSpec(
        (shape[0], 1, 8, WHOLE), lambda t, last=shape[1] - 1: (0, last, 0, 0)
    )
    whole = lambda shape: pl.BlockSpec(shape, lambda t: (0, 0, 0))
    held = lambda rows: pltpu.VMEM((n_lat * rows * subs, TILE), f32)
    moved = sum(2 * math.prod(s) for s in [a.shape for a in inputs] + outs)
    flops = sum(2 * math.prod(t.shape) for t in tables) * LANES
    return call(
        functools.partial(lane_body, work, subs, width, len(inputs), len(tables), len(outs)),
        name,
        flops,
        moved,
        grid=(WHOLE // TILE + 1,),
        in_specs=[tiled(a.shape) for a in inputs]
        + [tail(a.shape) for a in inputs]
        + [whole(t.shape) for t in tables],
        out_specs=[tiled(shape) for shape in outs],
        out_shape=[jax.ShapeDtypeStruct(shape, bf16) for shape in outs],
        scratch_shapes=[held(rows) for rows in rows_in]
        + [held(rows) for rows in rows_out]
        + [pltpu.VMEM((WHOLE // TILE, n_lat, 8, TILE), f32) for unused in outs],
    )(*inputs, *inputs, *tables)


def mix_body(
    pair_dev, subs, first, ends, backward, pairs, fine, fine_tail, coarse, coarse_tail, weight,
    carried, fine_out, coarse_out, members, carry, fine_held, coarse_held,
):
    step, last = pl.program_id(0), pl.num_programs(0) - 1
    n_lat, per = fine.shape[0], subs // 8
    rows = n_lat * subs
    width = (C if backward else WIDE) - MAIN
    count = C if backward else WIDE

    @pl.when(step == 0)
    def _():
        fine_held[...] = jnp.zeros_like(fine_held)
        coarse_held[...] = carried[...]

    def apply(values, slot):
        real, imag = split_parts(values, count)
        stacked = jnp.concatenate([real, imag], axis=0).astype(bf16)
        by_real = dot(stacked, weight[slot, 0], 1, 0 if backward else 1)
        by_imag = dot(stacked, weight[slot, 1], 1, 0 if backward else 1)
        if backward:
            out_real = by_real[:rows] + by_imag[rows:]
            out_imag = by_real[rows:] - by_imag[:rows]
        else:
            out_real = by_real[:rows] - by_imag[rows:]
            out_imag = by_imag[:rows] + by_real[rows:]
        return join_narrow(out_real[:, :C], out_imag[:, :C])

    @pl.when(step < last)
    def _():
        row = lax.broadcasted_iota(jnp.int32, (rows, 1), 0)
        sub = row % subs
        group = sub // pair_dev
        order_class = row // subs * pair_dev + sub % pair_dev
        share = HALF // width

        def packed_at(tail, place):
            whole = tail[:, 0].astype(f32)
            groups = packing(WHOLE // TILE // per * share, width)[1]
            tile = packed_group(whole, 0, subs)
            for index in range(1, groups):
                tile = jnp.where(place // share == index, packed_group(whole, index, subs), tile)
            return unpacked(tile, place % share, width)

        coarse_rows = jnp.concatenate(
            [flat(coarse[...]), packed_at(coarse_tail, step + first)], axis=1
        )
        coarse_made = jnp.zeros((rows, LANES), f32)
        for odd in range(2):
            pair = pairs[2 * (step + first) + odd]
            own = group == odd
            low = order_class <= pair
            fine_rows = jnp.concatenate(
                [
                    flat(fine[:, odd * per : (odd + 1) * per]),
                    packed_at(fine_tail, 2 * step + odd),
                ],
                axis=1,
            )
            lower = jnp.where(own, coarse_rows, jnp.where(low, fine_rows, 0.0))
            upper = jnp.where(own | ~low, fine_rows, 0.0)
            members[2 * odd] = lower.reshape(n_lat, subs, LANES).astype(bf16)
            members[2 * odd + 1] = upper.reshape(n_lat, subs, LANES).astype(bf16)
            from_lower = apply(lower, 2 * odd)
            from_upper = apply(upper, 2 * odd + 1)
            made = jnp.where(own, from_upper, from_lower + from_upper)
            fine_out[:, odd * per : (odd + 1) * per] = (
                made[:, :WHOLE].reshape(n_lat, per, 8, WHOLE).astype(bf16)
            )
            fine_held[...] += pltpu.roll(made[:, WHOLE:], 2 * step + odd, 1)
            coarse_made = jnp.where(own, from_lower, coarse_made)
        coarse_out[...] = coarse_made[:, :WHOLE].reshape(coarse_out.shape).astype(bf16)
        coarse_held[...] += pltpu.roll(coarse_made[:, WHOLE:], step + first, 1)

    @pl.when(step == last)
    def _():
        fine_out[:, 0] = last_eight([fine_held[...]], n_lat, subs).astype(bf16)
        carry[...] = coarse_held[...]
        if ends:
            coarse_out[:, 0] = last_eight([coarse_held[...]], n_lat, subs).astype(bf16)


def mix(fine, coarse, weight, local_pairs, subs, first, ends, backward, into, carried):
    n_lat, per = fine.shape[0], subs // 8
    count = (fine.shape[1] - 1) // per
    pair_dev = weight.shape[0] // 2
    turns = count // 2
    inside = lambda k: jnp.minimum(k, turns - 1)
    rows = lambda height, place: pl.BlockSpec(
        (n_lat, height, 8, WHOLE), lambda k, pairs: (0, place(k), 0, 0)
    )
    tail = lambda array: rows(1, lambda k: array.shape[1] - 1)
    whole = pl.BlockSpec((n_lat * subs, TILE), lambda k, pairs: (0, 0))
    body, extra, alias = filled(
        functools.partial(mix_body, pair_dev, subs, first, ends, backward), into, 7, 1
    )
    coarse_place = (lambda k: k + first) if ends else (lambda k: inside(k) + first)
    wave = lambda array: jax.ShapeDtypeStruct(array.shape, bf16)
    return call(
        body,
        "mix_back" if backward else "mix",
        2 * count * n_lat * subs * 8 * PADDED * PADDED,
        2 * weight.size * count // pair_dev + 12 * fine.size,
        grid_spec=pltpu.PrefetchScalarGridSpec(
            num_scalar_prefetch=1,
            grid=(turns + 1,),
            in_specs=[
                rows(2 * per, inside),
                tail(fine),
                rows(per, lambda k: inside(k) + first),
                tail(coarse),
                pl.BlockSpec(
                    (4,) + weight.shape[1:], lambda k, pairs: (inside(k) + first, 0, 0, 0)
                ),
                whole,
            ]
            + extra,
            out_specs=[
                rows(2 * per, lambda k: k),
                rows(per, coarse_place),
                pl.BlockSpec((4, n_lat, subs, LANES), lambda k, pairs: (inside(k), 0, 0, 0)),
                whole,
            ],
            scratch_shapes=[pltpu.VMEM((n_lat * subs, TILE), f32)] * 2,
        ),
        out_shape=[
            wave(fine),
            wave(coarse),
            jax.ShapeDtypeStruct((2 * count, n_lat, subs, LANES), bf16),
            jax.ShapeDtypeStruct((n_lat * subs, TILE), f32),
        ],
        input_output_aliases=alias,
    )(local_pairs, fine, fine, coarse, coarse, weight, carried, *([] if into is None else [into]))


def mix_grad_body(n_parts, *refs):
    values, grads, out = refs[:n_parts], refs[n_parts : 2 * n_parts], refs[2 * n_parts]
    gather = lambda parts: jnp.concatenate([flat(part[0]) for part in parts], axis=0)
    value_real, value_imag = [v.astype(bf16) for v in split_parts(gather(values), WIDE)]
    grad_real, grad_imag = [v.astype(bf16) for v in split_parts(gather(grads), C)]
    out[0, :, 0, :] = dot(grad_real, value_real, 0, 0) + dot(grad_imag, value_imag, 0, 0)
    out[0, :, 1, :] = dot(grad_imag, value_real, 0, 0) - dot(grad_real, value_imag, 0, 0)


def mix_gradient(values, grads):
    slots = values[0].shape[0]
    shape = values[0].shape[1:]
    spec = pl.BlockSpec((1,) + shape, lambda k: (k, 0, 0, 0))
    rows = len(values) * math.prod(shape[:2])
    return call(
        functools.partial(mix_grad_body, len(values)),
        "mix_gradient",
        8 * slots * rows * C * WIDE,
        slots * (4 * rows * LANES + 8 * C * WIDE),
        grid=(slots,),
        in_specs=[spec] * (2 * len(values)),
        out_specs=pl.BlockSpec((1, C, 2, WIDE), lambda k: (k, 0, 0, 0)),
        out_shape=jax.ShapeDtypeStruct((slots, C, 2, WIDE), f32),
    )(*values, *grads)


def pixel_body(
    synth, tail, state, cotangent, table, gain, bias, up, up_turned, up_bias, down, down_turned,
    down_bias, out, middle_grad, synth_grad, dense, wide_sums, narrow_sums, held,
    wide_held, narrow_held, tails,
):
    step, last = pl.program_id(0), pl.num_programs(0) - 1
    n_lat, per = synth.shape[:2]
    subs = 8 * per

    @pl.when(step == 0)
    def _():
        held[...] = jnp.zeros_like(held)
        dense[...] = jnp.zeros_like(dense)
        wide_held[...] = jnp.zeros_like(wide_held)
        narrow_held[...] = jnp.zeros_like(narrow_held)
        tails[...] = jnp.zeros_like(tails)

    @pl.when(step < last)
    def _():
        own = unpacked(packed_group(tail[:, 0].astype(f32), 0, subs), step, C - MAIN)
        real, imag = split_parts(jnp.concatenate([flat(synth[...]), own], axis=1), C)
        stacked = jnp.concatenate([real, imag], axis=0).astype(bf16)
        middle = state[0][:, 0, :] + dot(stacked, table[...], 0, 0)
        xhat, scale = norm_stats(middle)
        normed_low = (xhat * gain[...] + bias[...]).astype(bf16)
        pre_act = dot(up_turned[...], normed_low, 1, 0) + up_bias[...]
        share = 0.5 * (1.0 + lax.erf(pre_act * math.sqrt(0.5)))
        density = jnp.exp(-0.5 * pre_act * pre_act) * (1.0 / math.sqrt(2.0 * math.pi))
        hidden_low = (pre_act * share).astype(bf16)
        slope = share + pre_act * density
        out[0] = (middle + dot(down_turned[...], hidden_low, 1, 0) + down_bias[...])[:, None, :]
        grad = cotangent[0][:, 0, :]
        grad_low = grad.astype(bf16)
        pre_grad = dot(down[...], grad_low, 1, 0) * slope
        pre_low = pre_grad.astype(bf16)
        wide_held[...] += pre_grad
        dense[1, :C] += dot(grad_low, hidden_low, 1, 1)
        dense[0, :C] += dot(normed_low, pre_low, 1, 1)
        normed_grad = dot(up[...], pre_low, 1, 0)
        narrow_held[0] += normed_grad * xhat
        narrow_held[1] += normed_grad
        narrow_held[2] += grad
        scaled = normed_grad * gain[...]
        total = grad + scale * (
            scaled
            - jnp.mean(scaled, axis=0, keepdims=True)
            - xhat * jnp.mean(scaled * xhat, axis=0, keepdims=True)
        )
        middle_grad[0] = total
        held[:C] = total
        result = dot(table[...], held[...].astype(bf16), 1, 1)
        rows = result.shape[0] // 2
        joined = join_parts(result[:rows], result[rows:], C)
        synth_grad[...] = joined[:, :WHOLE].reshape(synth_grad.shape).astype(bf16)
        tails[...] += pltpu.roll(joined[:, WHOLE:], step, 1)

    @pl.when(step == last)
    def _():
        synth_grad[:, 0] = last_eight([tails[...]], n_lat, subs).astype(bf16)
        wide_sums[...] = jnp.sum(wide_held[...], axis=1, keepdims=True)
        narrow_sums[...] = jnp.sum(narrow_held[...], axis=2, keepdims=True)


def pixels(synth, state, cotangent, table, params, first, into, dense_rows):
    n_lat, subs = synth.shape[0], table.shape[0] // (2 * synth.shape[0])
    per = subs // 8
    count = (synth.shape[1] - 1) // per
    row = lambda r: jnp.minimum(r, count - 1)
    points = state.shape[3]
    hidden = params[2].shape[1]
    row_spec = pl.BlockSpec((1, C, 1, points), lambda r: (row(r) + first, 0, 0, 0))
    const = lambda array: pl.BlockSpec(array.shape, lambda r: (0,) * array.ndim)
    wave = lambda place: pl.BlockSpec((n_lat, per, 8, WHOLE), lambda r: (0, place(r), 0, 0))
    tail = pl.BlockSpec((n_lat, 1, 8, WHOLE), lambda r: (0, count * per, 0, 0))
    whole = lambda shape: pl.BlockSpec(shape, lambda r: (0,) * len(shape))
    shaped = lambda shape, kind=f32: jax.ShapeDtypeStruct(shape, kind)
    body, extra, alias = filled(pixel_body, into, 5 + len(params), 0, 1)
    return call(
        body,
        "feed_forward",
        2 * count * points * (6 * C * hidden + 2 * table.shape[0] * PADDED),
        count * (4 * C * points * 4 + 4 * n_lat * subs * LANES),
        grid=(count + 1,),
        in_specs=[wave(row), tail, row_spec, row_spec, const(table)] + [const(p) for p in params] + extra,
        input_output_aliases=alias,
        out_specs=[
            row_spec,
            pl.BlockSpec((1, C, points), lambda r: (row(r) + first, 0, 0)),
            wave(lambda r: r),
            whole((2, dense_rows, hidden)),
            whole((hidden, 1)),
            whole((3, C, 1)),
        ],
        out_shape=[
            shaped(state.shape),
            shaped((state.shape[0], C, points)),
            shaped(synth.shape, bf16),
            shaped((2, dense_rows, hidden)),
            shaped((hidden, 1)),
            shaped((3, C, 1)),
        ],
        scratch_shapes=[
            pltpu.VMEM((PADDED, points), f32),
            pltpu.VMEM((hidden, points), f32),
            pltpu.VMEM((3, C, points), f32),
            pltpu.VMEM((n_lat * subs, TILE), f32),
        ],
    )(synth, synth, state, cotangent, table, *params, *([] if into is None else into))


def final_body(wave, tail, state, middle_grad, table, gain, out, sums, held):
    step = pl.program_id(0)

    @pl.when(step == 0)
    def _():
        held[...] = jnp.zeros_like(held)

    own = unpacked(packed_group(tail[:, 0].astype(f32), 0, 8 * wave.shape[1]), step, C - MAIN)
    real, imag = split_parts(jnp.concatenate([flat(wave[...]), own], axis=1), C)
    stacked = jnp.concatenate([real, imag], axis=0).astype(bf16)
    spread_grad = dot(stacked, table[...], 0, 0)
    xhat, scale = norm_stats(state[0][:, 0, :])
    held[0] += spread_grad * xhat
    held[1] += spread_grad
    scaled = spread_grad * gain[...]
    out[0] = (
        middle_grad[0]
        + scale
        * (
            scaled
            - jnp.mean(scaled, axis=0, keepdims=True)
            - xhat * jnp.mean(scaled * xhat, axis=0, keepdims=True)
        )
    )[:, None, :]

    @pl.when(step == pl.num_programs(0) - 1)
    def _():
        sums[...] = jnp.sum(held[...], axis=2, keepdims=True)


def finish(wave, state, middle_grad, table, gain, first, into):
    n_lat, subs = wave.shape[0], table.shape[0] // (2 * wave.shape[0])
    per = subs // 8
    count = (wave.shape[1] - 1) // per
    points = state.shape[3]
    body, extra, alias = filled(final_body, into, 6, 0)
    return call(
        body,
        "first_norm_back",
        2 * count * points * table.shape[0] * PADDED,
        count * (3 * C * points * 4 + 2 * n_lat * subs * LANES),
        grid=(count,),
        in_specs=[
            pl.BlockSpec((n_lat, per, 8, WHOLE), lambda r: (0, r, 0, 0)),
            pl.BlockSpec((n_lat, 1, 8, WHOLE), lambda r: (0, count * per, 0, 0)),
            pl.BlockSpec((1, C, 1, points), lambda r: (r + first, 0, 0, 0)),
            pl.BlockSpec((1, C, points), lambda r: (r + first, 0, 0)),
            pl.BlockSpec(table.shape, lambda r: (0, 0)),
            pl.BlockSpec((C, 1), lambda r: (0, 0)),
        ]
        + extra,
        input_output_aliases=alias,
        out_specs=[
            pl.BlockSpec((1, C, 1, points), lambda r: (r + first, 0, 0, 0)),
            pl.BlockSpec((2, C, 1), lambda r: (0, 0, 0)),
        ],
        out_shape=[
            jax.ShapeDtypeStruct(state.shape, f32),
            jax.ShapeDtypeStruct((2, C, 1), f32),
        ],
        scratch_shapes=[pltpu.VMEM((2, C, points), f32)],
    )(wave, wave, state, middle_grad, table, gain, *([] if into is None else [into]))


def part_rows_body(paired, out):
    turned = paired[0][:, 0, :].T
    count = turned.shape[0] // 2
    for half in range(2):
        out[half] = turned[half * count : (half + 1) * count][:, None, :]


def part_rows(paired):
    pairs, points = paired.shape[0], paired.shape[3] // 2
    return call(
        part_rows_body,
        "part_rows",
        0,
        8 * paired.size,
        grid=(pairs,),
        in_specs=[pl.BlockSpec((1, C, 1, 2 * points), lambda r: (r, 0, 0, 0))],
        out_specs=pl.BlockSpec((2, points, 1, C), lambda r: (r, 0, 0, 0)),
        out_shape=jax.ShapeDtypeStruct((2 * pairs, points, 1, C), f32),
    )(paired)


def fourier_tables(orders, live, points, lon_count):
    phase = (orders * points % lon_count).astype(f32) * (2.0 * math.pi / lon_count)
    kept = live.astype(f32)
    cosine, sine = jnp.cos(phase) * kept, -jnp.sin(phase) * kept
    doubling = jnp.where(orders == 0, 1.0, 2.0).astype(f32)
    forward = jnp.concatenate([cosine / lon_count, sine / lon_count], axis=0)
    inverse = jnp.concatenate([cosine * doubling, sine * doubling], axis=0)
    return forward.astype(bf16), inverse.astype(bf16)


def order_rows(n_lat, pair_dev, subs):
    index = jnp.arange(n_lat * subs, dtype=jnp.int32)[:, None]
    return index // subs, index % subs


def fine_fourier(n_lat, pair_dev, subs, lon_count):
    device, sub = order_rows(n_lat, pair_dev, subs)
    kind = device * pair_dev + sub // 2
    member = sub % 2
    live = (sub < 2 * pair_dev) & jnp.where(
        member == 0, kind <= LB // 2, (kind >= 1) & (kind <= LB // 2 - 1)
    )
    orders = jnp.where(live, jnp.where(member == 0, kind, LB - kind), 0)
    points = jnp.arange(lon_count, dtype=jnp.int32)[None, :]
    return fourier_tables(orders, live, points, lon_count)


def coarse_fourier(n_lat, pair_dev, subs, lon_count):
    device, sub = order_rows(n_lat, pair_dev, subs)
    order = device * pair_dev + sub % pair_dev
    points = jnp.arange(2 * lon_count, dtype=jnp.int32)[None, :]
    live = (sub < 2 * pair_dev) & (order < LA) & (sub // pair_dev == points // lon_count)
    orders = jnp.where((sub < 2 * pair_dev) & (order < LA), order, 0)
    return fourier_tables(orders, live, points % lon_count, lon_count)


class Line:
    def __init__(self):
        self.before = self.last = None
        self.work, self.later = [], []
        self.aside = None

    def swap(self, values):
        self.step_aside()
        waits = self.work + ([] if self.last is None else [self.last])
        if waits:
            values = lax.optimization_barrier((values, waits))[0]
        self.before = self.last
        self.last = lax.all_to_all(values, "lat", split_axis=0, concat_axis=0, tiled=True)
        self.work, self.later = self.later, []
        return self.last

    def step_aside(self):
        if self.aside is not None:
            next(self.aside, None)

    def hold(self, values):
        if self.before is None:
            return values
        return lax.optimization_barrier((values, self.before))[0]

    def after_work(self, values):
        return lax.optimization_barrier((values, self.work))[0] if self.work else values

    def keep(self, values):
        self.work.append(values)
        return values

    def keep_later(self, values):
        self.later.append(values)
        return values


def partners(count, step):
    if count & (count - 1) == 0:
        return [(k, k ^ step) for k in range(count)], lambda rank: jnp.bitwise_xor(rank, step)
    return [(k, (k + step) % count) for k in range(count)], lambda rank: (rank + step) % count


def share_slots(members, n_chan, step):
    share = members.shape[0] // n_chan
    route, find = partners(n_chan, step)
    block = lax.dynamic_slice_in_dim(members, find(lax.axis_index("chan")) * share, share)
    return lax.ppermute(block, "chan", route) if step else block


def sum_over(values, sizes):
    for axis, size in sizes:
        if size & (size - 1):
            values = lax.psum(values, axis)
            continue
        step = 1
        while step < size:
            values = values + lax.ppermute(values, axis, partners(size, step)[0])
            step *= 2
    return values


def add_dense(array, n_lat, n_chan, line, result):
    shape, columns = array.shape, array.shape[2]
    sizes = {"chan": n_chan, "lat": n_lat}
    pairs = [("chan", 2**k) for k in range(n_chan.bit_length() - 1)] + [("lat", 1)]
    others = n_lat // 2
    held = array.reshape(-1, columns)
    odd = lambda axis, step: (lax.axis_index(axis) // step) % 2 == 1
    group = lax.axis_index("lat") // 2

    def halve(held, axis, step):
        low, high = jnp.split(line.hold(held), 2, axis=0)
        upper = odd(axis, step)
        other = lax.ppermute(jnp.where(upper, low, high), axis, partners(sizes[axis], step)[0])
        return line.keep(jnp.where(upper, high, low) + other)

    def double(held, axis, step):
        upper = odd(axis, step)
        other = lax.ppermute(line.hold(held), axis, partners(sizes[axis], step)[0])
        return line.keep_later(
            jnp.concatenate([jnp.where(upper, other, held), jnp.where(upper, held, other)], axis=0)
        )

    for axis, step in pairs[:-1]:
        held = halve(held, axis, step)
    yield
    yield
    held = halve(held, *pairs[-1])
    yield
    pieces = line.hold(held).reshape(others, -1, columns)
    own = lax.dynamic_index_in_dim(pieces, group, 0, False)
    for step in range(1, others):
        block = lax.dynamic_index_in_dim(pieces, jnp.bitwise_xor(group, step), 0, False)
        block = lax.ppermute(block.astype(bf16), "lat", partners(n_lat, 2 * step)[0])
        own = own + block.astype(f32)
    own = line.keep_later(own).astype(bf16)
    yield
    yield
    yield
    own = line.hold(own)
    held = jnp.zeros((others,) + own.shape, bf16)
    for step in range(others):
        block = lax.ppermute(own, "lat", partners(n_lat, 2 * step)[0]) if step else own
        held = lax.dynamic_update_index_in_dim(held, block, jnp.bitwise_xor(group, step), 0)
    held = line.keep_later(held).reshape(-1, columns)
    yield
    yield
    yield
    for axis, step in reversed(pairs[1:]):
        held = double(held, axis, step)
    yield
    held = double(held, *pairs[0])
    result.append(held.astype(f32).reshape(shape))


def shards(
    n_lat, n_chan, coarse_state, fine_state, coarse_noise, fine_noise, coarse_rows, fine_rows,
    pair_slots, first_gain, first_bias, mix_weight, second_gain, second_bias, up_weight, up_bias,
    down_weight, down_bias, coarse_cotangent, fine_cotangent,
):
    pair_dev = mix_weight.shape[0] // 2
    subs = -(-2 * pair_dev // 8) * 8
    lat_rank = lax.axis_index("lat")
    fine_dev, fine_points = fine_state.shape[1], fine_state.shape[2]
    coarse_dev, coarse_points = coarse_state.shape[1], coarse_state.shape[2]
    coarse_two = coarse_dev // 2
    column = lambda vector: vector[:, None]

    def fine_in(values):
        return values.transpose(1, 3, 0, 2)

    def coarse_in(values):
        paired = values[0].reshape(coarse_two, 2 * coarse_points, values.shape[3])
        return paired.transpose(0, 2, 1)[:, :, None, :]

    def fine_back(values):
        return values.transpose(2, 0, 3, 1)

    def coarse_back(values):
        return part_rows(values).transpose(2, 0, 1, 3)

    line = Line()
    dense_unit = 4 * n_lat * n_chan
    dense_rows = -(-(C + 3) // dense_unit) * dense_unit
    row_cuts = [(fine_dev + 1) // 2, fine_dev // 2] if fine_dev >= 8 else [fine_dev]
    row_starts = [sum(row_cuts[:k]) for k in range(len(row_cuts))]
    outer_cuts = [fine_dev // 4 + 1, fine_dev - fine_dev // 4 - 1] if fine_dev >= 8 else [fine_dev]
    outer_starts = [sum(outer_cuts[:k]) for k in range(len(outer_cuts))]
    n_chunks = 2 if pair_dev % 4 == 0 else 1
    chunk_pairs = pair_dev // n_chunks
    chunk_range = range(n_chunks)

    fine_x = fine_in(fine_state)
    fine_noise_in = fine_noise[0].transpose(0, 2, 1)
    fine_forward, fine_inverse = fine_fourier(n_lat, pair_dev, subs, fine_points)
    gain_one, bias_one = column(first_gain), column(first_bias)
    fine_four = []
    for start, count in zip(outer_starts, outer_cuts):
        made = spread(fine_x, fine_noise_in, gain_one, bias_one, fine_forward, n_lat, start, count)
        fine_four.append(line.swap(line.keep(made)))
    coarse_x = coarse_in(coarse_state)
    coarse_forward, coarse_inverse = coarse_fourier(n_lat, pair_dev, subs, coarse_points)
    coarse_noise_in = coarse_in(coarse_noise)[:, :, 0, :]
    coarse_four = line.swap(
        spread(coarse_x, coarse_noise_in, gain_one, bias_one, coarse_forward, n_lat, 0, coarse_two)
    )

    wide = -(-pair_dev // 8) * 8
    classes = lat_rank * pair_dev + jnp.arange(wide, dtype=jnp.int32)
    classes = jnp.where(jnp.arange(wide) < pair_dev, classes, LB).astype(jnp.int32)
    coarse_order = coarse_rows.reshape(-1, 2).T.reshape(-1)
    by_device = fine_rows.reshape(n_lat, fine_dev)
    in_order = lambda starts, cuts: jnp.concatenate(
        [by_device[:, a : a + c].reshape(-1) for a, c in zip(starts, cuts)]
    )
    unused, fine_quad = legendre_tables(
        in_order(outer_starts, outer_cuts), pair_slots, classes, LB, True
    )
    fine_plain, unused = legendre_tables(
        in_order(row_starts, row_cuts), pair_slots, classes, LB, True
    )
    coarse_plain, coarse_quad = legendre_tables(coarse_order, pair_slots, classes, LA, False)
    turn = lambda table, chunks=n_chunks: by_class(table, n_lat, pair_dev, chunks)

    def fine_tables(parts):
        first, near, far = [turn(part) for part in parts]
        table_a = jnp.concatenate([first, near], axis=1)
        return [table_a, far], [table_a.transpose(0, 2, 1), far.transpose(0, 2, 1)]

    fine_quad_in, fine_quad_out = fine_tables(fine_quad)
    fine_plain_in, fine_plain_out = fine_tables(fine_plain)
    coarse_quad_in = turn(coarse_quad[0], 1)
    coarse_plain_in = turn(coarse_plain[0], 1)
    coarse_quad_out = coarse_quad_in.transpose(0, 2, 1)
    coarse_plain_out = coarse_plain_in.transpose(0, 2, 1)
    local_pairs = lax.dynamic_slice_in_dim(pair_slots, lat_rank * pair_dev, pair_dev)
    weight = mix_weight.transpose(0, 1, 3, 2)

    fine_work = functools.partial(to_degrees_fine, pair_dev)
    fine_back_work = functools.partial(to_orders_fine, pair_dev)
    coarse_work = functools.partial(coarse_either_way, pair_dev)

    def spectral(coarse_chunk, fine_chunks, in_tables, out_tables, cuts, backward, aside):
        wide = (C if backward else WIDE) - MAIN
        fine_made = lane_call(
            fine_work, "rows_to_degrees", line.hold(fine_chunks), in_tables[1],
            [chunk_pairs] * n_chunks, subs, wide,
        )
        line.keep(fine_made)
        arrived, mixed, shared = [], [], []

        def mix_chunk(k):
            fine, coarse = line.hold((arrived[k], arrived_coarse))
            carried = mixed[-1][3] if mixed else jnp.zeros((n_lat * subs, TILE), f32)
            made = mix(
                fine, coarse, weight, local_pairs, subs, k * chunk_pairs // 2, k == n_chunks - 1,
                backward, mixed[-1][1] if mixed else None, carried,
            )
            mixed.append(line.keep(made))

        def share_next(count=1):
            members = joined_rows([made[2] for made in mixed])
            for step in range(len(shared), min(len(shared) + count, n_chan)):
                shared.append(line.keep_later(share_slots(line.hold(members), n_chan, step)))

        arrived.append(line.swap(fine_made[0]))
        coarse_made = lane_call(
            coarse_work, "rows_to_degrees", [line.hold(coarse_chunk)], [in_tables[0]],
            [pair_dev // 2], subs, wide,
        )[0]
        arrived_coarse = line.swap(line.keep(coarse_made))
        line.keep(out_tables)
        for k in range(1, n_chunks):
            arrived.append(line.swap(fine_made[k]))
            mix_chunk(k - 1)
        if n_chunks == 1:
            mix_chunk(0)
        fine_back = []
        for k in range(n_chunks - 1):
            fine_back.append(line.swap(mixed[k][0]))
            mix_chunk(k + 1)
        arrived_coarse = line.swap(mixed[-1][1])
        share_next(2)
        fine_back.append(line.swap(mixed[-1][0]))
        share_next()
        coarse_made = lane_call(
            coarse_work, "degrees_to_rows", [line.hold(arrived_coarse)], [out_tables[0]],
            [coarse_two], subs, C - MAIN,
        )[0]
        coarse_end = line.swap(line.keep(coarse_made))
        share_next(n_chan)
        fine_made = lane_call(
            fine_back_work, "degrees_to_rows", line.hold(fine_back), out_tables[1],
            cuts, subs, C - MAIN,
        )
        line.keep(fine_made)
        fine_end = [None] * len(cuts)
        order = list(range(len(cuts)))
        if backward:
            order.reverse()
        for k, place in enumerate(order):
            fine_end[place] = line.swap(fine_made[place])
            aside(k, coarse_end, fine_end, shared)
        return fine_end, shared

    params = [
        column(second_gain), column(second_bias), up_weight, up_weight.T, column(up_bias),
        down_weight, down_weight.T, column(down_bias),
    ]
    coarse_g, fine_g = coarse_in(coarse_cotangent), fine_in(fine_cotangent)
    coarse_made, fine_made = [], []

    def fine_pixels(k, synth):
        into = fine_made[-1][:2] if fine_made else None
        made = pixels(
            line.hold(synth), fine_x, fine_g, fine_inverse, params, row_starts[k], into,
            dense_rows,
        )
        fine_made.append(line.keep(made))

    def forward_aside(k, coarse_end, fine_end, shared):
        if k == 0:
            made = pixels(
                line.hold(coarse_end), coarse_x, coarse_g, coarse_inverse, params, 0, None,
                dense_rows,
            )
            coarse_made.extend(line.keep(made))
        else:
            fine_pixels(k - 1, fine_end[k - 1])

    fine_synth, values = spectral(
        coarse_four, fine_four, (coarse_quad_in, fine_quad_in), (coarse_plain_out, fine_plain_out),
        row_cuts, False, forward_aside,
    )
    if len(row_cuts) == 1:
        fine_pixels(0, fine_synth[0])
    fine_sgrad = []
    for k in range(len(row_cuts)):
        fine_sgrad.append(line.swap(fine_made[k][2]))
        if k + 1 < len(row_cuts):
            fine_pixels(k + 1, fine_synth[k + 1])
    axes = (("chan", n_chan), ("lat", n_lat))
    hidden = up_bias.shape[0]
    total = coarse_made[3:]
    for made in fine_made:
        total = [x + y for x, y in zip(total, made[3:])]
    narrow = jnp.concatenate([total[1][:, 0], total[2].reshape(-1)])
    narrow = jnp.pad(narrow, (0, 3 * hidden - narrow.shape[0])).reshape(1, 3, hidden)
    stacked = lax.dynamic_update_slice(total[0], narrow, (0, C, 0))
    dense = []
    line.aside = add_dense(line.hold(stacked), n_lat, n_chan, line, dense)
    line.step_aside()
    coarse_sgrad = line.swap(coarse_made[2])
    coarse_made[0] = line.keep(coarse_back(line.hold(coarse_made[0])))
    ends, mix_grads = [], []

    def finish_fine(place, wave):
        into = ends[-1][0] if len(ends) > 1 else None
        return finish(
            wave, fine_x, fine_made[-1][1], fine_forward, gain_one, outer_starts[place], into
        )

    def backward_aside(k, coarse_end, fine_end, shared):
        if k == 0:
            mix_grads.append(line.keep(mix_gradient(values, line.hold(shared))))
            made = finish(
                line.hold(coarse_end), coarse_x, coarse_made[1], coarse_forward, gain_one, 0, None
            )
            made = [coarse_back(made[0]), made[1]]
        else:
            made = finish_fine(len(outer_cuts) - k, line.hold(fine_end[-k]))
        ends.append(list(line.keep(made)))

    fine_fgrad, grads = spectral(
        coarse_sgrad, fine_sgrad, (coarse_plain_in, fine_plain_in), (coarse_quad_out, fine_quad_out),
        outer_cuts, True, backward_aside,
    )
    for unused in line.aside:
        pass
    up_grad, down_grad = line.keep((dense[0][0, :C], dense[0][1, :C]))
    narrow = dense[0][0, C : C + 3].reshape(-1)
    narrow_sums = narrow[hidden : hidden + 3 * C].reshape(3, C)
    last_wave = lax.optimization_barrier((fine_fgrad[0], line.work + line.later))[0]
    ends.append(finish_fine(0, last_wave))
    mix_grad = mix_grads[0].transpose(0, 2, 3, 1)
    sums = sum(end[1] for end in ends)
    first_sums = sum_over(sums[:, :, 0], axes)
    return (
        coarse_made[0],
        fine_back(fine_made[-1][0]),
        ends[0][0],
        fine_back(ends[-1][0]),
        first_sums[0],
        first_sums[1],
        mix_grad,
        narrow_sums[0],
        narrow_sums[1],
        up_grad,
        narrow[:hidden],
        down_grad.T,
        narrow_sums[2],
    )


def solution(mesh):
    pixel = P("chan", "lat", None, None)
    slots = P("lat", None, None, None)
    return jax.shard_map(
        functools.partial(shards, mesh.shape["lat"], mesh.shape["chan"]),
        mesh=mesh,
        in_specs=(pixel,) * 4 + (P(),) * 5 + (slots,) + (P(),) * 6 + (pixel,) * 2,
        out_specs=(pixel,) * 4 + (P(),) * 2 + (P(("lat", "chan"), None, None, None),) + (P(),) * 6,
        check_vma=False,
    )
```

```python
import functools
import math

import jax
import jax.numpy as jnp
from jax import lax
from jax.experimental import pallas as pl
from jax.experimental.pallas import tpu as pltpu
from jax.sharding import PartitionSpec as P

C = 641
NOISE = 8
WIDE = C + NOISE
LA = 90
LB = 180

TILE = 128
MAIN = C // TILE * TILE
HALF = TILE // 2
WHOLE = 2 * MAIN
LANES = WHOLE + TILE
PADDED = MAIN + TILE

epsilon = 1e-05
noise_scale = 1.0 / 262144.0
bf16 = jnp.bfloat16
f32 = jnp.float32
VMEM_LIMIT = 62 * 2**20


def call(body, name, flops, moved, **options):
    if "grid_spec" not in options:
        options.setdefault("scratch_shapes", [])
    return pl.pallas_call(
        body,
        compiler_params=pltpu.CompilerParams(vmem_limit_bytes=VMEM_LIMIT),
        cost_estimate=pl.CostEstimate(flops=int(flops), bytes_accessed=int(moved), transcendentals=0),
        name=name,
        **options,
    )


def filled(body, into, position, *outputs):
    if into is None:
        return body, [], {}
    count = len(outputs)

    def skipping(*refs):
        body(*refs[:position], *refs[position + count :])

    alias = {position + k: output for k, output in enumerate(outputs)}
    return skipping, [pl.BlockSpec(memory_space=pl.ANY)] * count, alias


def dot(left, right, left_dim, right_dim):
    return lax.dot_general(
        left, right, (((left_dim,), (right_dim,)), ((), ())), preferred_element_type=f32
    )


def join_parts(real, imag, count):
    tail = real[:, MAIN:] + pltpu.roll(imag[:, MAIN:], HALF, 1)
    return jnp.concatenate([real[:, :MAIN], imag[:, :MAIN], tail], axis=1)


def join_narrow(real, imag):
    lane = lax.broadcasted_iota(jnp.int32, (real.shape[0], TILE), 1)
    tail = jnp.where(
        lane == 0, real[:, MAIN:C], jnp.where(lane == HALF, imag[:, MAIN:C], 0.0)
    )
    return jnp.concatenate([real[:, :MAIN], imag[:, :MAIN], tail], axis=1)


def split_parts(joined, count):
    tail = joined[:, 2 * MAIN :]
    real = jnp.concatenate([joined[:, :MAIN], tail], axis=1)[:, :count]
    imag = jnp.concatenate(
        [joined[:, MAIN : 2 * MAIN], pltpu.roll(tail, HALF, 1)], axis=1
    )[:, :count]
    return real, imag


def packing(rows, width):
    share = HALF // width
    return share, -(-rows // share)


def eights(rows, subs):
    return rows * (subs // 8) + 1


def packed_group(tail, group, subs):
    count = subs // 8
    tiles = [tail[:, :, (group * count + k) * TILE :][:, :, :TILE] for k in range(count)]
    return jnp.stack(tiles, axis=1).reshape(-1, TILE)


def unpacked(group_tile, place, width):
    turned = pltpu.roll(group_tile, (TILE - place * width) % TILE, 1)
    lane = lax.broadcasted_iota(jnp.int32, turned.shape, 1)
    return jnp.where(lane % HALF < width, turned, 0.0)


def last_eight(groups, n_lat, subs):
    count = subs // 8
    tiles = []
    for group in groups:
        split = group.reshape(n_lat, count, 8, TILE)
        tiles += [split[:, k] for k in range(count)]
    blank = jnp.zeros((n_lat, 8, TILE), f32)
    return jnp.concatenate(tiles + [blank] * (WHOLE // TILE - len(tiles)), axis=2)


def flat(block):
    return block.astype(f32).reshape(-1, block.shape[-1])


def joined_rows(parts):
    return parts[0] if len(parts) == 1 else jnp.concatenate(parts, axis=0)


def norm_stats(values):
    centered = values - jnp.mean(values, axis=0, keepdims=True)
    variance = jnp.mean(centered * centered, axis=0, keepdims=True)
    scale = lax.rsqrt(variance + epsilon)
    return centered * scale, scale


def spread_body(state, noise, gain, bias, table, out, held, tails):
    step, last = pl.program_id(0), pl.num_programs(0) - 1
    n_lat, count, unused, lanes = out.shape
    width = WIDE - MAIN
    share = HALF // width

    @pl.when(step == 0)
    def _():
        held[...] = jnp.zeros_like(held)
        tails[...] = jnp.zeros_like(tails)

    @pl.when(step < last)
    def _():
        xhat, unused = norm_stats(state[0][:, 0, :])
        held[:C] = xhat * gain[...] + bias[...]
        held[C:WIDE] = ((noise[0].astype(f32) + 0.5) * noise_scale - 0.5) * math.sqrt(12.0)
        result = dot(table[...], held[...].astype(bf16), 1, 1)
        rows = result.shape[0] // 2
        joined = join_parts(result[:rows], result[rows:], WIDE)
        out[...] = joined[:, :WHOLE].reshape(out.shape).astype(bf16)
        tails[step // share] += pltpu.roll(joined[:, WHOLE:], step % share * width, 1)

    @pl.when(step == last)
    def _():
        groups = [tails[k] for k in range(tails.shape[0])]
        out[:, 0] = last_eight(groups, n_lat, 8 * count).astype(bf16)


def spread(state, noise, gain, bias, table, n_lat, first, count):
    points = state.shape[3]
    subs = table.shape[0] // (2 * n_lat)
    const = lambda r: (0, 0)
    row = lambda r: jnp.minimum(r, count - 1) + first
    return call(
        spread_body,
        "norm_and_dft",
        2 * count * table.shape[0] * points * PADDED,
        count * (C * points * 4 + n_lat * subs * LANES * 2),
        grid=(count + 1,),
        in_specs=[
            pl.BlockSpec((1, C, 1, points), lambda r: (row(r), 0, 0, 0)),
            pl.BlockSpec((1, NOISE, points), lambda r: (row(r), 0, 0)),
            pl.BlockSpec((C, 1), const),
            pl.BlockSpec((C, 1), const),
            pl.BlockSpec(table.shape, const),
        ],
        out_specs=pl.BlockSpec((n_lat, subs // 8, 8, WHOLE), lambda r: (0, r, 0, 0)),
        out_shape=jax.ShapeDtypeStruct((n_lat, eights(count, subs), 8, WHOLE), bf16),
        scratch_shapes=[
            pltpu.VMEM((PADDED, points), f32),
            pltpu.VMEM((packing(count, WIDE - MAIN)[1], n_lat * subs, TILE), f32),
        ],
    )(state, noise, gain, bias, table)


def legendre_body(total, pairs, order_a, order_b, diag_a, diag_b, cosine, classes, *refs):
    two = order_b is not None
    outs, (held_a, held_b) = refs[: 3 if two else 1], (refs[3:] if two else (refs[1], None))

    def advance(degree, order, diagonal, previous, earlier):
        real = degree.astype(f32)
        grow = jnp.sqrt(
            (4.0 * real * real - 1.0) / jnp.maximum(real * real - order * order, 1.0)
        )
        damp = jnp.sqrt(
            jnp.maximum((real - 1.0) * (real - 1.0) - order * order, 0.0)
            / jnp.maximum(4.0 * (real - 1.0) * (real - 1.0) - 1.0, 1.0)
        )
        grown = grow * (cosine[...] * previous - damp * earlier)
        return jnp.where(real == order, diagonal, jnp.where(real > order, grown, 0.0))

    def step(degree, carry):
        now_a = advance(degree, order_a[...], diag_a[...], carry[0], carry[1])
        held_a[degree] = now_a
        if not two:
            return (now_a, carry[0])
        now_b = advance(degree, order_b[...], diag_b[...], carry[2], carry[3])
        held_b[degree] = now_b
        return (now_a, carry[0], now_b, carry[2])

    zero = diag_a[...] * 0.0
    lax.fori_loop(0, total, step, (zero,) * (4 if two else 2))

    def pick(slot, unused):
        pair = pairs[slot]
        safe = jnp.maximum(pair, 0)
        live = jnp.where(pair >= 0, 1.0, 0.0)
        low = classes[...] <= pair
        near = held_a[safe] * live
        if two:
            far = held_a[LB - 1 - safe] * live
            outs[0][slot] = jnp.where(low, near, far)
            outs[1][slot] = jnp.where(low, far, 0.0)
            outs[2][slot] = jnp.where(low, 0.0, held_b[LB - 1 - safe] * live)
        else:
            outs[0][slot] = jnp.where(low, near, 0.0)
        return unused

    lax.fori_loop(0, pairs.shape[0], pick, 0)


def diagonal_values(orders, live, sines):
    order_real = orders.astype(f32)[:, None]
    log_start = 0.5 * jnp.log((2.0 * order_real + 1.0) / (4.0 * math.pi))
    log_start = log_start + 0.5 * (
        lax.lgamma(2.0 * order_real + 1.0)
        - 2.0 * order_real * math.log(2.0)
        - 2.0 * lax.lgamma(order_real + 1.0)
    )
    diagonal = jnp.exp(log_start + order_real * jnp.log(sines)[None, :])
    return jnp.where(live[:, None], diagonal, 0.0)


def legendre_tables(row_table, pair_slots, classes, total, two):
    slots, rows, wide = pair_slots.shape[0], row_table.shape[0], classes.shape[0]
    occupied = (row_table >= 0).astype(f32)
    colatitude = math.pi * (jnp.maximum(row_table, 0).astype(f32) + 0.5) / total
    sines = jnp.sin(colatitude)
    cosine = jnp.broadcast_to(jnp.cos(colatitude)[None, :], (wide, rows))
    spread_out = lambda v: jnp.broadcast_to(v.astype(f32)[:, None], (wide, rows))
    top = LB // 2 if two else LA - 1
    order_a = jnp.where(classes <= top, classes, 0)
    diag_a = diagonal_values(order_a, classes <= top, sines)
    live_b = (classes >= 1) & (classes <= LB // 2 - 1)
    order_b = jnp.where(live_b, LB - classes, 0)
    diag_b = diagonal_values(order_b, live_b, sines)
    class_wide = jnp.broadcast_to(classes[:, None], (wide, rows))
    if two:
        arrays = [spread_out(order_a), spread_out(order_b), diag_a, diag_b, cosine, class_wide]
        body = functools.partial(legendre_body, total)
    else:
        arrays = [spread_out(order_a), diag_a, cosine, class_wide]

        def body(pairs, order, diagonal, cosines, class_ref, *refs):
            legendre_body(total, pairs, order, None, diagonal, None, cosines, class_ref, *refs)

    shape = jax.ShapeDtypeStruct((slots, wide, rows), f32)
    count = 3 if two else 1
    tables = call(
        body,
        "legendre_tables",
        total * wide * rows * 40,
        count * slots * wide * rows * 4,
        in_specs=[pl.BlockSpec(memory_space=pltpu.SMEM)]
        + [pl.BlockSpec(memory_space=pltpu.VMEM)] * len(arrays),
        out_specs=[pl.BlockSpec(memory_space=pltpu.VMEM)] * count,
        out_shape=[shape] * count,
        scratch_shapes=[pltpu.VMEM((total, wide, rows), f32)] * (2 if two else 1),
    )(pair_slots, *arrays)
    plain = [table * occupied for table in tables]
    weight = sines * occupied * (2.0 * math.pi * math.pi / total)
    return plain, [table * weight for table in plain]


def by_class(table, n_lat, pair_dev, n_chunks):
    split = table.reshape(n_lat, n_chunks, pair_dev // (2 * n_chunks), 2, *table.shape[1:])
    moved = split.transpose(4, 3, 1, 0, 2, 5)[:pair_dev]
    return moved.reshape(pair_dev, n_lat * pair_dev, table.shape[2]).astype(bf16)


def to_degrees_fine(pair_dev, subs, tables, held, results):
    table_a, table_b = tables
    half = sum(result.shape[0] for result in results) // (2 * subs)

    def order_rows(sub):
        parts = [keep[pl.ds(sub, keep.shape[0] // subs, stride=subs), :] for keep in held]
        return joined_rows(parts).astype(bf16)

    for index in range(pair_dev):
        from_a = dot(table_a[index], order_rows(2 * index), 1, 0)
        from_b = dot(table_b[index], order_rows(2 * index + 1), 1, 0)
        first, second = from_a[: 2 * half], from_a[2 * half :] + from_b
        begin = 0
        for odd in range(2):
            start = odd * subs + index
            for result in results:
                count = result.shape[0] // (2 * subs)
                rows = slice(begin, begin + count)
                begin += count
                result[pl.ds(start + (1 - odd) * pair_dev, count, stride=2 * subs), :] = first[rows]
                result[pl.ds(start + odd * pair_dev, count, stride=2 * subs), :] = second[rows]


def to_orders_fine(pair_dev, subs, tables, held, results):
    table_a, table_b = tables
    for index in range(pair_dev):
        first, second = [], []
        for odd in range(2):
            start = odd * subs + index
            for keep in held:
                count = keep.shape[0] // (2 * subs)
                first.append(keep[pl.ds(start + (1 - odd) * pair_dev, count, stride=2 * subs), :])
                second.append(keep[pl.ds(start + odd * pair_dev, count, stride=2 * subs), :])
        second = joined_rows(second)
        both = joined_rows(first + [second]).astype(bf16)
        made = (dot(table_a[index], both, 1, 0), dot(table_b[index], second.astype(bf16), 1, 0))
        for member in range(2):
            begin = 0
            for result in results:
                rows = result.shape[0] // subs
                result[pl.ds(2 * index + member, rows, stride=subs), :] = made[member][
                    begin : begin + rows
                ]
                begin += rows


def coarse_either_way(pair_dev, subs, tables, held, results):
    (keep,), (result,), (table,) = held, results, tables
    before, after = keep.shape[0] // subs, result.shape[0] // subs
    for index in range(pair_dev):
        taken = joined_rows(
            [keep[pl.ds(odd * pair_dev + index, before, stride=subs), :] for odd in range(2)]
        ).astype(bf16)
        made = dot(table[index], taken, 1, 0)
        for odd in range(2):
            result[pl.ds(odd * pair_dev + index, after, stride=subs), :] = made[
                odd * after : (odd + 1) * after
            ]


def lane_body(work, subs, width, n_in, n_tables, n_out, *refs):
    cuts = [n_in, n_in, n_tables, n_out, n_in, n_out, n_out]
    mains, tails, tables, outs, held, results, packed = [
        refs[sum(cuts[:k]) : sum(cuts[: k + 1])] for k in range(len(cuts))
    ]
    step = pl.program_id(0)
    n_lat, per = mains[0].shape[0], subs // 8

    @pl.when(step == 0)
    def _():
        for tail, keep in zip(tails, held):
            rows = keep.shape[0] // (n_lat * subs)
            share, groups = packing(rows, width)
            whole = tail[:, 0].astype(f32)
            for group in range(groups):
                tile = packed_group(whole, group, subs)
                for row in range(group * share, min(rows, (group + 1) * share)):
                    own = unpacked(tile, row % share, width)
                    for device in range(n_lat):
                        keep[pl.ds((device * rows + row) * subs, subs), :] = own[
                            device * subs : (device + 1) * subs
                        ]
        for result in results:
            result[...] = jnp.zeros_like(result)

    @pl.when(step > 0)
    def _():
        for main, keep in zip(mains, held):
            keep[...] = flat(main[:, : main.shape[1] - 1])

    work(subs, tables, held, results)

    @pl.when(step == 0)
    def _():
        for result, pack in zip(results, packed):
            rows = result.shape[0] // (n_lat * subs)
            share, groups = packing(rows, width)
            pack[...] = jnp.zeros_like(pack)
            made = result[...].reshape(n_lat, rows, subs, TILE)
            for group in range(groups):
                total = jnp.zeros((n_lat * subs, TILE), f32)
                for row in range(group * share, min(rows, (group + 1) * share)):
                    own = made[:, row].reshape(n_lat * subs, TILE)
                    total = total + pltpu.roll(own, row % share * width, 1)
                split = total.reshape(n_lat, per, 8, TILE)
                for k in range(per):
                    pack[group * per + k] = split[:, k]

    @pl.when(step > 0)
    def _():
        for out, result, pack in zip(outs, results, packed):
            count = out.shape[1] - 1
            out[:, :count] = result[...].reshape(n_lat, count, 8, TILE).astype(bf16)
            out[:, count] = pack[step - 1].astype(bf16)


def lane_call(work, name, inputs, tables, rows_out, subs, width):
    n_lat = inputs[0].shape[0]
    outs = [(n_lat, eights(rows, subs), 8, WHOLE) for rows in rows_out]
    rows_in = [(a.shape[1] - 1) * 8 // subs for a in inputs]
    tiled = lambda shape: pl.BlockSpec(
        tuple(shape[:3]) + (TILE,), lambda t: (0, 0, 0, jnp.maximum(t - 1, 0))
    )
    tail = lambda shape: pl.BlockSpec(
        (shape[0], 1, 8, WHOLE), lambda t, last=shape[1] - 1: (0, last, 0, 0)
    )
    whole = lambda shape: pl.BlockSpec(shape, lambda t: (0, 0, 0))
    held = lambda rows: pltpu.VMEM((n_lat * rows * subs, TILE), f32)
    moved = sum(2 * math.prod(s) for s in [a.shape for a in inputs] + outs)
    flops = sum(2 * math.prod(t.shape) for t in tables) * LANES
    return call(
        functools.partial(lane_body, work, subs, width, len(inputs), len(tables), len(outs)),
        name,
        flops,
        moved,
        grid=(WHOLE // TILE + 1,),
        in_specs=[tiled(a.shape) for a in inputs]
        + [tail(a.shape) for a in inputs]
        + [whole(t.shape) for t in tables],
        out_specs=[tiled(shape) for shape in outs],
        out_shape=[jax.ShapeDtypeStruct(shape, bf16) for shape in outs],
        scratch_shapes=[held(rows) for rows in rows_in]
        + [held(rows) for rows in rows_out]
        + [pltpu.VMEM((WHOLE // TILE, n_lat, 8, TILE), f32) for unused in outs],
    )(*inputs, *inputs, *tables)


def mix_body(
    pair_dev, subs, first, ends, backward, pairs, fine, fine_tail, coarse, coarse_tail, weight,
    carried, fine_out, coarse_out, members, carry, fine_held, coarse_held,
):
    step, last = pl.program_id(0), pl.num_programs(0) - 1
    n_lat, per = fine.shape[0], subs // 8
    rows = n_lat * subs
    width = (C if backward else WIDE) - MAIN
    count = C if backward else WIDE

    @pl.when(step == 0)
    def _():
        fine_held[...] = jnp.zeros_like(fine_held)
        coarse_held[...] = carried[...]

    def apply(values, slot):
        real, imag = split_parts(values, count)
        stacked = jnp.concatenate([real, imag], axis=0).astype(bf16)
        by_real = dot(stacked, weight[slot, 0], 1, 0 if backward else 1)
        by_imag = dot(stacked, weight[slot, 1], 1, 0 if backward else 1)
        if backward:
            out_real = by_real[:rows] + by_imag[rows:]
            out_imag = by_real[rows:] - by_imag[:rows]
        else:
            out_real = by_real[:rows] - by_imag[rows:]
            out_imag = by_imag[:rows] + by_real[rows:]
        return join_narrow(out_real[:, :C], out_imag[:, :C])

    @pl.when(step < last)
    def _():
        row = lax.broadcasted_iota(jnp.int32, (rows, 1), 0)
        sub = row % subs
        group = sub // pair_dev
        order_class = row // subs * pair_dev + sub % pair_dev
        share = HALF // width

        def packed_at(tail, place):
            whole = tail[:, 0].astype(f32)
            groups = packing(WHOLE // TILE // per * share, width)[1]
            tile = packed_group(whole, 0, subs)
            for index in range(1, groups):
                tile = jnp.where(place // share == index, packed_group(whole, index, subs), tile)
            return unpacked(tile, place % share, width)

        coarse_rows = jnp.concatenate(
            [flat(coarse[...]), packed_at(coarse_tail, step + first)], axis=1
        )
        coarse_made = jnp.zeros((rows, LANES), f32)
        for odd in range(2):
            pair = pairs[2 * (step + first) + odd]
            own = group == odd
            low = order_class <= pair
            fine_rows = jnp.concatenate(
                [
                    flat(fine[:, odd * per : (odd + 1) * per]),
                    packed_at(fine_tail, 2 * step + odd),
                ],
                axis=1,
            )
            lower = jnp.where(own, coarse_rows, jnp.where(low, fine_rows, 0.0))
            upper = jnp.where(own | ~low, fine_rows, 0.0)
            members[2 * odd] = lower.reshape(n_lat, subs, LANES).astype(bf16)
            members[2 * odd + 1] = upper.reshape(n_lat, subs, LANES).astype(bf16)
            from_lower = apply(lower, 2 * odd)
            from_upper = apply(upper, 2 * odd + 1)
            made = jnp.where(own, from_upper, from_lower + from_upper)
            fine_out[:, odd * per : (odd + 1) * per] = (
                made[:, :WHOLE].reshape(n_lat, per, 8, WHOLE).astype(bf16)
            )
            fine_held[...] += pltpu.roll(made[:, WHOLE:], 2 * step + odd, 1)
            coarse_made = jnp.where(own, from_lower, coarse_made)
        coarse_out[...] = coarse_made[:, :WHOLE].reshape(coarse_out.shape).astype(bf16)
        coarse_held[...] += pltpu.roll(coarse_made[:, WHOLE:], step + first, 1)

    @pl.when(step == last)
    def _():
        fine_out[:, 0] = last_eight([fine_held[...]], n_lat, subs).astype(bf16)
        carry[...] = coarse_held[...]
        if ends:
            coarse_out[:, 0] = last_eight([coarse_held[...]], n_lat, subs).astype(bf16)


def mix(fine, coarse, weight, local_pairs, subs, first, ends, backward, into, carried):
    n_lat, per = fine.shape[0], subs // 8
    count = (fine.shape[1] - 1) // per
    pair_dev = weight.shape[0] // 2
    turns = count // 2
    inside = lambda k: jnp.minimum(k, turns - 1)
    rows = lambda height, place: pl.BlockSpec(
        (n_lat, height, 8, WHOLE), lambda k, pairs: (0, place(k), 0, 0)
    )
    tail = lambda array: rows(1, lambda k: array.shape[1] - 1)
    whole = pl.BlockSpec((n_lat * subs, TILE), lambda k, pairs: (0, 0))
    body, extra, alias = filled(
        functools.partial(mix_body, pair_dev, subs, first, ends, backward), into, 7, 1
    )
    coarse_place = (lambda k: k + first) if ends else (lambda k: inside(k) + first)
    wave = lambda array: jax.ShapeDtypeStruct(array.shape, bf16)
    return call(
        body,
        "mix_back" if backward else "mix",
        2 * count * n_lat * subs * 8 * PADDED * PADDED,
        2 * weight.size * count // pair_dev + 12 * fine.size,
        grid_spec=pltpu.PrefetchScalarGridSpec(
            num_scalar_prefetch=1,
            grid=(turns + 1,),
            in_specs=[
                rows(2 * per, inside),
                tail(fine),
                rows(per, lambda k: inside(k) + first),
                tail(coarse),
                pl.BlockSpec(
                    (4,) + weight.shape[1:], lambda k, pairs: (inside(k) + first, 0, 0, 0)
                ),
                whole,
            ]
            + extra,
            out_specs=[
                rows(2 * per, lambda k: k),
                rows(per, coarse_place),
                pl.BlockSpec((4, n_lat, subs, LANES), lambda k, pairs: (inside(k), 0, 0, 0)),
                whole,
            ],
            scratch_shapes=[pltpu.VMEM((n_lat * subs, TILE), f32)] * 2,
        ),
        out_shape=[
            wave(fine),
            wave(coarse),
            jax.ShapeDtypeStruct((2 * count, n_lat, subs, LANES), bf16),
            jax.ShapeDtypeStruct((n_lat * subs, TILE), f32),
        ],
        input_output_aliases=alias,
    )(local_pairs, fine, fine, coarse, coarse, weight, carried, *([] if into is None else [into]))


def mix_grad_body(n_parts, *refs):
    values, grads, out = refs[:n_parts], refs[n_parts : 2 * n_parts], refs[2 * n_parts]
    gather = lambda parts: jnp.concatenate([flat(part[0]) for part in parts], axis=0)
    value_real, value_imag = [v.astype(bf16) for v in split_parts(gather(values), WIDE)]
    grad_real, grad_imag = [v.astype(bf16) for v in split_parts(gather(grads), C)]
    out[0, :, 0, :] = dot(grad_real, value_real, 0, 0) + dot(grad_imag, value_imag, 0, 0)
    out[0, :, 1, :] = dot(grad_imag, value_real, 0, 0) - dot(grad_real, value_imag, 0, 0)


def mix_gradient(values, grads):
    slots = values[0].shape[0]
    shape = values[0].shape[1:]
    spec = pl.BlockSpec((1,) + shape, lambda k: (k, 0, 0, 0))
    rows = len(values) * math.prod(shape[:2])
    return call(
        functools.partial(mix_grad_body, len(values)),
        "mix_gradient",
        8 * slots * rows * C * WIDE,
        slots * (4 * rows * LANES + 8 * C * WIDE),
        grid=(slots,),
        in_specs=[spec] * (2 * len(values)),
        out_specs=pl.BlockSpec((1, C, 2, WIDE), lambda k: (k, 0, 0, 0)),
        out_shape=jax.ShapeDtypeStruct((slots, C, 2, WIDE), f32),
    )(*values, *grads)


def pixel_body(
    synth, tail, state, cotangent, table, gain, bias, up, up_turned, up_bias, down, down_turned,
    down_bias, out, middle_grad, synth_grad, dense, wide_sums, narrow_sums, held,
    wide_held, narrow_held, tails,
):
    step, last = pl.program_id(0), pl.num_programs(0) - 1
    n_lat, per = synth.shape[:2]
    subs = 8 * per

    @pl.when(step == 0)
    def _():
        held[...] = jnp.zeros_like(held)
        dense[...] = jnp.zeros_like(dense)
        wide_held[...] = jnp.zeros_like(wide_held)
        narrow_held[...] = jnp.zeros_like(narrow_held)
        tails[...] = jnp.zeros_like(tails)

    @pl.when(step < last)
    def _():
        own = unpacked(packed_group(tail[:, 0].astype(f32), 0, subs), step, C - MAIN)
        real, imag = split_parts(jnp.concatenate([flat(synth[...]), own], axis=1), C)
        stacked = jnp.concatenate([real, imag], axis=0).astype(bf16)
        middle = state[0][:, 0, :] + dot(stacked, table[...], 0, 0)
        xhat, scale = norm_stats(middle)
        normed_low = (xhat * gain[...] + bias[...]).astype(bf16)
        pre_act = dot(up_turned[...], normed_low, 1, 0) + up_bias[...]
        share = 0.5 * (1.0 + lax.erf(pre_act * math.sqrt(0.5)))
        density = jnp.exp(-0.5 * pre_act * pre_act) * (1.0 / math.sqrt(2.0 * math.pi))
        hidden_low = (pre_act * share).astype(bf16)
        slope = share + pre_act * density
        out[0] = (middle + dot(down_turned[...], hidden_low, 1, 0) + down_bias[...])[:, None, :]
        grad = cotangent[0][:, 0, :]
        grad_low = grad.astype(bf16)
        pre_grad = dot(down[...], grad_low, 1, 0) * slope
        pre_low = pre_grad.astype(bf16)
        wide_held[...] += pre_grad
        dense[1, :C] += dot(grad_low, hidden_low, 1, 1)
        dense[0, :C] += dot(normed_low, pre_low, 1, 1)
        normed_grad = dot(up[...], pre_low, 1, 0)
        narrow_held[0] += normed_grad * xhat
        narrow_held[1] += normed_grad
        narrow_held[2] += grad
        scaled = normed_grad * gain[...]
        total = grad + scale * (
            scaled
            - jnp.mean(scaled, axis=0, keepdims=True)
            - xhat * jnp.mean(scaled * xhat, axis=0, keepdims=True)
        )
        middle_grad[0] = total
        held[:C] = total
        result = dot(table[...], held[...].astype(bf16), 1, 1)
        rows = result.shape[0] // 2
        joined = join_parts(result[:rows], result[rows:], C)
        synth_grad[...] = joined[:, :WHOLE].reshape(synth_grad.shape).astype(bf16)
        tails[...] += pltpu.roll(joined[:, WHOLE:], step, 1)

    @pl.when(step == last)
    def _():
        synth_grad[:, 0] = last_eight([tails[...]], n_lat, subs).astype(bf16)
        wide_sums[...] = jnp.sum(wide_held[...], axis=1, keepdims=True)
        narrow_sums[...] = jnp.sum(narrow_held[...], axis=2, keepdims=True)


def pixels(synth, state, cotangent, table, params, first, into, dense_rows):
    n_lat, subs = synth.shape[0], table.shape[0] // (2 * synth.shape[0])
    per = subs // 8
    count = (synth.shape[1] - 1) // per
    row = lambda r: jnp.minimum(r, count - 1)
    points = state.shape[3]
    hidden = params[2].shape[1]
    row_spec = pl.BlockSpec((1, C, 1, points), lambda r: (row(r) + first, 0, 0, 0))
    const = lambda array: pl.BlockSpec(array.shape, lambda r: (0,) * array.ndim)
    wave = lambda place: pl.BlockSpec((n_lat, per, 8, WHOLE), lambda r: (0, place(r), 0, 0))
    tail = pl.BlockSpec((n_lat, 1, 8, WHOLE), lambda r: (0, count * per, 0, 0))
    whole = lambda shape: pl.BlockSpec(shape, lambda r: (0,) * len(shape))
    shaped = lambda shape, kind=f32: jax.ShapeDtypeStruct(shape, kind)
    body, extra, alias = filled(pixel_body, into, 5 + len(params), 0, 1)
    return call(
        body,
        "feed_forward",
        2 * count * points * (6 * C * hidden + 2 * table.shape[0] * PADDED),
        count * (4 * C * points * 4 + 4 * n_lat * subs * LANES),
        grid=(count + 1,),
        in_specs=[wave(row), tail, row_spec, row_spec, const(table)] + [const(p) for p in params] + extra,
        input_output_aliases=alias,
        out_specs=[
            row_spec,
            pl.BlockSpec((1, C, points), lambda r: (row(r) + first, 0, 0)),
            wave(lambda r: r),
            whole((2, dense_rows, hidden)),
            whole((hidden, 1)),
            whole((3, C, 1)),
        ],
        out_shape=[
            shaped(state.shape),
            shaped((state.shape[0], C, points)),
            shaped(synth.shape, bf16),
            shaped((2, dense_rows, hidden)),
            shaped((hidden, 1)),
            shaped((3, C, 1)),
        ],
        scratch_shapes=[
            pltpu.VMEM((PADDED, points), f32),
            pltpu.VMEM((hidden, points), f32),
            pltpu.VMEM((3, C, points), f32),
            pltpu.VMEM((n_lat * subs, TILE), f32),
        ],
    )(synth, synth, state, cotangent, table, *params, *([] if into is None else into))


def final_body(wave, tail, state, middle_grad, table, gain, out, sums, held):
    step = pl.program_id(0)

    @pl.when(step == 0)
    def _():
        held[...] = jnp.zeros_like(held)

    own = unpacked(packed_group(tail[:, 0].astype(f32), 0, 8 * wave.shape[1]), step, C - MAIN)
    real, imag = split_parts(jnp.concatenate([flat(wave[...]), own], axis=1), C)
    stacked = jnp.concatenate([real, imag], axis=0).astype(bf16)
    spread_grad = dot(stacked, table[...], 0, 0)
    xhat, scale = norm_stats(state[0][:, 0, :])
    held[0] += spread_grad * xhat
    held[1] += spread_grad
    scaled = spread_grad * gain[...]
    out[0] = (
        middle_grad[0]
        + scale
        * (
            scaled
            - jnp.mean(scaled, axis=0, keepdims=True)
            - xhat * jnp.mean(scaled * xhat, axis=0, keepdims=True)
        )
    )[:, None, :]

    @pl.when(step == pl.num_programs(0) - 1)
    def _():
        sums[...] = jnp.sum(held[...], axis=2, keepdims=True)


def finish(wave, state, middle_grad, table, gain, first, into):
    n_lat, subs = wave.shape[0], table.shape[0] // (2 * wave.shape[0])
    per = subs // 8
    count = (wave.shape[1] - 1) // per
    points = state.shape[3]
    body, extra, alias = filled(final_body, into, 6, 0)
    return call(
        body,
        "first_norm_back",
        2 * count * points * table.shape[0] * PADDED,
        count * (3 * C * points * 4 + 2 * n_lat * subs * LANES),
        grid=(count,),
        in_specs=[
            pl.BlockSpec((n_lat, per, 8, WHOLE), lambda r: (0, r, 0, 0)),
            pl.BlockSpec((n_lat, 1, 8, WHOLE), lambda r: (0, count * per, 0, 0)),
            pl.BlockSpec((1, C, 1, points), lambda r: (r + first, 0, 0, 0)),
            pl.BlockSpec((1, C, points), lambda r: (r + first, 0, 0)),
            pl.BlockSpec(table.shape, lambda r: (0, 0)),
            pl.BlockSpec((C, 1), lambda r: (0, 0)),
        ]
        + extra,
        input_output_aliases=alias,
        out_specs=[
            pl.BlockSpec((1, C, 1, points), lambda r: (r + first, 0, 0, 0)),
            pl.BlockSpec((2, C, 1), lambda r: (0, 0, 0)),
        ],
        out_shape=[
            jax.ShapeDtypeStruct(state.shape, f32),
            jax.ShapeDtypeStruct((2, C, 1), f32),
        ],
        scratch_shapes=[pltpu.VMEM((2, C, points), f32)],
    )(wave, wave, state, middle_grad, table, gain, *([] if into is None else [into]))


def part_rows_body(paired, out):
    turned = paired[0][:, 0, :].T
    count = turned.shape[0] // 2
    for half in range(2):
        out[half] = turned[half * count : (half + 1) * count][:, None, :]


def part_rows(paired):
    pairs, points = paired.shape[0], paired.shape[3] // 2
    return call(
        part_rows_body,
        "part_rows",
        0,
        8 * paired.size,
        grid=(pairs,),
        in_specs=[pl.BlockSpec((1, C, 1, 2 * points), lambda r: (r, 0, 0, 0))],
        out_specs=pl.BlockSpec((2, points, 1, C), lambda r: (r, 0, 0, 0)),
        out_shape=jax.ShapeDtypeStruct((2 * pairs, points, 1, C), f32),
    )(paired)


def fourier_tables(orders, live, points, lon_count):
    phase = (orders * points % lon_count).astype(f32) * (2.0 * math.pi / lon_count)
    kept = live.astype(f32)
    cosine, sine = jnp.cos(phase) * kept, -jnp.sin(phase) * kept
    doubling = jnp.where(orders == 0, 1.0, 2.0).astype(f32)
    forward = jnp.concatenate([cosine / lon_count, sine / lon_count], axis=0)
    inverse = jnp.concatenate([cosine * doubling, sine * doubling], axis=0)
    return forward.astype(bf16), inverse.astype(bf16)


def order_rows(n_lat, pair_dev, subs):
    index = jnp.arange(n_lat * subs, dtype=jnp.int32)[:, None]
    return index // subs, index % subs


def fine_fourier(n_lat, pair_dev, subs, lon_count):
    device, sub = order_rows(n_lat, pair_dev, subs)
    kind = device * pair_dev + sub // 2
    member = sub % 2
    live = (sub < 2 * pair_dev) & jnp.where(
        member == 0, kind <= LB // 2, (kind >= 1) & (kind <= LB // 2 - 1)
    )
    orders = jnp.where(live, jnp.where(member == 0, kind, LB - kind), 0)
    points = jnp.arange(lon_count, dtype=jnp.int32)[None, :]
    return fourier_tables(orders, live, points, lon_count)


def coarse_fourier(n_lat, pair_dev, subs, lon_count):
    device, sub = order_rows(n_lat, pair_dev, subs)
    order = device * pair_dev + sub % pair_dev
    points = jnp.arange(2 * lon_count, dtype=jnp.int32)[None, :]
    live = (sub < 2 * pair_dev) & (order < LA) & (sub // pair_dev == points // lon_count)
    orders = jnp.where((sub < 2 * pair_dev) & (order < LA), order, 0)
    return fourier_tables(orders, live, points % lon_count, lon_count)


class Line:
    def __init__(self):
        self.before = self.last = None
        self.work, self.later = [], []
        self.aside = None

    def swap(self, values):
        self.step_aside()
        waits = self.work + ([] if self.last is None else [self.last])
        if waits:
            values = lax.optimization_barrier((values, waits))[0]
        self.before = self.last
        self.last = lax.all_to_all(values, "lat", split_axis=0, concat_axis=0, tiled=True)
        self.work, self.later = self.later, []
        return self.last

    def step_aside(self):
        if self.aside is not None:
            next(self.aside, None)

    def hold(self, values):
        if self.before is None:
            return values
        return lax.optimization_barrier((values, self.before))[0]

    def after_work(self, values):
        return lax.optimization_barrier((values, self.work))[0] if self.work else values

    def keep(self, values):
        self.work.append(values)
        return values

    def keep_later(self, values):
        self.later.append(values)
        return values


def partners(count, step):
    if count & (count - 1) == 0:
        return [(k, k ^ step) for k in range(count)], lambda rank: jnp.bitwise_xor(rank, step)
    return [(k, (k + step) % count) for k in range(count)], lambda rank: (rank + step) % count


def share_slots(members, n_chan, step, half):
    share = members.shape[0] // n_chan
    route, find = partners(n_chan, step)
    begin = find(lax.axis_index("chan")) * share
    if half is not None:
        share //= 2
        begin = begin + half * share
    block = lax.dynamic_slice_in_dim(members, begin, share)
    return lax.ppermute(block, "chan", route) if step else block


def sum_over(values, sizes):
    for axis, size in sizes:
        if size & (size - 1):
            values = lax.psum(values, axis)
            continue
        step = 1
        while step < size:
            values = values + lax.ppermute(values, axis, partners(size, step)[0])
            step *= 2
    return values


def add_dense(array, n_lat, n_chan, line, result):
    shape, columns = array.shape, array.shape[2]
    sizes = {"chan": n_chan, "lat": n_lat}
    pairs = [("chan", 2**k) for k in range(n_chan.bit_length() - 1)] + [("lat", 1)]
    others = n_lat // 2
    held = array.reshape(-1, columns)
    odd = lambda axis, step: (lax.axis_index(axis) // step) % 2 == 1
    group = lax.axis_index("lat") // 2

    def halve(held, axis, step):
        low, high = jnp.split(line.hold(held), 2, axis=0)
        upper = odd(axis, step)
        other = lax.ppermute(jnp.where(upper, low, high), axis, partners(sizes[axis], step)[0])
        return line.keep(jnp.where(upper, high, low) + other)

    def double(held, axis, step):
        upper = odd(axis, step)
        other = lax.ppermute(line.hold(held), axis, partners(sizes[axis], step)[0])
        return line.keep_later(
            jnp.concatenate([jnp.where(upper, other, held), jnp.where(upper, held, other)], axis=0)
        )

    for axis, step in pairs[:-1]:
        held = halve(held, axis, step)
    yield
    yield
    held = halve(held, *pairs[-1])
    yield
    pieces = line.hold(held).reshape(others, -1, columns)
    own = lax.dynamic_index_in_dim(pieces, group, 0, False)
    for step in range(1, others):
        block = lax.dynamic_index_in_dim(pieces, jnp.bitwise_xor(group, step), 0, False)
        block = lax.ppermute(block.astype(bf16), "lat", partners(n_lat, 2 * step)[0])
        own = own + block.astype(f32)
    own = line.keep_later(own).astype(bf16)
    yield
    yield
    yield
    own = line.hold(own)
    held = jnp.zeros((others,) + own.shape, bf16)
    for step in range(others):
        block = lax.ppermute(own, "lat", partners(n_lat, 2 * step)[0]) if step else own
        held = lax.dynamic_update_index_in_dim(held, block, jnp.bitwise_xor(group, step), 0)
    held = line.keep_later(held).reshape(-1, columns)
    yield
    yield
    yield
    for axis, step in reversed(pairs[1:]):
        held = double(held, axis, step)
    yield
    held = double(held, *pairs[0])
    result.append(held.astype(f32).reshape(shape))


def shards(
    n_lat, n_chan, coarse_state, fine_state, coarse_noise, fine_noise, coarse_rows, fine_rows,
    pair_slots, first_gain, first_bias, mix_weight, second_gain, second_bias, up_weight, up_bias,
    down_weight, down_bias, coarse_cotangent, fine_cotangent,
):
    pair_dev = mix_weight.shape[0] // 2
    subs = -(-2 * pair_dev // 8) * 8
    lat_rank = lax.axis_index("lat")
    fine_dev, fine_points = fine_state.shape[1], fine_state.shape[2]
    coarse_dev, coarse_points = coarse_state.shape[1], coarse_state.shape[2]
    coarse_two = coarse_dev // 2
    column = lambda vector: vector[:, None]

    def fine_in(values):
        return values.transpose(1, 3, 0, 2)

    def coarse_in(values):
        paired = values[0].reshape(coarse_two, 2 * coarse_points, values.shape[3])
        return paired.transpose(0, 2, 1)[:, :, None, :]

    def fine_back(values):
        return values.transpose(2, 0, 3, 1)

    def coarse_back(values):
        return part_rows(values).transpose(2, 0, 1, 3)

    line = Line()
    dense_unit = 4 * n_lat * n_chan
    dense_rows = -(-(C + 3) // dense_unit) * dense_unit
    row_cuts = [(fine_dev + 1) // 2, fine_dev // 2] if fine_dev >= 8 else [fine_dev]
    row_starts = [sum(row_cuts[:k]) for k in range(len(row_cuts))]
    outer_cuts = [fine_dev // 4 + 1, fine_dev - fine_dev // 4 - 1] if fine_dev >= 8 else [fine_dev]
    outer_starts = [sum(outer_cuts[:k]) for k in range(len(outer_cuts))]
    n_chunks = 2 if pair_dev % 4 == 0 else 1
    chunk_pairs = pair_dev // n_chunks
    chunk_range = range(n_chunks)

    fine_x = fine_in(fine_state)
    fine_noise_in = fine_noise[0].transpose(0, 2, 1)
    fine_forward, fine_inverse = fine_fourier(n_lat, pair_dev, subs, fine_points)
    gain_one, bias_one = column(first_gain), column(first_bias)
    fine_four = []
    for start, count in zip(outer_starts, outer_cuts):
        made = spread(fine_x, fine_noise_in, gain_one, bias_one, fine_forward, n_lat, start, count)
        fine_four.append(line.swap(line.keep(made)))
    coarse_x = coarse_in(coarse_state)
    coarse_forward, coarse_inverse = coarse_fourier(n_lat, pair_dev, subs, coarse_points)
    coarse_noise_in = coarse_in(coarse_noise)[:, :, 0, :]
    coarse_four = line.swap(
        spread(coarse_x, coarse_noise_in, gain_one, bias_one, coarse_forward, n_lat, 0, coarse_two)
    )

    wide = -(-pair_dev // 8) * 8
    classes = lat_rank * pair_dev + jnp.arange(wide, dtype=jnp.int32)
    classes = jnp.where(jnp.arange(wide) < pair_dev, classes, LB).astype(jnp.int32)
    coarse_order = coarse_rows.reshape(-1, 2).T.reshape(-1)
    by_device = fine_rows.reshape(n_lat, fine_dev)
    in_order = lambda starts, cuts: jnp.concatenate(
        [by_device[:, a : a + c].reshape(-1) for a, c in zip(starts, cuts)]
    )
    unused, fine_quad = legendre_tables(
        in_order(outer_starts, outer_cuts), pair_slots, classes, LB, True
    )
    fine_plain, unused = legendre_tables(
        in_order(row_starts, row_cuts), pair_slots, classes, LB, True
    )
    coarse_plain, coarse_quad = legendre_tables(coarse_order, pair_slots, classes, LA, False)
    turn = lambda table, chunks=n_chunks: by_class(table, n_lat, pair_dev, chunks)

    def fine_tables(parts):
        first, near, far = [turn(part) for part in parts]
        table_a = jnp.concatenate([first, near], axis=1)
        return [table_a, far], [table_a.transpose(0, 2, 1), far.transpose(0, 2, 1)]

    fine_quad_in, fine_quad_out = fine_tables(fine_quad)
    fine_plain_in, fine_plain_out = fine_tables(fine_plain)
    coarse_quad_in = turn(coarse_quad[0], 1)
    coarse_plain_in = turn(coarse_plain[0], 1)
    coarse_quad_out = coarse_quad_in.transpose(0, 2, 1)
    coarse_plain_out = coarse_plain_in.transpose(0, 2, 1)
    local_pairs = lax.dynamic_slice_in_dim(pair_slots, lat_rank * pair_dev, pair_dev)
    weight = mix_weight.transpose(0, 1, 3, 2)

    fine_work = functools.partial(to_degrees_fine, pair_dev)
    fine_back_work = functools.partial(to_orders_fine, pair_dev)
    coarse_work = functools.partial(coarse_either_way, pair_dev)

    def spectral(coarse_chunk, fine_chunks, in_tables, out_tables, cuts, backward, aside):
        wide = (C if backward else WIDE) - MAIN
        fine_made = lane_call(
            fine_work, "rows_to_degrees", line.hold(fine_chunks), in_tables[1],
            [chunk_pairs] * n_chunks, subs, wide,
        )
        line.keep(fine_made)
        arrived, mixed, shared = [], [], []

        def mix_chunk(k):
            fine, coarse = line.hold((arrived[k], arrived_coarse))
            carried = mixed[-1][3] if mixed else jnp.zeros((n_lat * subs, TILE), f32)
            made = mix(
                fine, coarse, weight, local_pairs, subs, k * chunk_pairs // 2, k == n_chunks - 1,
                backward, mixed[-1][1] if mixed else None, carried,
            )
            mixed.append(line.keep(made))

        def share_next(wanted, keep):
            members = joined_rows([made[2] for made in mixed])
            for step, half in wanted:
                block = share_slots(line.hold(members), n_chan, step, half)
                shared.append(((step, half), keep(block)))

        final = n_chan - 1
        whole_share = 2 * pair_dev // n_chan % 2 or final < 2

        arrived.append(line.swap(fine_made[0]))
        coarse_made = lane_call(
            coarse_work, "rows_to_degrees", [line.hold(coarse_chunk)], [in_tables[0]],
            [pair_dev // 2], subs, wide,
        )[0]
        arrived_coarse = line.swap(line.keep(coarse_made))
        line.keep(out_tables)
        for k in range(1, n_chunks):
            arrived.append(line.swap(fine_made[k]))
            mix_chunk(k - 1)
        if n_chunks == 1:
            mix_chunk(0)
        fine_back = []
        for k in range(n_chunks - 1):
            fine_back.append(line.swap(mixed[k][0]))
            mix_chunk(k + 1)
        arrived_coarse = line.swap(mixed[-1][1])
        share_next([(k, None) for k in range(min(2, n_chan))], line.keep_later)
        if not whole_share:
            share_next([(final, 0)], line.keep)
        fine_back.append(line.swap(mixed[-1][0]))
        share_next([(k, None) for k in range(2, final)], line.keep_later)
        coarse_made = lane_call(
            coarse_work, "degrees_to_rows", [line.hold(arrived_coarse)], [out_tables[0]],
            [coarse_two], subs, C - MAIN,
        )[0]
        coarse_end = line.swap(line.keep(coarse_made))
        if final >= 2:
            share_next([(final, None if whole_share else 1)], line.keep_later)
        shared = [
            joined_rows([block for (place, half), block in shared if place == step])
            for step in range(n_chan)
        ]
        fine_made = lane_call(
            fine_back_work, "degrees_to_rows", line.hold(fine_back), out_tables[1],
            cuts, subs, C - MAIN,
        )
        line.keep(fine_made)
        fine_end = [None] * len(cuts)
        order = list(range(len(cuts)))
        if backward:
            order.reverse()
        for k, place in enumerate(order):
            fine_end[place] = line.swap(fine_made[place])
            aside(k, coarse_end, fine_end, shared)
        return fine_end, shared

    params = [
        column(second_gain), column(second_bias), up_weight, up_weight.T, column(up_bias),
        down_weight, down_weight.T, column(down_bias),
    ]
    coarse_g, fine_g = coarse_in(coarse_cotangent), fine_in(fine_cotangent)
    coarse_made, fine_made = [], []

    def fine_pixels(k, synth):
        into = fine_made[-1][:2] if fine_made else None
        made = pixels(
            line.hold(synth), fine_x, fine_g, fine_inverse, params, row_starts[k], into,
            dense_rows,
        )
        fine_made.append(line.keep(made))

    def forward_aside(k, coarse_end, fine_end, shared):
        if k == 0:
            made = pixels(
                line.hold(coarse_end), coarse_x, coarse_g, coarse_inverse, params, 0, None,
                dense_rows,
            )
            coarse_made.extend(line.keep(made))
        else:
            fine_pixels(k - 1, fine_end[k - 1])

    fine_synth, values = spectral(
        coarse_four, fine_four, (coarse_quad_in, fine_quad_in), (coarse_plain_out, fine_plain_out),
        row_cuts, False, forward_aside,
    )
    if len(row_cuts) == 1:
        fine_pixels(0, fine_synth[0])
    fine_sgrad = []
    for k in range(len(row_cuts)):
        fine_sgrad.append(line.swap(fine_made[k][2]))
        if k + 1 < len(row_cuts):
            fine_pixels(k + 1, fine_synth[k + 1])
    axes = (("chan", n_chan), ("lat", n_lat))
    hidden = up_bias.shape[0]
    total = coarse_made[3:]
    for made in fine_made:
        total = [x + y for x, y in zip(total, made[3:])]
    narrow = jnp.concatenate([total[1][:, 0], total[2].reshape(-1)])
    narrow = jnp.pad(narrow, (0, 3 * hidden - narrow.shape[0])).reshape(1, 3, hidden)
    stacked = lax.dynamic_update_slice(total[0], narrow, (0, C, 0))
    dense = []
    line.aside = add_dense(line.hold(stacked), n_lat, n_chan, line, dense)
    line.step_aside()
    coarse_sgrad = line.swap(coarse_made[2])
    coarse_made[0] = line.keep(coarse_back(line.hold(coarse_made[0])))
    ends, mix_grads = [], []

    def finish_fine(place, wave):
        into = ends[-1][0] if len(ends) > 1 else None
        return finish(
            wave, fine_x, fine_made[-1][1], fine_forward, gain_one, outer_starts[place], into
        )

    def backward_aside(k, coarse_end, fine_end, shared):
        if k == 0:
            mix_grads.append(line.keep(mix_gradient(values, line.hold(shared))))
            made = finish(
                line.hold(coarse_end), coarse_x, coarse_made[1], coarse_forward, gain_one, 0, None
            )
            made = [coarse_back(made[0]), made[1]]
        else:
            made = finish_fine(len(outer_cuts) - k, line.hold(fine_end[-k]))
        ends.append(list(line.keep(made)))

    fine_fgrad, grads = spectral(
        coarse_sgrad, fine_sgrad, (coarse_plain_in, fine_plain_in), (coarse_quad_out, fine_quad_out),
        outer_cuts, True, backward_aside,
    )
    for unused in line.aside:
        pass
    up_grad, down_grad = line.keep((dense[0][0, :C], dense[0][1, :C]))
    narrow = dense[0][0, C : C + 3].reshape(-1)
    narrow_sums = narrow[hidden : hidden + 3 * C].reshape(3, C)
    last_wave = lax.optimization_barrier((fine_fgrad[0], line.work + line.later))[0]
    ends.append(finish_fine(0, last_wave))
    mix_grad = mix_grads[0].transpose(0, 2, 3, 1)
    sums = sum(end[1] for end in ends)
    first_sums = sum_over(sums[:, :, 0], axes)
    return (
        coarse_made[0],
        fine_back(fine_made[-1][0]),
        ends[0][0],
        fine_back(ends[-1][0]),
        first_sums[0],
        first_sums[1],
        mix_grad,
        narrow_sums[0],
        narrow_sums[1],
        up_grad,
        narrow[:hidden],
        down_grad.T,
        narrow_sums[2],
    )


def solution(mesh):
    pixel = P("chan", "lat", None, None)
    slots = P("lat", None, None, None)
    return jax.shard_map(
        functools.partial(shards, mesh.shape["lat"], mesh.shape["chan"]),
        mesh=mesh,
        in_specs=(pixel,) * 4 + (P(),) * 5 + (slots,) + (P(),) * 6 + (pixel,) * 2,
        out_specs=(pixel,) * 4 + (P(),) * 2 + (P(("lat", "chan"), None, None, None),) + (P(),) * 6,
        check_vma=False,
    )
```
